512 devices in a mesh: ctx: 32 (over y_hi, z), tp: 16 (over y_lo, x, core).
Axes of the slice: x: 4, y: 8 (y_hi: 4, y_lo: 2; y = y_hi * 2 + y_lo), z: 8, core: 2. Of those that a mesh axis runs over, the one named last changes fastest.
Arguments:
- tokens: bfloat16 [4096, 4096], P('ctx', 'tp'), may hold values from -6 to 6
- in_weight: bfloat16 [3, 4096, 4096], P(None, 'ctx', 'tp'), may hold values from -0.1875 to 0.1875
- out_weight: bfloat16 [4096, 4096], P('tp', 'ctx'), may hold values from -0.1875 to 0.1875
- mr_filter: float32 [256, 128], P('tp'), may hold values from -0.5 to 0.5
- cotangent: bfloat16 [4096, 4096], P('ctx', 'tp'), may hold values from -6 to 6
Outputs:
- mixed_out: bfloat16 [4096, 4096], P('ctx', 'tp')
- grad_tokens: bfloat16 [4096, 4096], P('ctx', 'tp')
The draws below stay inside these ranges and needn't reach their ends.
All inputs are finite; a program needn't handle non-finite values.
Results may differ from the reference program's by a relative error of at most 0.03.
Values may be sent and summed in bfloat16 or wider, within the bound.
No kernel may reach another device: no remote copies, remote signals or barrier semaphores. Data moves between devices by JAX's collectives and lax.ppermute only.
A program may use at most 128 MiB of HBM per device.

```python
import jax
import jax.numpy as jnp
from jax import lax

D = 4096
GROUP = 16
TAPS = 128
FILTERS = 256
TOKENS = 4096
N_TP = 16


def raised(values, own_key, source, target, shards_of, factor):
    def block_of(axis_at):
        return (jnp.arange(values.shape[axis_at]) // (values.shape[axis_at] // shards_of)).reshape((-1,) + (1,) * (values.ndim - 1 - axis_at))

    first = jax.random.permutation(own_key, shards_of)[block_of(target)]
    other_side = (block_of(target) + shards_of // 2) % shards_of
    return jnp.where((block_of(source) == first) | (block_of(source) == other_side), factor * values, values)


def level_of(own_key, extent, split, smallest, high):
    def one(dim, blocks):
        heights = jax.random.uniform(jax.random.fold_in(jax.random.fold_in(own_key, 6), dim), (blocks,), jnp.float32, smallest / len(split), high / len(split))
        return jnp.repeat(jnp.exp(heights), extent[dim] // blocks).reshape((-1,) + (1,) * (len(extent) - dim - 1))

    level = one(*split[0])
    for cut in split[1:]:
        level = level * one(*cut)
    return level


def gaussian(own_key, shape, deviation, reach, shards=(), dtype=jnp.bfloat16):
    factor_of = level_of(own_key, shape, shards, -0.22, 0.18) if shards else 1.0
    drawn = jax.random.normal(own_key, shape, jnp.float32) * deviation * factor_of
    return jnp.minimum(jnp.maximum(drawn, -reach), reach).astype(dtype)


def gaussian_with(own_key, shape, scale, most, shards, heavy, kind=jnp.bfloat16):
    array = scale * jax.random.normal(own_key, shape, jnp.float32)
    if shards:
        array = array * level_of(own_key, shape, shards, -0.22, 0.18)
    return jnp.clip(raised(array, jax.random.fold_in(own_key, 3), *heavy), -most, most).astype(kind)


def setup_inputs(seed: int = 0) -> dict:
    splits = jax.random.split(jax.random.key(seed), 6)
    tokens = gaussian(splits[0], (TOKENS, D), 1.0, 6.0, ((0, 32), (1, 16)))
    in_weight = gaussian_with(splits[1], (3, D, D), D ** -0.5, 0.1875, ((1, 32), (2, 16)), (2, 1, 32, 2.75))
    out_weight = gaussian_with(splits[2], (D, D), D ** -0.5, 0.1875, ((0, 16), (1, 32)), (0, 1, 32, 2.75))
    mr_filter = gaussian(splits[3], (FILTERS, TAPS), TAPS ** -0.5, 0.5, ((0, 16),), jnp.float32)
    cotangent = gaussian(splits[4], (TOKENS, D), 1.0, 6.0, ((0, 32), (1, 16)))
    return {"tokens": tokens, "in_weight": in_weight, "out_weight": out_weight, "mr_filter": mr_filter, "cotangent": cotangent}


def causal_filter(values, spread):
    length = values.shape[0]
    padded = jnp.concatenate([jnp.zeros((TAPS - 1, values.shape[1]), jnp.float32), values], 0)

    def add_tap(tap_index, running):
        begin = (TAPS - 1 - tap_index).astype(jnp.int32)
        window = lax.dynamic_slice_in_dim(padded, begin, length, 0)
        return running + window * lax.dynamic_index_in_dim(spread, tap_index, 1, keepdims=False)

    return lax.fori_loop(0, TAPS, add_tap, jnp.zeros(values.shape, jnp.float32))


def anticausal_filter(values, spread):
    length = values.shape[0]
    padded = jnp.concatenate([values, jnp.zeros((TAPS - 1, values.shape[1]), jnp.float32)], 0)

    def add_tap(tap_index, running):
        begin = tap_index.astype(jnp.int32)
        window = lax.dynamic_slice_in_dim(padded, begin, length, 0)
        return running + window * lax.dynamic_index_in_dim(spread, tap_index, 1, keepdims=False)

    return lax.fori_loop(0, TAPS, add_tap, jnp.zeros(values.shape, jnp.float32))


def reference(tokens, in_weight, out_weight, mr_filter, cotangent):
    model_width = tokens.shape[1]
    share_width = model_width // N_TP
    row_total = tokens.shape[0]
    streams = [jnp.dot(tokens, in_weight[stream], preferred_element_type=jnp.float32).astype(jnp.bfloat16) for stream in range(3)]
    query_part = streams[0].astype(jnp.float32)
    key_part = streams[1].astype(jnp.float32)
    value_part = streams[2].astype(jnp.float32)
    product = (key_part * value_part).astype(jnp.bfloat16)
    spread = jnp.repeat(mr_filter, GROUP, axis=0)
    mixed_conv = causal_filter(product.astype(jnp.float32), spread)
    gating = (query_part * mixed_conv).astype(jnp.bfloat16)
    mixed_out = jnp.zeros((row_total, model_width), jnp.float32)
    for rank_index in range(N_TP):
        lower = rank_index * share_width
        partial_out = jnp.dot(gating[:, lower:lower + share_width], out_weight[lower:lower + share_width], preferred_element_type=jnp.float32)
        partial_out = lax.optimization_barrier(partial_out.astype(jnp.bfloat16))
        mixed_out = mixed_out + partial_out.astype(jnp.float32)
    grad_gate = lax.dot_general(cotangent, out_weight, (((1,), (1,)), ((), ())), preferred_element_type=jnp.float32)
    grad_query = grad_gate * mixed_conv
    grad_mixed = (grad_gate * query_part).astype(jnp.bfloat16)
    grad_product = anticausal_filter(grad_mixed.astype(jnp.float32), spread)
    grad_streams = [grad_query.astype(jnp.bfloat16), (grad_product * value_part).astype(jnp.bfloat16), (grad_product * key_part).astype(jnp.bfloat16)]
    grad_tokens = jnp.zeros((row_total, model_width), jnp.float32)
    for rank_index in range(N_TP):
        lower = rank_index * share_width
        partial_grad = jnp.zeros((row_total, model_width), jnp.float32)
        for stream in range(3):
            partial_grad = partial_grad + lax.dot_general(grad_streams[stream][:, lower:lower + share_width], in_weight[stream, :, lower:lower + share_width], (((1,), (1,)), ((), ())), preferred_element_type=jnp.float32)
        partial_grad = lax.optimization_barrier(partial_grad.astype(jnp.bfloat16))
        grad_tokens = grad_tokens + partial_grad.astype(jnp.float32)
    return mixed_out.astype(jnp.bfloat16), grad_tokens.astype(jnp.bfloat16)
```

```python
import functools

import jax
import jax.numpy as jnp
from jax import lax
from jax.experimental import pallas as pl
from jax.experimental.pallas import tpu as pltpu
from jax.sharding import Mesh, PartitionSpec as P

AXES = ("h", "l", "z", "ylo", "x", "core")
SIZES = (2, 2, 8, 2, 4, 2)
ROWS = 128
HALF = 128
TAPS = 128
GROUP = 16
GROUPS = HALF // GROUP
STREAMS = 4 * HALF
BACK = 3 * HALF


def bands_kernel(base_ref, band_ref):
    for row in range(base_ref.shape[0]):
        spread = jnp.broadcast_to(base_ref[row : row + 1, :], (ROWS, 2 * ROWS))
        band_ref[row] = pltpu.roll(spread, 0, 1, stride=1, stride_axis=0).astype(jnp.bfloat16)


def bands(filters):
    count = filters.shape[0]
    zeros = jnp.zeros((count, TAPS), filters.dtype)
    causal = jnp.concatenate([zeros[:, :1], filters[:, ::-1], zeros[:, 1:]], 1)
    anticausal = jnp.concatenate([filters, zeros], 1)
    return pl.pallas_call(
        bands_kernel,
        out_shape=jax.ShapeDtypeStruct((2 * count, ROWS, 2 * ROWS), jnp.bfloat16),
    )(jnp.concatenate([causal, anticausal], 0))


def forward_kernel(place_ref, own_ref, other_ref, weight_ref, streams_ref, gate_ref, product_ref, mixed_ref, total):
    step = pl.program_id(0)
    core = place_ref[0]

    @pl.when(step == 0)
    def _():
        total[...] = jnp.zeros_like(total)

    for values_ref, which in ((own_ref, core), (other_ref, 1 - core)):
        weight = weight_ref[pl.ds(2 * which, 2), 0].reshape(2 * ROWS, STREAMS)
        tokens = values_ref[0, :, 0, 0].reshape(2 * ROWS, 2 * HALF)
        cotangent = values_ref[0, :, 0, 1].reshape(2 * ROWS, 2 * HALF)
        total[:, :BACK] += jnp.dot(tokens, weight[:, :BACK], preferred_element_type=jnp.float32)
        total[:, BACK:] += jnp.dot(cotangent, weight[:, BACK:], preferred_element_type=jnp.float32)

    @pl.when(step == pl.num_programs(0) - 1)
    def _():
        streams = total[:, :BACK].astype(jnp.bfloat16)
        streams_ref[...] = streams
        grad_gate = total[:, BACK:]
        gate_ref[...] = grad_gate
        query, key, value = (streams[:, i * HALF : (i + 1) * HALF].astype(jnp.float32) for i in range(3))
        product_ref[...] = (key * value).astype(jnp.bfloat16)
        mixed_ref[...] = (grad_gate * query).astype(jnp.bfloat16)


def forward(place, own, other, weight):
    values = pl.BlockSpec((1, 2, 1, 2, ROWS, 2 * HALF), lambda j, p: (j // 2, 0, j % 2, 0, 0, 0))
    whole = lambda width: pl.BlockSpec((2 * ROWS, width), lambda j, p: (0, 0))
    shape = lambda width, kind: jax.ShapeDtypeStruct((2 * ROWS, width), kind)
    return pl.pallas_call(
        forward_kernel,
        out_shape=(
            shape(BACK, jnp.bfloat16),
            shape(HALF, jnp.float32),
            shape(HALF, jnp.bfloat16),
            shape(HALF, jnp.bfloat16),
        ),
        grid_spec=pltpu.PrefetchScalarGridSpec(
            num_scalar_prefetch=1,
            grid=(8,),
            in_specs=[
                values,
                values,
                pl.BlockSpec((4, 1, ROWS, STREAMS), lambda j, p: ((j // 2) % 2, (j % 2) * 2 + j // 4, 0, 0)),
            ],
            out_specs=[whole(BACK), whole(HALF), whole(HALF), whole(HALF)],
            scratch_shapes=[pltpu.VMEM((2 * ROWS, STREAMS), jnp.float32)],
        ),
        cost_estimate=pl.CostEstimate(flops=1 << 30, bytes_accessed=9 << 20, transcendentals=0),
    )(place, own, other, weight)


def pick(result, segment):
    rows = result.reshape(GROUPS, ROWS, 2 * HALF)[:, :, segment * HALF : (segment + 1) * HALF]
    group = lax.broadcasted_iota(jnp.int32, (ROWS, HALF), 1) // GROUP
    picked = rows[0]
    for g in range(1, GROUPS):
        picked = jnp.where(group == g, rows[g], picked)
    return picked


def middle_kernel(place_ref, band_ref, streams_ref, gate_ref, product_ref, mixed_ref, before_ref, after_ref, out_ref):
    position = place_ref[1]
    first = position == 0
    last = position == 15
    product = [product_ref[s * ROWS : (s + 1) * ROWS] for s in range(2)]
    mixed = [mixed_ref[s * ROWS : (s + 1) * ROWS] for s in range(2)]
    before = [before_ref[s * ROWS : (s + 1) * ROWS] for s in range(2)]
    after = [after_ref[s * ROWS : (s + 1) * ROWS] for s in range(2)]
    zero = jnp.zeros_like(before[0])
    earlier = [jnp.where(first, zero, before[0]), jnp.where(first, before[0], before[1])]
    later = [jnp.where(last, after[1], after[0]), jnp.where(last, zero, after[1])]
    causal = jnp.concatenate(
        [jnp.concatenate(earlier, 1), jnp.concatenate(product, 1)], 0
    )
    anticausal = jnp.concatenate(
        [jnp.concatenate(mixed, 1), jnp.concatenate(later, 1)], 0
    )
    count = GROUPS * ROWS
    conv = jnp.dot(
        band_ref[:GROUPS].reshape(count, 2 * ROWS), causal, preferred_element_type=jnp.float32
    )
    back = jnp.dot(
        band_ref[GROUPS:].reshape(count, 2 * ROWS), anticausal, preferred_element_type=jnp.float32
    )
    for s in range(2):
        rows = slice(s * ROWS, (s + 1) * ROWS)
        query, key, value = (
            streams_ref[rows, i * HALF : (i + 1) * HALF].astype(jnp.float32) for i in range(3)
        )
        mixed_conv = pick(conv, s)
        grad_product = pick(back, s)
        out_ref[rows, :HALF] = (gate_ref[rows] * mixed_conv).astype(jnp.bfloat16)
        out_ref[rows, HALF : 2 * HALF] = (grad_product * value).astype(jnp.bfloat16)
        out_ref[rows, 2 * HALF : 3 * HALF] = (grad_product * key).astype(jnp.bfloat16)
        out_ref[rows, 3 * HALF :] = (query * mixed_conv).astype(jnp.bfloat16)


def middle(place, band, streams, gate, product, mixed, before, after):
    smem = pl.BlockSpec(memory_space=pltpu.SMEM)
    vmem = pl.BlockSpec(memory_space=pltpu.VMEM)
    return pl.pallas_call(
        middle_kernel,
        out_shape=jax.ShapeDtypeStruct((2 * ROWS, STREAMS), jnp.bfloat16),
        in_specs=[smem] + [vmem] * 7,
        out_specs=vmem,
        compiler_params=pltpu.CompilerParams(vmem_limit_bytes=32 << 20),
        cost_estimate=pl.CostEstimate(flops=1 << 28, bytes_accessed=3 << 20, transcendentals=0),
    )(place, band, streams, gate, product, mixed, before, after)


def backward_kernel(which_ref, terms_ref, weight_ref, out_ref):
    weight = weight_ref[:, 0].reshape(2 * ROWS, STREAMS)
    contract = (((1,), (1,)), ((), ()))
    mixed = lax.dot_general(
        terms_ref[:, BACK:], weight[:, BACK:], contract, preferred_element_type=jnp.float32
    )
    grad = lax.dot_general(
        terms_ref[:, :BACK], weight[:, :BACK], contract, preferred_element_type=jnp.float32
    )
    out_ref[0, :, 0, 0] = mixed.astype(jnp.bfloat16).reshape(2, ROWS, 2 * HALF)
    out_ref[0, :, 0, 1] = grad.astype(jnp.bfloat16).reshape(2, ROWS, 2 * HALF)


def backward(which, terms, weight):
    return pl.pallas_call(
        backward_kernel,
        out_shape=jax.ShapeDtypeStruct((4, 2, 2, 2, ROWS, 2 * HALF), jnp.bfloat16),
        grid_spec=pltpu.PrefetchScalarGridSpec(
            num_scalar_prefetch=1,
            grid=(8,),
            in_specs=[
                pl.BlockSpec((2 * ROWS, STREAMS), lambda j, c: (0, 0)),
                pl.BlockSpec(
                    (2, 1, ROWS, STREAMS),
                    lambda j, c: (((j // 2) % 2) * 2 + c[0], (j % 2) * 2 + j // 4, 0, 0),
                ),
            ],
            out_specs=pl.BlockSpec((1, 2, 1, 2, ROWS, 2 * HALF), lambda j, c: (j // 2, 0, j % 2, 0, 0, 0)),
        ),
        cost_estimate=pl.CostEstimate(flops=1 << 29, bytes_accessed=4 << 20, transcendentals=0),
    )(which, terms, weight)


def swapped(value, axes):
    return lax.all_to_all(value, axes, 0, 0, tiled=True)


def gathered(value, axes, count):
    return swapped(jnp.broadcast_to(value[None], (count,) + value.shape), axes)


def local(tokens, in_weight, out_weight, mr_filter, cotangent):
    half, core = lax.axis_index("h"), lax.axis_index("core")
    position = lax.axis_index(("l", "z"))
    place = jnp.stack([core, position]).astype(jnp.int32)

    weight = jnp.concatenate([in_weight, out_weight.T[None]], 0)
    weight = weight.reshape(4, ROWS, 2, HALF).transpose(2, 1, 0, 3).reshape(2, 1, ROWS, STREAMS)
    weight = jnp.broadcast_to(weight, (2, 2, ROWS, STREAMS)).reshape(4, ROWS, STREAMS)
    weight = swapped(weight, ("h", "l"))
    values = jnp.stack([tokens, cotangent], 0)
    weight, values, mr_filter = lax.optimization_barrier((weight, values, mr_filter))
    weight = lax.all_gather(weight, "z", axis=0)

    filters = lax.dynamic_slice_in_dim(mr_filter, half * GROUPS, GROUPS, 0)
    band = bands(filters)

    values = gathered(values, ("h", "ylo"), 4)
    values = gathered(values, "x", 4).reshape(4, 2, 2, 2, ROWS, 2 * HALF)
    cross = [(0, 1), (1, 0)]
    other = lax.ppermute(values, "core", cross)

    streams, gate, product, mixed = forward(place, values, other, weight)
    ring = [(n, (n + 1) % 16) for n in range(16)]
    before = lax.ppermute(product, ("l", "z"), ring)
    after = lax.ppermute(mixed, ("l", "z"), [(b, a) for a, b in ring])
    terms = middle(place, band, streams, gate, product, mixed, before, after)

    far = backward((1 - core).reshape(1).astype(jnp.int32), terms, weight)
    near = backward(core.reshape(1).astype(jnp.int32), terms, weight)
    far = lax.ppermute(far, "core", cross)
    sums = (near.astype(jnp.float32) + far.astype(jnp.float32)).astype(jnp.bfloat16)
    sums = swapped(sums, "x").astype(jnp.float32).sum(0).astype(jnp.bfloat16)
    sums = swapped(sums.reshape(4, 2, ROWS, 2 * HALF), ("h", "ylo")).astype(jnp.float32).sum(0)
    sums = sums.astype(jnp.bfloat16)
    return sums[0], sums[1]


def solution(mesh):
    fine = Mesh(mesh.devices.reshape(SIZES), AXES)
    ctx, tp = AXES[:3], AXES[3:]
    return jax.shard_map(
        local,
        mesh=fine,
        in_specs=(P(ctx, tp), P(None, ctx, tp), P(tp, ctx), P(tp, None), P(ctx, tp)),
        out_specs=(P(ctx, tp), P(ctx, tp)),
        check_vma=False,
    )
```

```python
import jax
import jax.numpy as jnp
from jax import lax
from jax.experimental import pallas as pl
from jax.experimental.pallas import tpu as pltpu
from jax.sharding import Mesh, PartitionSpec as P

AXES = ("h", "l", "z", "ylo", "x", "core")
SIZES = (2, 2, 8, 2, 4, 2)
ROWS = 128
HALF = 128
TAPS = 128
GROUP = 16
GROUPS = HALF // GROUP
FEATURES = 256
STREAMS = 4 * HALF
BACK = 3 * HALF
BF16 = jnp.bfloat16
F32 = jnp.float32


def bands_kernel(base_ref, band_ref):
    for row in range(2 * GROUPS):
        spread = jnp.broadcast_to(base_ref[row : row + 1, :], (2 * ROWS, 2 * ROWS))
        rolled = pltpu.roll(spread, 0, 1, stride=1, stride_axis=0)
        band_ref[:, row * ROWS : (row + 1) * ROWS] = rolled[:, :ROWS].astype(BF16)


def bands(filters):
    zeros = jnp.zeros((GROUPS, TAPS), filters.dtype)
    causal = jnp.concatenate([zeros, filters], 1)
    anticausal = jnp.concatenate([filters[:, :1], zeros, filters[:, :0:-1]], 1)
    return pl.pallas_call(
        bands_kernel,
        out_shape=jax.ShapeDtypeStruct((2 * ROWS, 2 * GROUPS * ROWS), BF16),
    )(jnp.concatenate([causal, anticausal], 0))


def forward_kernel(place_ref, own_ref, other_ref, weight_ref, streams_ref, gate_ref, product_ref, mixed_ref, total):
    step = pl.program_id(0)
    core = place_ref[0]

    @pl.when(step == 0)
    def _():
        total[...] = jnp.zeros_like(total)

    tokens, cotangent, weight = [], [], []
    for values_ref, which in ((own_ref, core), (other_ref, 1 - core)):
        for y in range(2):
            tokens.append(values_ref[0, :, y, 0].reshape(2 * ROWS, FEATURES))
            cotangent.append(values_ref[0, :, y, 1].reshape(2 * ROWS, FEATURES))
            weight.append(weight_ref[pl.ds(2 * which, 2), y, 0].reshape(FEATURES, STREAMS))
    tokens, cotangent = jnp.concatenate(tokens, 1), jnp.concatenate(cotangent, 1)
    weight = jnp.concatenate(weight, 0)
    total[:, :BACK] += jnp.dot(tokens, weight[:, :BACK], preferred_element_type=F32)
    total[:, BACK:] += jnp.dot(cotangent, weight[:, BACK:], preferred_element_type=F32)

    @pl.when(step == pl.num_programs(0) - 1)
    def _():
        turned = total[...].T
        streams = turned[:BACK].astype(BF16)
        streams_ref[...] = streams
        grad_gate = turned[BACK:]
        gate_ref[...] = grad_gate
        query, key, value = (streams[i * HALF : (i + 1) * HALF].astype(F32) for i in range(3))
        product_ref[...] = (key * value).astype(BF16)
        mixed_ref[...] = (grad_gate * query).astype(BF16)


def forward(place, own, other, weight):
    values = pl.BlockSpec((1, 2, 2, 2, ROWS, FEATURES), lambda j, p: (j, 0, 0, 0, 0, 0))
    whole = lambda height: pl.BlockSpec((height, 2 * ROWS), lambda j, p: (0, 0))
    shape = lambda height, kind: jax.ShapeDtypeStruct((height, 2 * ROWS), kind)
    return pl.pallas_call(
        forward_kernel,
        out_shape=(shape(BACK, BF16), shape(HALF, F32), shape(HALF, BF16), shape(HALF, BF16)),
        grid_spec=pltpu.PrefetchScalarGridSpec(
            num_scalar_prefetch=1,
            grid=(4,),
            in_specs=[
                values,
                values,
                pl.BlockSpec((4, 2, 1, ROWS, STREAMS), lambda j, p: (j % 2, 0, j // 2, 0, 0)),
            ],
            out_specs=[whole(BACK), whole(HALF), whole(HALF), whole(HALF)],
            scratch_shapes=[pltpu.VMEM((2 * ROWS, STREAMS), F32)],
        ),
        compiler_params=pltpu.CompilerParams(vmem_limit_bytes=24 << 20),
        cost_estimate=pl.CostEstimate(flops=1 << 30, bytes_accessed=9 << 20, transcendentals=0),
    )(place, own, other, weight)


def filtered(left, right, band):
    segments = [
        jnp.concatenate([left[s], right[s]], 1) for s in range(2)
    ]
    result = jnp.dot(jnp.concatenate(segments, 0), band, preferred_element_type=F32)
    return [
        jnp.concatenate(
            [
                result[s * HALF + g * GROUP : s * HALF + (g + 1) * GROUP, g * ROWS : (g + 1) * ROWS]
                for g in range(GROUPS)
            ],
            0,
        )
        for s in range(2)
    ]


def middle(position, band_ref, streams_ref, gate_ref, product_ref, mixed_ref, before_ref, after_ref, terms_ref):
    first = position == 0
    last = position == 15
    lanes = [slice(s * ROWS, (s + 1) * ROWS) for s in range(2)]
    product, mixed, before, after = (
        [ref[:, lanes[s]] for s in range(2)] for ref in (product_ref, mixed_ref, before_ref, after_ref)
    )
    zero = jnp.zeros_like(before[0])
    earlier = [jnp.where(first, zero, before[0]), jnp.where(first, before[0], before[1])]
    later = [jnp.where(last, after[1], after[0]), jnp.where(last, zero, after[1])]
    conv = filtered(earlier, product, band_ref[:, : GROUPS * ROWS])
    back = filtered(mixed, later, band_ref[:, GROUPS * ROWS :])
    for s in range(2):
        query, key, value = (
            streams_ref[i * HALF : (i + 1) * HALF, lanes[s]].astype(F32) for i in range(3)
        )
        terms_ref[:HALF, lanes[s]] = (gate_ref[:, lanes[s]] * conv[s]).astype(BF16)
        terms_ref[HALF : 2 * HALF, lanes[s]] = (back[s] * value).astype(BF16)
        terms_ref[2 * HALF : BACK, lanes[s]] = (back[s] * key).astype(BF16)
        terms_ref[BACK:, lanes[s]] = (query * conv[s]).astype(BF16)


def halves(result):
    return result[:, :ROWS], result[:, ROWS:]


def mixed_far_kernel(
    place_ref, band_ref, streams_ref, gate_ref, product_ref, mixed_ref, before_ref, after_ref, weight_ref, terms_ref, out_ref
):
    @pl.when(pl.program_id(0) == 0)
    def _():
        middle(
            place_ref[1], band_ref, streams_ref, gate_ref, product_ref, mixed_ref, before_ref, after_ref, terms_ref
        )

    gating = terms_ref[BACK:]
    for y in range(2):
        weight = weight_ref[:, y, 0].reshape(FEATURES, HALF)
        for h, part in enumerate(halves(jnp.dot(weight, gating, preferred_element_type=F32))):
            out_ref[0, h, y] = part.astype(BF16)


def out_weight_spec(core):
    return pl.BlockSpec((2, 2, 1, ROWS, HALF), lambda j, p: ((j % 2) * 2 + core(p), 0, j // 2, 0, 3))


def in_weight_spec(core):
    return pl.BlockSpec((2, 2, 1, ROWS, BACK), lambda j, p: ((j % 2) * 2 + core(p), 0, j // 2, 0, 0))


MIXED_SHAPE = (4, 2, 2, FEATURES, ROWS)
MIXED_SPEC = pl.BlockSpec((1, 2, 2, FEATURES, ROWS), lambda j, p: (j, 0, 0, 0, 0))
GRAD_SHAPE = (2, 2, 4, FEATURES, ROWS)
GRAD_SPEC = pl.BlockSpec((2, 2, 1, FEATURES, ROWS), lambda j, p: (0, 0, j, 0, 0))
TERMS_SPEC = pl.BlockSpec((STREAMS, 2 * ROWS), lambda j, p: (0, 0))


def mixed_far(place, band, streams, gate, product, mixed, before, after, weight):
    flat = lambda value: pl.BlockSpec(value.shape, lambda j, p: (0, 0))
    operands = (band, streams, gate, product, mixed, before, after)
    return pl.pallas_call(
        mixed_far_kernel,
        out_shape=(
            jax.ShapeDtypeStruct((STREAMS, 2 * ROWS), BF16),
            jax.ShapeDtypeStruct(MIXED_SHAPE, BF16),
        ),
        grid_spec=pltpu.PrefetchScalarGridSpec(
            num_scalar_prefetch=1,
            grid=(4,),
            in_specs=[flat(value) for value in operands] + [out_weight_spec(lambda p: 1 - p[0])],
            out_specs=[TERMS_SPEC, MIXED_SPEC],
        ),
        compiler_params=pltpu.CompilerParams(vmem_limit_bytes=24 << 20),
        cost_estimate=pl.CostEstimate(flops=1 << 28, bytes_accessed=4 << 20, transcendentals=0),
    )(place, *operands, weight)


def mixed_near_kernel(place_ref, terms_ref, weight_ref, far_ref, out_ref):
    gating = terms_ref[BACK:]
    for y in range(2):
        weight = weight_ref[:, y, 0].reshape(FEATURES, HALF)
        for h, part in enumerate(halves(jnp.dot(weight, gating, preferred_element_type=F32))):
            out_ref[0, h, y] = (part + far_ref[0, h, y].astype(F32)).astype(BF16)


def mixed_near(place, terms, weight, far):
    return pl.pallas_call(
        mixed_near_kernel,
        out_shape=jax.ShapeDtypeStruct(MIXED_SHAPE, BF16),
        grid_spec=pltpu.PrefetchScalarGridSpec(
            num_scalar_prefetch=1,
            grid=(4,),
            in_specs=[TERMS_SPEC, out_weight_spec(lambda p: p[0]), MIXED_SPEC],
            out_specs=MIXED_SPEC,
        ),
        cost_estimate=pl.CostEstimate(flops=1 << 27, bytes_accessed=3 << 20, transcendentals=0),
    )(place, terms, weight, far)


def grad_far_kernel(place_ref, terms_ref, weight_ref, out_ref):
    for y in range(2):
        weight = weight_ref[:, y, 0].reshape(FEATURES, BACK)
        for h, part in enumerate(halves(jnp.dot(weight, terms_ref[:BACK], preferred_element_type=F32))):
            out_ref[h, y, 0] = part.astype(BF16)


def grad_near_kernel(place_ref, terms_ref, weight_ref, far_ref, out_ref):
    for y in range(2):
        weight = weight_ref[:, y, 0].reshape(FEATURES, BACK)
        for h, part in enumerate(halves(jnp.dot(weight, terms_ref[:BACK], preferred_element_type=F32))):
            out_ref[h, y, 0] = (part + far_ref[h, y, 0].astype(F32)).astype(BF16)


def grad_part(place, terms, weight, far=None):
    near = far is not None
    core = (lambda p: p[0]) if near else (lambda p: 1 - p[0])
    return pl.pallas_call(
        grad_near_kernel if near else grad_far_kernel,
        out_shape=jax.ShapeDtypeStruct(GRAD_SHAPE, BF16),
        grid_spec=pltpu.PrefetchScalarGridSpec(
            num_scalar_prefetch=1,
            grid=(4,),
            in_specs=[TERMS_SPEC, in_weight_spec(core)] + [GRAD_SPEC] * near,
            out_specs=GRAD_SPEC,
        ),
        cost_estimate=pl.CostEstimate(flops=1 << 28, bytes_accessed=4 << 20, transcendentals=0),
    )(place, terms, weight, *([far] if near else []))


def swapped(value, axes):
    return lax.all_to_all(value, axes, 0, 0, tiled=True)


def gathered(value, axes, count):
    return swapped(jnp.broadcast_to(value[None], (count,) + value.shape), axes)


def reduced(value, axes):
    return swapped(value, axes).astype(F32).sum(0).astype(BF16)


def local(tokens, in_weight, out_weight, mr_filter, cotangent):
    half, core = lax.axis_index("h"), lax.axis_index("core")
    position = lax.axis_index(("l", "z"))
    place = jnp.stack([core, position]).astype(jnp.int32)

    weight = jnp.concatenate([in_weight, out_weight.T[None]], 0)
    weight = weight.reshape(4, ROWS, 2, HALF).transpose(2, 1, 0, 3).reshape(2, 1, ROWS, STREAMS)
    weight = jnp.broadcast_to(weight, (2, 2, ROWS, STREAMS)).reshape(4, ROWS, STREAMS)
    weight = swapped(weight, ("h", "l"))
    values = jnp.stack([tokens, cotangent], 0)
    weight, values = lax.optimization_barrier((weight, values))
    weight = lax.all_gather(weight, "z", axis=0).reshape(8, 2, 2, ROWS, STREAMS)

    band = bands(lax.dynamic_slice_in_dim(mr_filter, half * GROUPS, GROUPS, 0))
    values = gathered(values, ("h", "ylo"), 4)
    values = gathered(values, "x", 4).reshape(4, 2, 2, 2, ROWS, FEATURES)
    values, band = lax.optimization_barrier((values, band))
    cross = [(0, 1), (1, 0)]
    other = lax.ppermute(values, "core", cross)

    streams, gate, product, mixed = forward(place, values, other, weight)
    ring = [(n, (n + 1) % 16) for n in range(16)]
    before = lax.ppermute(product, ("l", "z"), ring)
    after = lax.ppermute(mixed, ("l", "z"), [(b, a) for a, b in ring])

    terms, far_mixed = mixed_far(place, band, streams, gate, product, mixed, before, after, weight)
    far_mixed = lax.ppermute(far_mixed, "core", cross)
    far_grad = lax.ppermute(grad_part(place, terms, weight), "core", cross)
    mixed_sum = mixed_near(place, terms, weight, far_mixed)
    grad_sum = grad_part(place, terms, weight, far_grad)
    mixed_sum = reduced(mixed_sum, "x").reshape(4, FEATURES, ROWS)
    grad_sum = reduced(grad_sum.reshape(4, 4, FEATURES, ROWS), ("h", "ylo"))
    mixed_sum = reduced(mixed_sum, ("h", "ylo"))
    grad_sum = reduced(grad_sum, "x")
    return mixed_sum.T, grad_sum.T


def solution(mesh):
    fine = Mesh(mesh.devices.reshape(SIZES), AXES)
    ctx, tp = AXES[:3], AXES[3:]
    return jax.shard_map(
        local,
        mesh=fine,
        in_specs=(P(ctx, tp), P(None, ctx, tp), P(tp, ctx), P(tp, None), P(ctx, tp)),
        out_specs=(P(ctx, tp), P(ctx, tp)),
        check_vma=False,
    )
```

```python
import jax
import jax.numpy as jnp
from jax import lax
from jax.experimental import pallas as pl
from jax.experimental.pallas import tpu as pltpu
from jax.sharding import Mesh, PartitionSpec as P

AXES = ("h", "l", "z", "ylo", "x", "core")
SIZES = (2, 2, 8, 2, 4, 2)
ROWS = 128
HALF = 128
TAPS = 128
GROUP = 16
GROUPS = HALF // GROUP
FEATURES = 256
STREAMS = 4 * HALF
BACK = 3 * HALF
BF16 = jnp.bfloat16
F32 = jnp.float32
VMEM_FORWARD = 56 << 20


def bands_kernel(base_ref, band_ref):
    for row in range(2 * GROUPS):
        spread = jnp.broadcast_to(base_ref[row : row + 1, :], (2 * ROWS, 2 * ROWS))
        rolled = pltpu.roll(spread, 0, 1, stride=1, stride_axis=0)
        band_ref[:, row * ROWS : (row + 1) * ROWS] = rolled[:, :ROWS].astype(BF16)


def bands(filters):
    zeros = jnp.zeros((GROUPS, TAPS), filters.dtype)
    causal = jnp.concatenate([zeros, filters], 1)
    anticausal = jnp.concatenate([filters[:, :1], zeros, filters[:, :0:-1]], 1)
    return pl.pallas_call(
        bands_kernel,
        out_shape=jax.ShapeDtypeStruct((2 * ROWS, 2 * GROUPS * ROWS), BF16),
    )(jnp.concatenate([causal, anticausal], 0))


def forward_kernel(place_ref, own_ref, other_ref, weight_ref, streams_ref, gate_ref, product_ref, mixed_ref, total):
    step = pl.program_id(0)
    core = place_ref[0]

    @pl.when(step == 0)
    def _():
        total[...] = jnp.zeros_like(total)

    tokens, cotangent, weight = [], [], []
    for values_ref, which in ((own_ref, core), (other_ref, 1 - core)):
        for y in range(2):
            tokens.append(values_ref[0, :, y, 0].reshape(2 * ROWS, FEATURES))
            cotangent.append(values_ref[0, :, y, 1].reshape(2 * ROWS, FEATURES))
            weight.append(weight_ref[pl.ds(2 * which, 2), 0, y, 0].reshape(FEATURES, STREAMS))
    tokens, cotangent = jnp.concatenate(tokens, 1), jnp.concatenate(cotangent, 1)
    weight = jnp.concatenate(weight, 0)
    total[:, :BACK] += jnp.dot(tokens, weight[:, :BACK], preferred_element_type=F32)
    total[:, BACK:] += jnp.dot(cotangent, weight[:, BACK:], preferred_element_type=F32)

    @pl.when(step == pl.num_programs(0) - 1)
    def _():
        turned = total[...].T
        streams = turned[:BACK].astype(BF16)
        streams_ref[...] = streams
        grad_gate = turned[BACK:]
        gate_ref[...] = grad_gate
        query, key, value = (streams[i * HALF : (i + 1) * HALF].astype(F32) for i in range(3))
        product_ref[...] = (key * value).astype(BF16)
        mixed_ref[...] = (grad_gate * query).astype(BF16)


def forward(place, own, other, weight):
    values = pl.BlockSpec((1, 2, 2, 2, ROWS, FEATURES), lambda j, p: (j, 0, 0, 0, 0, 0))
    whole = lambda height: pl.BlockSpec((height, 2 * ROWS), lambda j, p: (0, 0))
    shape = lambda height, kind: jax.ShapeDtypeStruct((height, 2 * ROWS), kind)
    return pl.pallas_call(
        forward_kernel,
        out_shape=(shape(BACK, BF16), shape(HALF, F32), shape(HALF, BF16), shape(HALF, BF16)),
        grid_spec=pltpu.PrefetchScalarGridSpec(
            num_scalar_prefetch=1,
            grid=(4,),
            in_specs=[
                values,
                values,
                pl.BlockSpec((4, 1, 2, 1, ROWS, STREAMS), lambda j, p: (j % 2, p[0], 0, j // 2, 0, 0)),
            ],
            out_specs=[whole(BACK), whole(HALF), whole(HALF), whole(HALF)],
            scratch_shapes=[pltpu.VMEM((2 * ROWS, STREAMS), F32)],
        ),
        compiler_params=pltpu.CompilerParams(vmem_limit_bytes=VMEM_FORWARD),
        cost_estimate=pl.CostEstimate(flops=1 << 30, bytes_accessed=9 << 20, transcendentals=0),
    )(place, own, other, weight)


def filtered(left, right, band):
    segments = [
        jnp.concatenate([left[s], right[s]], 1) for s in range(2)
    ]
    result = jnp.dot(jnp.concatenate(segments, 0), band, preferred_element_type=F32)
    return [
        jnp.concatenate(
            [
                result[s * HALF + g * GROUP : s * HALF + (g + 1) * GROUP, g * ROWS : (g + 1) * ROWS]
                for g in range(GROUPS)
            ],
            0,
        )
        for s in range(2)
    ]


def middle_kernel(
    place_ref, band_ref, streams_ref, gate_ref, product_ref, mixed_ref, before_ref, after_ref, terms_ref
):
    first = place_ref[1] == 0
    last = place_ref[1] == 15
    lanes = [slice(s * ROWS, (s + 1) * ROWS) for s in range(2)]
    product, mixed, before, after = (
        [ref[:, lanes[s]] for s in range(2)] for ref in (product_ref, mixed_ref, before_ref, after_ref)
    )
    zero = jnp.zeros_like(before[0])
    earlier = [jnp.where(first, zero, before[0]), jnp.where(first, before[0], before[1])]
    later = [jnp.where(last, after[1], after[0]), jnp.where(last, zero, after[1])]
    conv = filtered(earlier, product, band_ref[:, : GROUPS * ROWS])
    back = filtered(mixed, later, band_ref[:, GROUPS * ROWS :])
    for s in range(2):
        query, key, value = (
            streams_ref[i * HALF : (i + 1) * HALF, lanes[s]].astype(F32) for i in range(3)
        )
        terms_ref[:HALF, lanes[s]] = (gate_ref[:, lanes[s]] * conv[s]).astype(BF16)
        terms_ref[HALF : 2 * HALF, lanes[s]] = (back[s] * value).astype(BF16)
        terms_ref[2 * HALF : BACK, lanes[s]] = (back[s] * key).astype(BF16)
        terms_ref[BACK:, lanes[s]] = (query * conv[s]).astype(BF16)


TERMS_SPEC = pl.BlockSpec((STREAMS, 2 * ROWS), lambda j, p: (0, 0))


def middle(place, *operands):
    return pl.pallas_call(
        middle_kernel,
        out_shape=jax.ShapeDtypeStruct((STREAMS, 2 * ROWS), BF16),
        grid_spec=pltpu.PrefetchScalarGridSpec(
            num_scalar_prefetch=1,
            grid=(1,),
            in_specs=[pl.BlockSpec(value.shape, lambda j, p: (0, 0)) for value in operands],
            out_specs=TERMS_SPEC,
        ),
        cost_estimate=pl.CostEstimate(flops=1 << 28, bytes_accessed=3 << 20, transcendentals=0),
    )(place, *operands)


def backward_kernel(place_ref, own_ref, other_ref, weight_ref, *rest):
    *arrived, out_ref = rest
    core = place_ref[0]
    results = [0.0, 0.0]
    for terms_ref, which in ((own_ref, core), (other_ref, 1 - core)):
        weight = weight_ref[:, pl.ds(which, 1), 0, 0].reshape(FEATURES, STREAMS)
        results[0] += jnp.dot(weight[:, BACK:], terms_ref[BACK:], preferred_element_type=F32)
        results[1] += jnp.dot(weight[:, :BACK], terms_ref[:BACK], preferred_element_type=F32)
    for which in range(2):
        for h in range(2):
            part = results[which][:, h * ROWS : (h + 1) * ROWS]
            for ref in arrived:
                part += ref[h, 0, which].astype(F32)
            out_ref[h, 0, which] = part.astype(BF16)


def backward(steps, place, own, other, weight, arrived=()):
    spec = pl.BlockSpec((2, 1, 2, FEATURES, ROWS), lambda j, p: (0, j, 0, 0, 0))

    def weight_at(j, p):
        x = lax.rem(p[2] + steps, 4)
        return (lax.rem(x, 2) * 2 + p[0], 0, j, x // 2, 0, 0)

    return pl.pallas_call(
        backward_kernel,
        out_shape=jax.ShapeDtypeStruct((2, 2, 2, FEATURES, ROWS), BF16),
        grid_spec=pltpu.PrefetchScalarGridSpec(
            num_scalar_prefetch=1,
            grid=(2,),
            in_specs=[TERMS_SPEC, TERMS_SPEC, pl.BlockSpec((2, 2, 1, 1, ROWS, STREAMS), weight_at)]
            + [spec] * len(arrived),
            out_specs=spec,
        ),
        cost_estimate=pl.CostEstimate(flops=1 << 28, bytes_accessed=3 << 20, transcendentals=0),
    )(place, own, other, weight, *arrived)


def swapped(value, axes):
    return lax.all_to_all(value, axes, 0, 0, tiled=True)


def gathered(value, axes, count):
    return swapped(jnp.broadcast_to(value[None], (count,) + value.shape), axes)


def local(tokens, in_weight, out_weight, mr_filter, cotangent):
    half = lax.axis_index("h")
    position = lax.axis_index(("l", "z"))
    place = jnp.stack([lax.axis_index("core"), position, lax.axis_index("x")]).astype(jnp.int32)

    weight = jnp.concatenate([in_weight, out_weight.T[None]], 0)
    weight = weight.reshape(4, ROWS, 2, HALF).transpose(2, 1, 0, 3).reshape(2, 1, ROWS, STREAMS)
    weight = jnp.broadcast_to(weight, (2, 2, ROWS, STREAMS)).reshape(4, ROWS, STREAMS)
    weight = swapped(weight, ("h", "l"))
    values = jnp.stack([tokens, cotangent], 0)
    weight, values = lax.optimization_barrier((weight, values))
    weight = lax.all_gather(weight, ("z", "core"), axis=0).reshape(8, 2, 2, 2, ROWS, STREAMS)

    band = bands(lax.dynamic_slice_in_dim(mr_filter, half * GROUPS, GROUPS, 0))
    values = gathered(values, ("h", "ylo"), 4)
    values = gathered(values, "x", 4).reshape(4, 2, 2, 2, ROWS, FEATURES)
    values, band = lax.optimization_barrier((values, band))
    cross = [(0, 1), (1, 0)]
    other = lax.ppermute(values, "core", cross)

    streams, gate, product, mixed = forward(place, values, other, weight)
    ring = [(n, (n + 1) % 16) for n in range(16)]
    before = lax.ppermute(product, ("l", "z"), ring)
    after = lax.ppermute(mixed, ("l", "z"), [(b, a) for a, b in ring])

    terms = middle(place, band, streams, gate, product, mixed, before, after)
    other_terms = lax.ppermute(terms, "core", cross)
    arrived = []
    for steps in (2, 1, 3):
        part = backward(steps, place, terms, other_terms, weight)
        arrived.append(lax.ppermute(part, "x", [(n, (n + steps) % 4) for n in range(4)]))
    sums = backward(0, place, terms, other_terms, weight, arrived)
    sums = swapped(sums.reshape(4, 2, FEATURES, ROWS), ("h", "ylo")).astype(F32).sum(0).astype(BF16)
    return sums[0].T, sums[1].T


def solution(mesh):
    fine = Mesh(mesh.devices.reshape(SIZES), AXES)
    ctx, tp = AXES[:3], AXES[3:]
    return jax.shard_map(
        local,
        mesh=fine,
        in_specs=(P(ctx, tp), P(None, ctx, tp), P(tp, ctx), P(tp, None), P(ctx, tp)),
        out_specs=(P(ctx, tp), P(ctx, tp)),
        check_vma=False,
    )
```

```python
import jax
import jax.numpy as jnp
from jax import lax
from jax.experimental import pallas as pl
from jax.experimental.pallas import tpu as pltpu
from jax.sharding import Mesh, PartitionSpec as P

AXES = ("h", "l", "z", "ylo", "x", "core")
SIZES = (2, 2, 8, 2, 4, 2)
ROWS = 128
HALF = 128
TAPS = 128
GROUP = 16
GROUPS = HALF // GROUP
FEATURES = 256
STREAMS = 4 * HALF
BACK = 3 * HALF
BF16 = jnp.bfloat16
F32 = jnp.float32
VMEM_FORWARD = 56 << 20


def bands_kernel(base_ref, band_ref):
    for row in range(2 * GROUPS):
        spread = jnp.broadcast_to(base_ref[row : row + 1, :], (2 * ROWS, 2 * ROWS))
        rolled = pltpu.roll(spread, 0, 1, stride=1, stride_axis=0)
        band_ref[:, row * ROWS : (row + 1) * ROWS] = rolled[:, :ROWS].astype(BF16)


def bands(filters):
    zeros = jnp.zeros((GROUPS, TAPS), filters.dtype)
    causal = jnp.concatenate([zeros, filters], 1)
    anticausal = jnp.concatenate([filters[:, :1], zeros, filters[:, :0:-1]], 1)
    return pl.pallas_call(
        bands_kernel,
        out_shape=jax.ShapeDtypeStruct((2 * ROWS, 2 * GROUPS * ROWS), BF16),
    )(jnp.concatenate([causal, anticausal], 0))


def forward_kernel(place_ref, own_ref, other_ref, weight_ref, streams_ref, gate_ref, product_ref, mixed_ref, total):
    step = pl.program_id(0)
    core = place_ref[0]

    @pl.when(step == 0)
    def _():
        total[...] = jnp.zeros_like(total)

    tokens, cotangent, weight = [], [], []
    for values_ref, which in ((own_ref, core), (other_ref, 1 - core)):
        for y in range(2):
            tokens.append(values_ref[0, :, y, 0].reshape(2 * ROWS, FEATURES))
            cotangent.append(values_ref[0, :, y, 1].reshape(2 * ROWS, FEATURES))
            weight.append(weight_ref[pl.ds(2 * which, 2), 0, y, 0].reshape(FEATURES, STREAMS))
    tokens, cotangent = jnp.concatenate(tokens, 1), jnp.concatenate(cotangent, 1)
    weight = jnp.concatenate(weight, 0)
    total[:, :BACK] += jnp.dot(tokens, weight[:, :BACK], preferred_element_type=F32)
    total[:, BACK:] += jnp.dot(cotangent, weight[:, BACK:], preferred_element_type=F32)

    @pl.when(step == pl.num_programs(0) - 1)
    def _():
        turned = total[...].T
        streams = turned[:BACK].astype(BF16)
        streams_ref[...] = streams
        grad_gate = turned[BACK:]
        gate_ref[...] = grad_gate
        query, key, value = (streams[i * HALF : (i + 1) * HALF].astype(F32) for i in range(3))
        product_ref[...] = (key * value).astype(BF16)
        mixed_ref[...] = (grad_gate * query).astype(BF16)


def forward(place, own, other, weight):
    values = pl.BlockSpec((1, 2, 2, 2, ROWS, FEATURES), lambda j, p: (j, 0, 0, 0, 0, 0))
    whole = lambda height: pl.BlockSpec((height, 2 * ROWS), lambda j, p: (0, 0))
    shape = lambda height, kind: jax.ShapeDtypeStruct((height, 2 * ROWS), kind)
    return pl.pallas_call(
        forward_kernel,
        out_shape=(shape(BACK, BF16), shape(HALF, F32), shape(HALF, BF16), shape(HALF, BF16)),
        grid_spec=pltpu.PrefetchScalarGridSpec(
            num_scalar_prefetch=1,
            grid=(4,),
            in_specs=[
                values,
                values,
                pl.BlockSpec((4, 1, 2, 1, ROWS, STREAMS), lambda j, p: (j % 2, p[0], 0, j // 2, 0, 0)),
            ],
            out_specs=[whole(BACK), whole(HALF), whole(HALF), whole(HALF)],
            scratch_shapes=[pltpu.VMEM((2 * ROWS, STREAMS), F32)],
        ),
        compiler_params=pltpu.CompilerParams(vmem_limit_bytes=VMEM_FORWARD),
        cost_estimate=pl.CostEstimate(flops=1 << 30, bytes_accessed=9 << 20, transcendentals=0),
    )(place, own, other, weight)


def filtered(left, right, band):
    segments = [
        jnp.concatenate([left[s], right[s]], 1) for s in range(2)
    ]
    result = jnp.dot(jnp.concatenate(segments, 0), band, preferred_element_type=F32)
    return [
        jnp.concatenate(
            [
                result[s * HALF + g * GROUP : s * HALF + (g + 1) * GROUP, g * ROWS : (g + 1) * ROWS]
                for g in range(GROUPS)
            ],
            0,
        )
        for s in range(2)
    ]


def middle_kernel(
    place_ref, band_ref, streams_ref, gate_ref, product_ref, mixed_ref, before_ref, after_ref, terms_ref
):
    first = place_ref[1] == 0
    last = place_ref[1] == 15
    lanes = [slice(s * ROWS, (s + 1) * ROWS) for s in range(2)]
    product, mixed, before, after = (
        [ref[:, lanes[s]] for s in range(2)] for ref in (product_ref, mixed_ref, before_ref, after_ref)
    )
    zero = jnp.zeros_like(before[0])
    earlier = [jnp.where(first, zero, before[0]), jnp.where(first, before[0], before[1])]
    later = [jnp.where(last, after[1], after[0]), jnp.where(last, zero, after[1])]
    conv = filtered(earlier, product, band_ref[:, : GROUPS * ROWS])
    back = filtered(mixed, later, band_ref[:, GROUPS * ROWS :])
    for s in range(2):
        query, key, value = (
            streams_ref[i * HALF : (i + 1) * HALF, lanes[s]].astype(F32) for i in range(3)
        )
        terms_ref[:HALF, lanes[s]] = (gate_ref[:, lanes[s]] * conv[s]).astype(BF16)
        terms_ref[HALF : 2 * HALF, lanes[s]] = (back[s] * value).astype(BF16)
        terms_ref[2 * HALF : BACK, lanes[s]] = (back[s] * key).astype(BF16)
        terms_ref[BACK:, lanes[s]] = (query * conv[s]).astype(BF16)


TERMS_SPEC = pl.BlockSpec((STREAMS, 2 * ROWS), lambda j, p: (0, 0))


def middle(place, *operands):
    return pl.pallas_call(
        middle_kernel,
        out_shape=jax.ShapeDtypeStruct((STREAMS, 2 * ROWS), BF16),
        grid_spec=pltpu.PrefetchScalarGridSpec(
            num_scalar_prefetch=1,
            grid=(1,),
            in_specs=[pl.BlockSpec(value.shape, lambda j, p: (0, 0)) for value in operands],
            out_specs=TERMS_SPEC,
        ),
        cost_estimate=pl.CostEstimate(flops=1 << 28, bytes_accessed=3 << 20, transcendentals=0),
    )(place, *operands)


def backward_kernel(place_ref, own_ref, other_ref, weight_ref, *rest):
    *arrived, out_ref = rest
    core = place_ref[0]
    results = [0.0, 0.0]
    for terms_ref, which in ((own_ref, core), (other_ref, 1 - core)):
        weight = weight_ref[:, pl.ds(which, 1), 0, 0].reshape(FEATURES, STREAMS)
        results[0] += jnp.dot(weight[:, BACK:], terms_ref[BACK:], preferred_element_type=F32)
        results[1] += jnp.dot(weight[:, :BACK], terms_ref[:BACK], preferred_element_type=F32)
    for which in range(2):
        for h in range(2):
            part = results[which][:, h * ROWS : (h + 1) * ROWS]
            for ref in arrived:
                part += ref[h, 0, which].astype(F32)
            out_ref[h, 0, which] = part.astype(BF16)


def backward(steps, place, own, other, weight, arrived=()):
    spec = pl.BlockSpec((2, 1, 2, FEATURES, ROWS), lambda j, p: (0, j, 0, 0, 0))

    def weight_at(j, p):
        x = lax.rem(p[2] + steps, 4)
        return (lax.rem(x, 2) * 2 + p[0], 0, j, x // 2, 0, 0)

    return pl.pallas_call(
        backward_kernel,
        out_shape=jax.ShapeDtypeStruct((2, 2, 2, FEATURES, ROWS), BF16),
        grid_spec=pltpu.PrefetchScalarGridSpec(
            num_scalar_prefetch=1,
            grid=(2,),
            in_specs=[TERMS_SPEC, TERMS_SPEC, pl.BlockSpec((2, 2, 1, 1, ROWS, STREAMS), weight_at)]
            + [spec] * len(arrived),
            out_specs=spec,
        ),
        cost_estimate=pl.CostEstimate(flops=1 << 28, bytes_accessed=3 << 20, transcendentals=0),
    )(place, own, other, weight, *arrived)


def swapped(value, axes):
    return lax.all_to_all(value, axes, 0, 0, tiled=True)


def gathered(value, axes, count):
    return swapped(jnp.broadcast_to(value[None], (count,) + value.shape), axes)


def ring_gathered(piece):
    z, core = lax.axis_index("z"), lax.axis_index("core")
    away = 2 * core - 1
    ring = [(2 * n + c, 2 * ((n + 1 - 2 * c) % 8) + c) for n in range(8) for c in range(2)]
    cross = [(0, 1), (1, 0)]
    current = gathered(piece, "core", 2)
    whole = jnp.zeros((8,) + current.shape, current.dtype)
    whole = lax.dynamic_update_slice_in_dim(whole, current[None], z, 0)
    for step in range(1, 4):
        current = lax.ppermute(current, ("z", "core"), ring)
        passed = lax.ppermute(current, "core", cross)
        whole = lax.dynamic_update_slice_in_dim(whole, current[None], (z + away * step) % 8, 0)
        whole = lax.dynamic_update_slice_in_dim(whole, passed[None], (z - away * step) % 8, 0)
    part = lax.dynamic_slice_in_dim(current, core, 1, 0)
    part = lax.ppermute(part, ("z", "core"), ring)
    passed = lax.ppermute(part, "core", cross)
    zero = jnp.zeros_like(z)
    at = lambda c: ((z + 4) % 8, c) + (zero,) * 3
    whole = lax.dynamic_update_slice(whole, part[None], at(core))
    return lax.dynamic_update_slice(whole, passed[None], at(1 - core))


def local(tokens, in_weight, out_weight, mr_filter, cotangent):
    half = lax.axis_index("h")
    position = lax.axis_index(("l", "z"))
    place = jnp.stack([lax.axis_index("core"), position, lax.axis_index("x")]).astype(jnp.int32)

    weight = jnp.concatenate([in_weight, out_weight.T[None]], 0)
    weight = weight.reshape(4, ROWS, 2, HALF).transpose(2, 1, 0, 3).reshape(2, 1, ROWS, STREAMS)
    weight = jnp.broadcast_to(weight, (2, 2, ROWS, STREAMS)).reshape(4, ROWS, STREAMS)
    weight = swapped(weight, ("h", "l"))
    values = jnp.stack([tokens, cotangent], 0)
    weight, values = lax.optimization_barrier((weight, values))
    weight = ring_gathered(weight).reshape(8, 2, 2, 2, ROWS, STREAMS)

    band = bands(lax.dynamic_slice_in_dim(mr_filter, half * GROUPS, GROUPS, 0))
    values = gathered(values, ("h", "ylo"), 4)
    values = gathered(values, "x", 4).reshape(4, 2, 2, 2, ROWS, FEATURES)
    values, band = lax.optimization_barrier((values, band))
    cross = [(0, 1), (1, 0)]
    other = lax.ppermute(values, "core", cross)

    streams, gate, product, mixed = forward(place, values, other, weight)
    ring = [(n, (n + 1) % 16) for n in range(16)]
    before = lax.ppermute(product, ("l", "z"), ring)
    after = lax.ppermute(mixed, ("l", "z"), [(b, a) for a, b in ring])

    terms = middle(place, band, streams, gate, product, mixed, before, after)
    other_terms = lax.ppermute(terms, "core", cross)
    arrived = []
    for steps in (2, 1, 3):
        part = backward(steps, place, terms, other_terms, weight)
        arrived.append(lax.ppermute(part, "x", [(n, (n + steps) % 4) for n in range(4)]))
    sums = backward(0, place, terms, other_terms, weight, arrived)
    sums = swapped(sums.reshape(4, 2, FEATURES, ROWS), ("h", "ylo")).astype(F32).sum(0).astype(BF16)
    return sums[0].T, sums[1].T


def solution(mesh):
    fine = Mesh(mesh.devices.reshape(SIZES), AXES)
    ctx, tp = AXES[:3], AXES[3:]
    return jax.shard_map(
        local,
        mesh=fine,
        in_specs=(P(ctx, tp), P(None, ctx, tp), P(tp, ctx), P(tp, None), P(ctx, tp)),
        out_specs=(P(ctx, tp), P(ctx, tp)),
        check_vma=False,
    )
```

```python
import jax
import jax.numpy as jnp
from jax import lax
from jax.experimental import pallas as pl
from jax.experimental.pallas import tpu as pltpu
from jax.sharding import Mesh, PartitionSpec as P

AXES = ("h", "l", "z", "ylo", "x", "core")
SIZES = (2, 2, 8, 2, 4, 2)
ROWS = 128
HALF = 128
TAPS = 128
GROUP = 16
GROUPS = HALF // GROUP
FEATURES = 256
STREAMS = 4 * HALF
BACK = 3 * HALF
BF16 = jnp.bfloat16
F32 = jnp.float32
VMEM_FORWARD = 52 << 20


def bands_kernel(base_ref, band_ref):
    for row in range(2 * GROUPS):
        spread = jnp.broadcast_to(base_ref[row : row + 1, :], (2 * ROWS, 2 * ROWS))
        rolled = pltpu.roll(spread, 0, 1, stride=1, stride_axis=0)
        band_ref[:, row * ROWS : (row + 1) * ROWS] = rolled[:, :ROWS].astype(BF16)


def bands(filters):
    zeros = jnp.zeros((GROUPS, TAPS), filters.dtype)
    causal = jnp.concatenate([zeros, filters], 1)
    anticausal = jnp.concatenate([filters[:, :1], zeros, filters[:, :0:-1]], 1)
    return pl.pallas_call(
        bands_kernel,
        out_shape=jax.ShapeDtypeStruct((2 * ROWS, 2 * GROUPS * ROWS), BF16),
    )(jnp.concatenate([causal, anticausal], 0))


def forward_kernel(place_ref, own_ref, other_ref, weight_ref, streams_ref, gate_ref, product_ref, mixed_ref, total):
    step = pl.program_id(0)
    core = place_ref[0]

    @pl.when(step == 0)
    def _():
        total[...] = jnp.zeros_like(total)

    tokens, cotangent, weight = [], [], []
    for values_ref, which in ((own_ref, core), (other_ref, 1 - core)):
        for y in range(2):
            tokens.append(values_ref[0, :, y, 0].reshape(2 * ROWS, FEATURES))
            cotangent.append(values_ref[0, :, y, 1].reshape(2 * ROWS, FEATURES))
            weight.append(weight_ref[pl.ds(2 * which, 2), 0, y, 0].reshape(FEATURES, STREAMS))
    tokens, cotangent = jnp.concatenate(tokens, 1), jnp.concatenate(cotangent, 1)
    weight = jnp.concatenate(weight, 0)
    total[:, :BACK] += jnp.dot(tokens, weight[:, :BACK], preferred_element_type=F32)
    total[:, BACK:] += jnp.dot(cotangent, weight[:, BACK:], preferred_element_type=F32)

    @pl.when(step == pl.num_programs(0) - 1)
    def _():
        turned = total[...].T
        streams = turned[:BACK].astype(BF16)
        streams_ref[...] = streams
        grad_gate = turned[BACK:]
        gate_ref[...] = grad_gate
        query, key, value = (streams[i * HALF : (i + 1) * HALF].astype(F32) for i in range(3))
        product_ref[...] = (key * value).astype(BF16)
        mixed_ref[...] = (grad_gate * query).astype(BF16)


def forward(place, own, other, weight):
    values = pl.BlockSpec((1, 2, 2, 2, ROWS, FEATURES), lambda j, p: (j, 0, 0, 0, 0, 0))
    whole = lambda height: pl.BlockSpec((height, 2 * ROWS), lambda j, p: (0, 0))
    shape = lambda height, kind: jax.ShapeDtypeStruct((height, 2 * ROWS), kind)
    return pl.pallas_call(
        forward_kernel,
        out_shape=(shape(BACK, BF16), shape(HALF, F32), shape(HALF, BF16), shape(HALF, BF16)),
        grid_spec=pltpu.PrefetchScalarGridSpec(
            num_scalar_prefetch=1,
            grid=(4,),
            in_specs=[
                values,
                values,
                pl.BlockSpec((4, 1, 2, 1, ROWS, STREAMS), lambda j, p: (j % 2, p[0], 0, j // 2, 0, 0)),
            ],
            out_specs=[whole(BACK), whole(HALF), whole(HALF), whole(HALF)],
            scratch_shapes=[pltpu.VMEM((2 * ROWS, STREAMS), F32)],
        ),
        compiler_params=pltpu.CompilerParams(vmem_limit_bytes=VMEM_FORWARD),
        cost_estimate=pl.CostEstimate(flops=1 << 30, bytes_accessed=9 << 20, transcendentals=0),
    )(place, own, other, weight)


def filtered(left, right, band):
    segments = [
        jnp.concatenate([left[s], right[s]], 1) for s in range(2)
    ]
    result = jnp.dot(jnp.concatenate(segments, 0), band, preferred_element_type=F32)
    return [
        jnp.concatenate(
            [
                result[s * HALF + g * GROUP : s * HALF + (g + 1) * GROUP, g * ROWS : (g + 1) * ROWS]
                for g in range(GROUPS)
            ],
            0,
        )
        for s in range(2)
    ]


def middle_kernel(
    place_ref, band_ref, streams_ref, gate_ref, product_ref, mixed_ref, before_ref, after_ref, terms_ref
):
    first = place_ref[1] == 0
    last = place_ref[1] == 15
    lanes = [slice(s * ROWS, (s + 1) * ROWS) for s in range(2)]
    product, mixed, before, after = (
        [ref[:, lanes[s]] for s in range(2)] for ref in (product_ref, mixed_ref, before_ref, after_ref)
    )
    zero = jnp.zeros_like(before[0])
    earlier = [jnp.where(first, zero, before[0]), jnp.where(first, before[0], before[1])]
    later = [jnp.where(last, after[1], after[0]), jnp.where(last, zero, after[1])]
    conv = filtered(earlier, product, band_ref[:, : GROUPS * ROWS])
    back = filtered(mixed, later, band_ref[:, GROUPS * ROWS :])
    for s in range(2):
        query, key, value = (
            streams_ref[i * HALF : (i + 1) * HALF, lanes[s]].astype(F32) for i in range(3)
        )
        terms_ref[:HALF, lanes[s]] = (gate_ref[:, lanes[s]] * conv[s]).astype(BF16)
        terms_ref[HALF : 2 * HALF, lanes[s]] = (back[s] * value).astype(BF16)
        terms_ref[2 * HALF : BACK, lanes[s]] = (back[s] * key).astype(BF16)
        terms_ref[BACK:, lanes[s]] = (query * conv[s]).astype(BF16)


def on_chip(kernel, out_shape, operands, flops):
    smem, vmem = pl.BlockSpec(memory_space=pltpu.SMEM), pl.BlockSpec(memory_space=pltpu.VMEM)
    return pl.pallas_call(
        kernel,
        out_shape=out_shape,
        in_specs=[smem] + [vmem] * (len(operands) - 1),
        out_specs=jax.tree.map(lambda _: vmem, out_shape),
        compiler_params=pltpu.CompilerParams(vmem_limit_bytes=24 << 20),
        cost_estimate=pl.CostEstimate(flops=flops, bytes_accessed=1 << 20, transcendentals=0),
    )(*operands)


def middle(*operands):
    return on_chip(middle_kernel, jax.ShapeDtypeStruct((STREAMS, 2 * ROWS), BF16), operands, 1 << 28)


MIXED, GRAD = 0, 1
BLOCK = (2, 2, FEATURES, ROWS)


def backward(steps, parts, operands, arrived=(), last=False):
    def kernel(place_ref, own_ref, other_ref, weight_ref, *refs):
        *arrived_refs, out_ref = refs
        core = place_ref[0]
        x = lax.rem(place_ref[2] + steps, 4)
        for y in range(2):
            for at, part in enumerate(parts):
                rows = slice(0, BACK) if part == GRAD else slice(BACK, STREAMS)
                result = 0.0
                for terms_ref, which in ((own_ref, core), (other_ref, 1 - core)):
                    weight = weight_ref[lax.rem(x, 2), :, which, y, lax.div(x, 2)].reshape(FEATURES, STREAMS)
                    result += jnp.dot(weight[:, rows], terms_ref[rows], preferred_element_type=F32)
                for h in range(2):
                    total = result[:, h * ROWS : (h + 1) * ROWS]
                    for (held, _), ref in zip(arrived, arrived_refs):
                        if part in held:
                            total += ref[held.index(part), h, y].astype(F32)
                    if last:
                        out_ref[2 * h + y, at] = total.astype(BF16)
                    else:
                        out_ref[at, h, y] = total.astype(BF16)

    shape = (4, len(parts)) + BLOCK[2:] if last else (len(parts),) + BLOCK
    return on_chip(
        kernel,
        jax.ShapeDtypeStruct(shape, BF16),
        operands + tuple(array for _, array in arrived),
        len(parts) << 27,
    )


def pack_kernel(in_ref, out_ref, packed_ref):
    for h in range(2):
        chans = slice(h * HALF, (h + 1) * HALF)
        turned = out_ref[chans].astype(F32).T.astype(BF16)
        for l in range(2):
            for stream in range(3):
                packed_ref[2 * h + l, :, stream * HALF : (stream + 1) * HALF] = in_ref[stream, :, chans]
            packed_ref[2 * h + l, :, BACK:] = turned


def packed(in_weight, out_weight):
    vmem = pl.BlockSpec(memory_space=pltpu.VMEM)
    return pl.pallas_call(
        pack_kernel,
        out_shape=jax.ShapeDtypeStruct((4, ROWS, STREAMS), BF16),
        in_specs=[vmem] * 2,
        out_specs=vmem,
    )(in_weight, out_weight)


def finish_kernel(parts_ref, mixed_ref, grad_ref):
    for at, ref in ((MIXED, mixed_ref), (GRAD, grad_ref)):
        total = parts_ref[0, at].astype(F32)
        for source in range(1, 4):
            total += parts_ref[source, at].astype(F32)
        ref[...] = total.T.astype(BF16)


def finish(parts):
    vmem = pl.BlockSpec(memory_space=pltpu.VMEM)
    return pl.pallas_call(
        finish_kernel,
        out_shape=(jax.ShapeDtypeStruct((ROWS, FEATURES), BF16),) * 2,
        in_specs=[vmem],
        out_specs=(vmem, vmem),
    )(parts)


def swapped(value, axes):
    return lax.all_to_all(value, axes, 0, 0, tiled=True)


def gathered(value, axes, count):
    return swapped(jnp.broadcast_to(value[None], (count,) + value.shape), axes)


def local(tokens, in_weight, out_weight, mr_filter, cotangent):
    half, core = lax.axis_index("h"), lax.axis_index("core")
    position = lax.axis_index(("l", "z"))
    place = jnp.stack([core, position, lax.axis_index("x")]).astype(jnp.int32)

    weight = swapped(packed(in_weight, out_weight), ("h", "l"))
    values = jnp.stack([tokens, cotangent], 0)
    weight, values = lax.optimization_barrier((weight, values))
    weight = lax.all_gather(weight, ("z", "core"), axis=0).reshape(8, 2, 2, 2, ROWS, STREAMS)

    band = bands(lax.dynamic_slice_in_dim(mr_filter, half * GROUPS, GROUPS, 0))
    values = gathered(values, ("h", "ylo"), 4)
    values = gathered(values, "x", 4).reshape(4, 2, 2, 2, ROWS, FEATURES)
    values, band = lax.optimization_barrier((values, band))
    cross = [(0, 1), (1, 0)]
    other = lax.ppermute(values, "core", cross)

    streams, gate, product, mixed = forward(place, values, other, weight)
    ring = [(n, (n + 1) % 16) for n in range(16)]
    before = lax.ppermute(product, ("l", "z"), ring)
    after = lax.ppermute(mixed, ("l", "z"), [(b, a) for a, b in ring])
    weight, gate = lax.optimization_barrier((weight, gate))
    weight = lax.dynamic_index_in_dim(
        weight.reshape(2, 2, 2, 2, 2, 2, ROWS, STREAMS), core, 1, keepdims=False
    )

    terms = middle(place, band, streams, gate, product, mixed, before, after)
    operands = (place, terms, lax.ppermute(terms, "core", cross), weight)

    def sent(array, steps):
        return lax.ppermute(array, "x", [(n, (n + steps) % 4) for n in range(4)])

    both = (MIXED, GRAD)
    relayed = sent(backward(2, (GRAD,), operands), 3)
    direct = sent(backward(2, (MIXED,), operands), 2)
    right = sent(backward(1, both, operands), 1)
    left = sent(backward(3, both, operands, [((GRAD,), relayed)]), 3)
    sums = backward(0, both, operands, [((MIXED,), direct), (both, right), (both, left)], last=True)
    return finish(swapped(sums, ("h", "ylo")))


def solution(mesh):
    fine = Mesh(mesh.devices.reshape(SIZES), AXES)
    ctx, tp = AXES[:3], AXES[3:]
    return jax.shard_map(
        local,
        mesh=fine,
        in_specs=(P(ctx, tp), P(None, ctx, tp), P(tp, ctx), P(tp, None), P(ctx, tp)),
        out_specs=(P(ctx, tp), P(ctx, tp)),
        check_vma=False,
    )
```

```python
import jax
import jax.numpy as jnp
from jax import lax
from jax.experimental import pallas as pl
from jax.experimental.pallas import tpu as pltpu
from jax.sharding import Mesh, PartitionSpec as P

AXES = ("h", "l", "z", "ylo", "x", "core")
SIZES = (2, 2, 8, 2, 4, 2)
ROWS = 128
HALF = 128
TAPS = 128
GROUP = 16
GROUPS = HALF // GROUP
FEATURES = 256
STREAMS = 4 * HALF
BACK = 3 * HALF
BF16 = jnp.bfloat16
F32 = jnp.float32
VMEM_FORWARD = 52 << 20


def bands_kernel(base_ref, band_ref):
    for row in range(2 * GROUPS):
        spread = jnp.broadcast_to(base_ref[row : row + 1, :], (2 * ROWS, 2 * ROWS))
        rolled = pltpu.roll(spread, 0, 1, stride=1, stride_axis=0)
        band_ref[:, row * ROWS : (row + 1) * ROWS] = rolled[:, :ROWS].astype(BF16)


def bands(filters):
    zeros = jnp.zeros((GROUPS, TAPS), filters.dtype)
    causal = jnp.concatenate([zeros, filters], 1)
    anticausal = jnp.concatenate([filters[:, :1], zeros, filters[:, :0:-1]], 1)
    return pl.pallas_call(
        bands_kernel,
        out_shape=jax.ShapeDtypeStruct((2 * ROWS, 2 * GROUPS * ROWS), BF16),
    )(jnp.concatenate([causal, anticausal], 0))


def forward_kernel(place_ref, own_ref, other_ref, weight_ref, streams_ref, gate_ref, product_ref, mixed_ref, total):
    step = pl.program_id(0)
    core = place_ref[0]

    @pl.when(step == 0)
    def _():
        total[...] = jnp.zeros_like(total)

    tokens, cotangent, weight = [], [], []
    for values_ref, which in ((own_ref, core), (other_ref, 1 - core)):
        for y in range(2):
            tokens.append(values_ref[0, :, y, 0].reshape(2 * ROWS, FEATURES))
            cotangent.append(values_ref[0, :, y, 1].reshape(2 * ROWS, FEATURES))
            weight.append(weight_ref[pl.ds(2 * which, 2), 0, y, 0].reshape(FEATURES, STREAMS))
    tokens, cotangent = jnp.concatenate(tokens, 1), jnp.concatenate(cotangent, 1)
    weight = jnp.concatenate(weight, 0)
    total[:, :BACK] += jnp.dot(tokens, weight[:, :BACK], preferred_element_type=F32)
    total[:, BACK:] += jnp.dot(cotangent, weight[:, BACK:], preferred_element_type=F32)

    @pl.when(step == pl.num_programs(0) - 1)
    def _():
        turned = total[...].T
        streams = turned[:BACK].astype(BF16)
        streams_ref[...] = streams
        grad_gate = turned[BACK:]
        gate_ref[...] = grad_gate
        query, key, value = (streams[i * HALF : (i + 1) * HALF].astype(F32) for i in range(3))
        product_ref[...] = (key * value).astype(BF16)
        mixed_ref[...] = (grad_gate * query).astype(BF16)


def forward(place, own, other, weight):
    values = pl.BlockSpec((1, 2, 2, 2, ROWS, FEATURES), lambda j, p: (j, 0, 0, 0, 0, 0))
    whole = lambda height: pl.BlockSpec((height, 2 * ROWS), lambda j, p: (0, 0))
    shape = lambda height, kind: jax.ShapeDtypeStruct((height, 2 * ROWS), kind)
    return pl.pallas_call(
        forward_kernel,
        out_shape=(shape(BACK, BF16), shape(HALF, F32), shape(HALF, BF16), shape(HALF, BF16)),
        grid_spec=pltpu.PrefetchScalarGridSpec(
            num_scalar_prefetch=1,
            grid=(4,),
            in_specs=[
                values,
                values,
                pl.BlockSpec((4, 1, 2, 1, ROWS, STREAMS), lambda j, p: (j % 2, p[0], 0, j // 2, 0, 0)),
            ],
            out_specs=[whole(BACK), whole(HALF), whole(HALF), whole(HALF)],
            scratch_shapes=[pltpu.VMEM((2 * ROWS, STREAMS), F32)],
        ),
        compiler_params=pltpu.CompilerParams(vmem_limit_bytes=VMEM_FORWARD),
        cost_estimate=pl.CostEstimate(flops=1 << 30, bytes_accessed=9 << 20, transcendentals=0),
    )(place, own, other, weight)


def filtered(left, right, band):
    segments = [
        jnp.concatenate([left[s], right[s]], 1) for s in range(2)
    ]
    result = jnp.dot(jnp.concatenate(segments, 0), band, preferred_element_type=F32)
    return [
        jnp.concatenate(
            [
                result[s * HALF + g * GROUP : s * HALF + (g + 1) * GROUP, g * ROWS : (g + 1) * ROWS]
                for g in range(GROUPS)
            ],
            0,
        )
        for s in range(2)
    ]


def middle_kernel(
    place_ref, band_ref, streams_ref, gate_ref, product_ref, mixed_ref, before_ref, after_ref, terms_ref
):
    first = place_ref[1] == 0
    last = place_ref[1] == 15
    lanes = [slice(s * ROWS, (s + 1) * ROWS) for s in range(2)]
    product, mixed, before, after = (
        [ref[:, lanes[s]] for s in range(2)] for ref in (product_ref, mixed_ref, before_ref, after_ref)
    )
    zero = jnp.zeros_like(before[0])
    earlier = [jnp.where(first, zero, before[0]), jnp.where(first, before[0], before[1])]
    later = [jnp.where(last, after[1], after[0]), jnp.where(last, zero, after[1])]
    conv = filtered(earlier, product, band_ref[:, : GROUPS * ROWS])
    back = filtered(mixed, later, band_ref[:, GROUPS * ROWS :])
    for s in range(2):
        query, key, value = (
            streams_ref[i * HALF : (i + 1) * HALF, lanes[s]].astype(F32) for i in range(3)
        )
        terms_ref[:HALF, lanes[s]] = (gate_ref[:, lanes[s]] * conv[s]).astype(BF16)
        terms_ref[HALF : 2 * HALF, lanes[s]] = (back[s] * value).astype(BF16)
        terms_ref[2 * HALF : BACK, lanes[s]] = (back[s] * key).astype(BF16)
        terms_ref[BACK:, lanes[s]] = (query * conv[s]).astype(BF16)


def on_chip(kernel, out_shape, operands, flops):
    smem, vmem = pl.BlockSpec(memory_space=pltpu.SMEM), pl.BlockSpec(memory_space=pltpu.VMEM)
    return pl.pallas_call(
        kernel,
        out_shape=out_shape,
        in_specs=[smem] + [vmem] * (len(operands) - 1),
        out_specs=jax.tree.map(lambda _: vmem, out_shape),
        compiler_params=pltpu.CompilerParams(vmem_limit_bytes=24 << 20),
        cost_estimate=pl.CostEstimate(flops=flops, bytes_accessed=1 << 20, transcendentals=0),
    )(*operands)


def middle(*operands):
    return on_chip(middle_kernel, jax.ShapeDtypeStruct((STREAMS, 2 * ROWS), BF16), operands, 1 << 28)


MIXED, GRAD = 0, 1
BLOCK = (2, 2, FEATURES, ROWS)


def backward(steps, parts, operands, arrived=(), last=False):
    def kernel(place_ref, own_ref, other_ref, weight_ref, *refs):
        *arrived_refs, out_ref = refs
        core = place_ref[0]
        x = lax.rem(place_ref[2] + steps, 4)
        for y in range(2):
            for at, part in enumerate(parts):
                rows = slice(0, BACK) if part == GRAD else slice(BACK, STREAMS)
                result = 0.0
                for terms_ref, which in ((own_ref, core), (other_ref, 1 - core)):
                    weight = weight_ref[lax.rem(x, 2), :, which, y, lax.div(x, 2)].reshape(FEATURES, STREAMS)
                    result += jnp.dot(weight[:, rows], terms_ref[rows], preferred_element_type=F32)
                for h in range(2):
                    total = result[:, h * ROWS : (h + 1) * ROWS]
                    for (held, _), ref in zip(arrived, arrived_refs):
                        if part in held:
                            total += ref[held.index(part), h, y].astype(F32)
                    if last:
                        out_ref[2 * h + y, at] = total.astype(BF16)
                    else:
                        out_ref[at, h, y] = total.astype(BF16)

    shape = (4, len(parts)) + BLOCK[2:] if last else (len(parts),) + BLOCK
    return on_chip(
        kernel,
        jax.ShapeDtypeStruct(shape, BF16),
        operands + tuple(array for _, array in arrived),
        len(parts) << 27,
    )


def pack_kernel(in_ref, out_ref, packed_ref):
    for h in range(2):
        chans = slice(h * HALF, (h + 1) * HALF)
        turned = out_ref[chans].astype(F32).T.astype(BF16)
        for l in range(2):
            for stream in range(3):
                packed_ref[2 * h + l, :, stream * HALF : (stream + 1) * HALF] = in_ref[stream, :, chans]
            packed_ref[2 * h + l, :, BACK:] = turned


def packed(in_weight, out_weight):
    vmem = pl.BlockSpec(memory_space=pltpu.VMEM)
    return pl.pallas_call(
        pack_kernel,
        out_shape=jax.ShapeDtypeStruct((4, ROWS, STREAMS), BF16),
        in_specs=[vmem] * 2,
        out_specs=vmem,
    )(in_weight, out_weight)


def finish_kernel(parts_ref, mixed_ref, grad_ref):
    for at, ref in ((MIXED, mixed_ref), (GRAD, grad_ref)):
        total = parts_ref[0, at].astype(F32)
        for source in range(1, 4):
            total += parts_ref[source, at].astype(F32)
        ref[...] = total.T.astype(BF16)


def finish(parts):
    vmem = pl.BlockSpec(memory_space=pltpu.VMEM)
    return pl.pallas_call(
        finish_kernel,
        out_shape=(jax.ShapeDtypeStruct((ROWS, FEATURES), BF16),) * 2,
        in_specs=[vmem],
        out_specs=(vmem, vmem),
    )(parts)


def swapped(value, axes):
    return lax.all_to_all(value, axes, 0, 0, tiled=True)


def gathered(value, axes, count):
    return swapped(jnp.broadcast_to(value[None], (count,) + value.shape), axes)


def local(tokens, in_weight, out_weight, mr_filter, cotangent):
    half, core = lax.axis_index("h"), lax.axis_index("core")
    position = lax.axis_index(("l", "z"))
    place = jnp.stack([core, position, lax.axis_index("x")]).astype(jnp.int32)

    weight = swapped(packed(in_weight, out_weight), ("h", "l"))
    values = jnp.stack([tokens, cotangent], 0)
    weight, values = lax.optimization_barrier((weight, values))
    weight = lax.all_gather(weight, ("z", "core"), axis=0).reshape(8, 2, 2, 2, ROWS, STREAMS)

    band = bands(lax.dynamic_slice_in_dim(mr_filter, half * GROUPS, GROUPS, 0))
    values = gathered(values, ("h", "ylo"), 4)
    values = gathered(values, "x", 4).reshape(4, 2, 2, 2, ROWS, FEATURES)
    values, band = lax.optimization_barrier((values, band))
    cross = [(0, 1), (1, 0)]
    other = lax.ppermute(values, "core", cross)

    streams, gate, product, mixed = forward(place, values, other, weight)
    ring = [(n, (n + 1) % 16) for n in range(16)]
    before = lax.ppermute(product, ("l", "z"), ring)
    after = lax.ppermute(mixed, ("l", "z"), [(b, a) for a, b in ring])
    weight, gate = lax.optimization_barrier((weight, gate))
    weight = lax.dynamic_index_in_dim(
        weight.reshape(2, 2, 2, 2, 2, 2, ROWS, STREAMS), core, 1, keepdims=False
    )

    before, weight = lax.optimization_barrier((before, weight))

    terms = middle(place, band, streams, gate, product, mixed, before, after)
    other_terms = lax.ppermute(terms, "core", cross)

    both = (MIXED, GRAD)

    def sent(steps, parts, target, arrived=()):
        nonlocal terms
        block = backward(steps, parts, (place, terms, other_terms, weight), arrived)
        block, terms = lax.optimization_barrier((block, terms))
        return lax.ppermute(block, "x", [(n, (n + target) % 4) for n in range(4)])

    relayed = sent(2, (GRAD,), 3)
    direct = sent(2, (MIXED,), 2)
    right = sent(1, both, 1)
    left = sent(3, both, 3, [((GRAD,), relayed)])
    arrived = [((MIXED,), direct), (both, right), (both, left)]
    sums = backward(0, both, (place, terms, other_terms, weight), arrived, last=True)
    return finish(swapped(sums, ("h", "ylo")))


def solution(mesh):
    fine = Mesh(mesh.devices.reshape(SIZES), AXES)
    ctx, tp = AXES[:3], AXES[3:]
    return jax.shard_map(
        local,
        mesh=fine,
        in_specs=(P(ctx, tp), P(None, ctx, tp), P(tp, ctx), P(tp, None), P(ctx, tp)),
        out_specs=(P(ctx, tp), P(ctx, tp)),
        check_vma=False,
    )
```

```python
import jax
import jax.numpy as jnp
from jax import lax
from jax.experimental import pallas as pl
from jax.experimental.pallas import tpu as pltpu
from jax.sharding import Mesh, PartitionSpec as P

AXES = ("h", "l", "z", "ylo", "x", "core")
SIZES = (2, 2, 8, 2, 4, 2)
ROWS = 128
HALF = 128
TAPS = 128
GROUP = 16
GROUPS = HALF // GROUP
FEATURES = 256
STREAMS = 4 * HALF
BACK = 3 * HALF
BF16 = jnp.bfloat16
F32 = jnp.float32
VMEM_FORWARD = 40 << 20


def bands_kernel(base_ref, band_ref):
    for row in range(2 * GROUPS):
        spread = jnp.broadcast_to(base_ref[row : row + 1, :], (2 * ROWS, 2 * ROWS))
        rolled = pltpu.roll(spread, 0, 1, stride=1, stride_axis=0)
        band_ref[:, row * ROWS : (row + 1) * ROWS] = rolled[:, :ROWS].astype(BF16)


def bands(filters):
    zeros = jnp.zeros((GROUPS, TAPS), filters.dtype)
    causal = jnp.concatenate([zeros, filters], 1)
    anticausal = jnp.concatenate([filters[:, :1], zeros, filters[:, :0:-1]], 1)
    return pl.pallas_call(
        bands_kernel,
        out_shape=jax.ShapeDtypeStruct((2 * ROWS, 2 * GROUPS * ROWS), BF16),
    )(jnp.concatenate([causal, anticausal], 0))


def forward_kernel(
    place_ref,
    own_ref,
    other_ref,
    weight_hbm,
    streams_ref,
    gate_ref,
    product_ref,
    mixed_ref,
    back_ref,
    weight_ref,
    arrived,
):
    core = place_ref[0]
    copies = [
        pltpu.make_async_copy(
            weight_hbm.at[pl.ds((x % 2) * 4, 4), core, :, x // 2], weight_ref.at[x], arrived.at[x]
        )
        for x in range(4)
    ]
    copies += [
        pltpu.make_async_copy(weight_hbm.at[pl.ds(x * 4 + 2 * core, 2)], back_ref.at[x], arrived.at[4 + x])
        for x in range(2)
    ]
    for copy in copies:
        copy.start()
    streams, grad_gate = 0.0, 0.0
    contract = (((1,), (1,)), ((), ()))
    for x in range(4):
        tokens, cotangent, weight = [], [], []
        copies[x].wait()
        for values_ref, which in ((own_ref, core), (other_ref, 1 - core)):
            for y in range(2):
                tokens.append(values_ref[x, :, y, 0].reshape(2 * ROWS, FEATURES))
                cotangent.append(values_ref[x, :, y, 1].reshape(2 * ROWS, FEATURES))
                weight += [weight_ref[x, 2 * which + z, y] for z in range(2)]
        tokens, cotangent = jnp.concatenate(tokens, 1), jnp.concatenate(cotangent, 1)
        weight = jnp.concatenate(weight, 1)
        streams += lax.dot_general(weight[:BACK], tokens, contract, preferred_element_type=F32)
        grad_gate += lax.dot_general(weight[BACK:], cotangent, contract, preferred_element_type=F32)
    streams = streams.astype(BF16)
    streams_ref[...] = streams
    gate_ref[...] = grad_gate
    query, key, value = (streams[i * HALF : (i + 1) * HALF].astype(F32) for i in range(3))
    product_ref[...] = (key * value).astype(BF16)
    mixed_ref[...] = (grad_gate * query).astype(BF16)
    copies[4].wait()
    copies[5].wait()


def forward(place, own, other, weight):
    vmem = pl.BlockSpec(memory_space=pltpu.VMEM)
    shape = lambda height, kind: jax.ShapeDtypeStruct((height, 2 * ROWS), kind)
    return pl.pallas_call(
        forward_kernel,
        out_shape=(
            shape(BACK, BF16),
            shape(HALF, F32),
            shape(HALF, BF16),
            shape(HALF, BF16),
            jax.ShapeDtypeStruct((2, 2, 2, 2, 2, STREAMS, ROWS), BF16),
        ),
        in_specs=[
            pl.BlockSpec(memory_space=pltpu.SMEM),
            vmem,
            vmem,
            pl.BlockSpec(memory_space=pl.ANY),
        ],
        out_specs=(vmem,) * 5,
        scratch_shapes=[pltpu.VMEM((4, 4, 2, STREAMS, ROWS), BF16), pltpu.SemaphoreType.DMA((6,))],
        compiler_params=pltpu.CompilerParams(vmem_limit_bytes=VMEM_FORWARD),
        cost_estimate=pl.CostEstimate(flops=1 << 30, bytes_accessed=9 << 20, transcendentals=0),
    )(place, own, other, weight)


def filtered(left, right, band):
    segments = [
        jnp.concatenate([left[s], right[s]], 1) for s in range(2)
    ]
    result = jnp.dot(jnp.concatenate(segments, 0), band, preferred_element_type=F32)
    return [
        jnp.concatenate(
            [
                result[s * HALF + g * GROUP : s * HALF + (g + 1) * GROUP, g * ROWS : (g + 1) * ROWS]
                for g in range(GROUPS)
            ],
            0,
        )
        for s in range(2)
    ]


def middle_kernel(
    place_ref, band_ref, streams_ref, gate_ref, product_ref, mixed_ref, before_ref, after_ref, terms_ref
):
    first = place_ref[1] == 0
    last = place_ref[1] == 15
    lanes = [slice(s * ROWS, (s + 1) * ROWS) for s in range(2)]
    product, mixed, before, after = (
        [ref[:, lanes[s]] for s in range(2)] for ref in (product_ref, mixed_ref, before_ref, after_ref)
    )
    zero = jnp.zeros_like(before[0])
    earlier = [jnp.where(first, zero, before[0]), jnp.where(first, before[0], before[1])]
    later = [jnp.where(last, after[1], after[0]), jnp.where(last, zero, after[1])]
    conv = filtered(earlier, product, band_ref[:, : GROUPS * ROWS])
    back = filtered(mixed, later, band_ref[:, GROUPS * ROWS :])
    for s in range(2):
        query, key, value = (
            streams_ref[i * HALF : (i + 1) * HALF, lanes[s]].astype(F32) for i in range(3)
        )
        terms = (gate_ref[:, lanes[s]] * conv[s], back[s] * value, back[s] * key, query * conv[s])
        for i in range(4):
            terms_ref[lanes[s], i * HALF : (i + 1) * HALF] = terms[i].T.astype(BF16)


def on_chip(kernel, out_shape, operands, flops):
    smem, vmem = pl.BlockSpec(memory_space=pltpu.SMEM), pl.BlockSpec(memory_space=pltpu.VMEM)
    return pl.pallas_call(
        kernel,
        out_shape=out_shape,
        in_specs=[smem] + [vmem] * (len(operands) - 1),
        out_specs=jax.tree.map(lambda _: vmem, out_shape),
        compiler_params=pltpu.CompilerParams(vmem_limit_bytes=24 << 20),
        cost_estimate=pl.CostEstimate(flops=flops, bytes_accessed=1 << 20, transcendentals=0),
    )(*operands)


def middle(*operands):
    return on_chip(middle_kernel, jax.ShapeDtypeStruct((2 * ROWS, STREAMS), BF16), operands, 1 << 28)


def backward_kernel(place_ref, own_ref, other_ref, weight_ref, out_ref):
    core = place_ref[0]
    for part, cols in enumerate((slice(BACK, STREAMS), slice(0, BACK))):
        terms = jnp.concatenate([own_ref[:, cols], other_ref[:, cols]], 1)
        for y in range(2):
            for x in range(4):
                weight = [
                    jnp.concatenate([weight_ref[x % 2, z, which, y, x // 2, cols] for z in range(2)], 1)
                    for which in (core, 1 - core)
                ]
                result = jnp.dot(terms, jnp.concatenate(weight, 0), preferred_element_type=F32)
                for h in range(2):
                    out_ref[4 * y + x, h, part] = result[h * ROWS : (h + 1) * ROWS].astype(BF16)


def backward(*operands):
    shape = (8, 2, 2, ROWS, FEATURES)
    return on_chip(backward_kernel, jax.ShapeDtypeStruct(shape, BF16), operands, 1 << 30)


def combine_kernel(place_ref, parts_ref, mine_ref, theirs_ref):
    half = place_ref[3]
    for part in range(2):
        mine, theirs = 0.0, 0.0
        for source in range(8):
            mine += parts_ref[source, half, part].astype(F32)
            theirs += parts_ref[source, 1 - half, part].astype(F32)
        mine_ref[part] = mine
        theirs_ref[part] = theirs.astype(BF16)


def combine(*operands):
    shape = (2, ROWS, FEATURES)
    out_shape = (jax.ShapeDtypeStruct(shape, F32), jax.ShapeDtypeStruct(shape, BF16))
    return on_chip(combine_kernel, out_shape, operands, 1 << 20)


def pack_kernel(in_ref, out_ref, packed_ref):
    for h in range(2):
        chans = slice(h * HALF, (h + 1) * HALF)
        streams = [in_ref[stream, :, chans].astype(F32).T.astype(BF16) for stream in range(3)]
        for l in range(2):
            for stream in range(3):
                packed_ref[2 * h + l, stream * HALF : (stream + 1) * HALF] = streams[stream]
            packed_ref[2 * h + l, BACK:] = out_ref[chans]


def packed(in_weight, out_weight):
    vmem = pl.BlockSpec(memory_space=pltpu.VMEM)
    return pl.pallas_call(
        pack_kernel,
        out_shape=jax.ShapeDtypeStruct((4, STREAMS, ROWS), BF16),
        in_specs=[vmem] * 2,
        out_specs=vmem,
    )(in_weight, out_weight)


def finish_kernel(mine_ref, theirs_ref, mixed_ref, grad_ref):
    for part, ref in enumerate((mixed_ref, grad_ref)):
        ref[...] = (mine_ref[part] + theirs_ref[part].astype(F32)).astype(BF16)


def finish(*parts):
    vmem = pl.BlockSpec(memory_space=pltpu.VMEM)
    return pl.pallas_call(
        finish_kernel,
        out_shape=(jax.ShapeDtypeStruct((ROWS, FEATURES), BF16),) * 2,
        in_specs=[vmem] * 2,
        out_specs=(vmem, vmem),
    )(*parts)


def swapped(value, axes):
    return lax.all_to_all(value, axes, 0, 0, tiled=True)


def gathered(value, axes, count):
    return swapped(jnp.broadcast_to(value[None], (count,) + value.shape), axes)


def local(tokens, in_weight, out_weight, mr_filter, cotangent):
    half, core = lax.axis_index("h"), lax.axis_index("core")
    position = lax.axis_index(("l", "z"))
    place = jnp.stack([core, position, lax.axis_index("x"), half]).astype(jnp.int32)

    weight = swapped(packed(in_weight, out_weight), ("h", "l"))
    values = jnp.stack([tokens, cotangent], 0)
    weight, values = lax.optimization_barrier((weight, values))
    weight = lax.all_gather(weight, ("z", "core"), axis=0).reshape(8, 2, 2, 2, STREAMS, ROWS)

    band = bands(lax.dynamic_slice_in_dim(mr_filter, half * GROUPS, GROUPS, 0))
    values = gathered(values, ("h", "ylo"), 4)
    values = gathered(values, "x", 4).reshape(4, 2, 2, 2, ROWS, FEATURES)
    values, band = lax.optimization_barrier((values, band))
    cross = [(0, 1), (1, 0)]
    other = lax.ppermute(values, "core", cross)

    streams, gate, product, mixed, weight = forward(place, values, other, weight)
    ring = [(n, (n + 1) % 16) for n in range(16)]
    before = lax.ppermute(product, ("l", "z"), ring)
    after = lax.ppermute(mixed, ("l", "z"), [(b, a) for a, b in ring])

    terms = middle(place, band, streams, gate, product, mixed, before, after)
    other_terms = lax.ppermute(terms, "core", cross)

    parts = swapped(backward(place, terms, other_terms, weight), ("ylo", "x"))
    mine, theirs = combine(place, parts)
    return finish(mine, lax.ppermute(theirs, "h", cross))


def solution(mesh):
    fine = Mesh(mesh.devices.reshape(SIZES), AXES)
    ctx, tp = AXES[:3], AXES[3:]
    return jax.shard_map(
        local,
        mesh=fine,
        in_specs=(P(ctx, tp), P(None, ctx, tp), P(tp, ctx), P(tp, None), P(ctx, tp)),
        out_specs=(P(ctx, tp), P(ctx, tp)),
        check_vma=False,
    )
```

```python
import jax
import jax.numpy as jnp
from jax import lax
from jax.experimental import pallas as pl
from jax.experimental.pallas import tpu as pltpu
from jax.sharding import Mesh, PartitionSpec as P

AXES = ("h", "l", "z", "ylo", "x", "core")
SIZES = (2, 2, 8, 2, 4, 2)
ROWS = 128
HALF = 128
TAPS = 128
GROUP = 16
GROUPS = HALF // GROUP
FEATURES = 256
STREAMS = 4 * HALF
BACK = 3 * HALF
BF16 = jnp.bfloat16
F32 = jnp.float32
VMEM_FORWARD = 40 << 20


def bands_kernel(base_ref, band_ref):
    for row in range(2 * GROUPS):
        spread = jnp.broadcast_to(base_ref[row : row + 1, :], (2 * ROWS, 2 * ROWS))
        rolled = pltpu.roll(spread, 0, 1, stride=1, stride_axis=0)
        band_ref[:, row * ROWS : (row + 1) * ROWS] = rolled[:, :ROWS].astype(BF16)


def bands(filters):
    zeros = jnp.zeros((GROUPS, TAPS), filters.dtype)
    causal = jnp.concatenate([zeros, filters], 1)
    anticausal = jnp.concatenate([filters[:, :1], zeros, filters[:, :0:-1]], 1)
    return pl.pallas_call(
        bands_kernel,
        out_shape=jax.ShapeDtypeStruct((2 * ROWS, 2 * GROUPS * ROWS), BF16),
    )(jnp.concatenate([causal, anticausal], 0))


def forward_kernel(
    place_ref,
    own_ref,
    other_ref,
    weight_hbm,
    streams_ref,
    gate_ref,
    product_ref,
    mixed_ref,
    back_ref,
    weight_ref,
    arrived,
):
    core = place_ref[0]
    copies = [
        pltpu.make_async_copy(
            weight_hbm.at[pl.ds((x % 2) * 4, 4), core, :, x // 2], weight_ref.at[x], arrived.at[x]
        )
        for x in range(4)
    ]
    copies += [
        pltpu.make_async_copy(weight_hbm.at[pl.ds(x * 4 + 2 * core, 2)], back_ref.at[x], arrived.at[4 + x])
        for x in range(2)
    ]
    for copy in copies[:4]:
        copy.start()
    streams, grad_gate = 0.0, 0.0
    contract = (((1,), (1,)), ((), ()))
    for x in range(4):
        tokens, cotangent, weight = [], [], []
        copies[x].wait()
        if x < 2:
            copies[4 + x].start()
        for values_ref, which in ((own_ref, core), (other_ref, 1 - core)):
            for y in range(2):
                tokens.append(values_ref[x, :, y, 0].reshape(2 * ROWS, FEATURES))
                cotangent.append(values_ref[x, :, y, 1].reshape(2 * ROWS, FEATURES))
                weight += [weight_ref[x, 2 * which + z, y] for z in range(2)]
        tokens, cotangent = jnp.concatenate(tokens, 1), jnp.concatenate(cotangent, 1)
        weight = jnp.concatenate(weight, 1)
        streams += lax.dot_general(weight[:BACK], tokens, contract, preferred_element_type=F32)
        grad_gate += lax.dot_general(weight[BACK:], cotangent, contract, preferred_element_type=F32)
    streams = streams.astype(BF16)
    streams_ref[...] = streams
    gate_ref[...] = grad_gate
    query, key, value = (streams[i * HALF : (i + 1) * HALF].astype(F32) for i in range(3))
    product_ref[...] = (key * value).astype(BF16)
    mixed_ref[...] = (grad_gate * query).astype(BF16)
    copies[4].wait()
    copies[5].wait()


def forward(place, own, other, weight):
    vmem = pl.BlockSpec(memory_space=pltpu.VMEM)
    shape = lambda height, kind: jax.ShapeDtypeStruct((height, 2 * ROWS), kind)
    return pl.pallas_call(
        forward_kernel,
        out_shape=(
            shape(BACK, BF16),
            shape(HALF, F32),
            shape(HALF, BF16),
            shape(HALF, BF16),
            jax.ShapeDtypeStruct((2, 2, 2, 2, 2, STREAMS, ROWS), BF16),
        ),
        in_specs=[
            pl.BlockSpec(memory_space=pltpu.SMEM),
            vmem,
            vmem,
            pl.BlockSpec(memory_space=pl.ANY),
        ],
        out_specs=(vmem,) * 5,
        scratch_shapes=[pltpu.VMEM((4, 4, 2, STREAMS, ROWS), BF16), pltpu.SemaphoreType.DMA((6,))],
        compiler_params=pltpu.CompilerParams(vmem_limit_bytes=VMEM_FORWARD),
        cost_estimate=pl.CostEstimate(flops=1 << 30, bytes_accessed=9 << 20, transcendentals=0),
    )(place, own, other, weight)


def filtered(left, right, band):
    segments = [
        jnp.concatenate([left[s], right[s]], 1) for s in range(2)
    ]
    result = jnp.dot(jnp.concatenate(segments, 0), band, preferred_element_type=F32)
    return [
        jnp.concatenate(
            [
                result[s * HALF + g * GROUP : s * HALF + (g + 1) * GROUP, g * ROWS : (g + 1) * ROWS]
                for g in range(GROUPS)
            ],
            0,
        )
        for s in range(2)
    ]


def middle_kernel(
    place_ref, band_ref, streams_ref, gate_ref, product_ref, mixed_ref, before_ref, after_ref, terms_ref
):
    first = place_ref[1] == 0
    last = place_ref[1] == 15
    lanes = [slice(s * ROWS, (s + 1) * ROWS) for s in range(2)]
    product, mixed, before, after = (
        [ref[:, lanes[s]] for s in range(2)] for ref in (product_ref, mixed_ref, before_ref, after_ref)
    )
    zero = jnp.zeros_like(before[0])
    earlier = [jnp.where(first, zero, before[0]), jnp.where(first, before[0], before[1])]
    later = [jnp.where(last, after[1], after[0]), jnp.where(last, zero, after[1])]
    conv = filtered(earlier, product, band_ref[:, : GROUPS * ROWS])
    back = filtered(mixed, later, band_ref[:, GROUPS * ROWS :])
    for s in range(2):
        query, key, value = (
            streams_ref[i * HALF : (i + 1) * HALF, lanes[s]].astype(F32) for i in range(3)
        )
        terms = (gate_ref[:, lanes[s]] * conv[s], back[s] * value, back[s] * key, query * conv[s])
        for i in range(4):
            terms_ref[lanes[s], i * HALF : (i + 1) * HALF] = terms[i].T.astype(BF16)


def on_chip(kernel, out_shape, operands, flops):
    smem, vmem = pl.BlockSpec(memory_space=pltpu.SMEM), pl.BlockSpec(memory_space=pltpu.VMEM)
    return pl.pallas_call(
        kernel,
        out_shape=out_shape,
        in_specs=[smem] + [vmem] * (len(operands) - 1),
        out_specs=jax.tree.map(lambda _: vmem, out_shape),
        compiler_params=pltpu.CompilerParams(vmem_limit_bytes=24 << 20),
        cost_estimate=pl.CostEstimate(flops=flops, bytes_accessed=1 << 20, transcendentals=0),
    )(*operands)


def middle(*operands):
    return on_chip(middle_kernel, jax.ShapeDtypeStruct((2 * ROWS, STREAMS), BF16), operands, 1 << 28)


def backward(turn, place, *operands):
    def kernel(place_ref, own_ref, other_ref, weight_ref, out_ref):
        core = place_ref[0]
        block = place_ref[3] if turn == 0 else 1 - place_ref[3]
        rows = pl.ds(pl.multiple_of(block * ROWS, ROWS), ROWS)
        for part, cols in enumerate((slice(BACK, STREAMS), slice(0, BACK))):
            terms = jnp.concatenate([own_ref[rows, cols], other_ref[rows, cols]], 1)
            for y in range(2):
                for x in range(4):
                    weight = [
                        jnp.concatenate([weight_ref[x % 2, z, which, y, x // 2, cols] for z in range(2)], 1)
                        for which in (core, 1 - core)
                    ]
                    result = jnp.dot(terms, jnp.concatenate(weight, 0), preferred_element_type=F32)
                    out_ref[4 * y + x, part] = result.astype(BF16)

    shape = (8, 2, ROWS, FEATURES)
    return on_chip(kernel, jax.ShapeDtypeStruct(shape, BF16), (place,) + operands, 1 << 29)


def summed(parts_ref, part):
    total = parts_ref[0, part].astype(F32)
    for source in range(1, 8):
        total += parts_ref[source, part].astype(F32)
    return total


def combine_kernel(parts_ref, total_ref):
    for part in range(2):
        total_ref[part] = summed(parts_ref, part).astype(BF16)


def combine(parts):
    vmem = pl.BlockSpec(memory_space=pltpu.VMEM)
    return pl.pallas_call(
        combine_kernel,
        out_shape=jax.ShapeDtypeStruct((2, ROWS, FEATURES), BF16),
        in_specs=[vmem],
        out_specs=vmem,
    )(parts)


def pack_kernel(in_ref, out_ref, packed_ref):
    for h in range(2):
        chans = slice(h * HALF, (h + 1) * HALF)
        streams = [in_ref[stream, :, chans].astype(F32).T.astype(BF16) for stream in range(3)]
        for l in range(2):
            for stream in range(3):
                packed_ref[2 * h + l, stream * HALF : (stream + 1) * HALF] = streams[stream]
            packed_ref[2 * h + l, BACK:] = out_ref[chans]


def packed(in_weight, out_weight):
    vmem = pl.BlockSpec(memory_space=pltpu.VMEM)
    return pl.pallas_call(
        pack_kernel,
        out_shape=jax.ShapeDtypeStruct((4, STREAMS, ROWS), BF16),
        in_specs=[vmem] * 2,
        out_specs=vmem,
    )(in_weight, out_weight)


def finish_kernel(parts_ref, received_ref, mixed_ref, grad_ref):
    for part, ref in enumerate((mixed_ref, grad_ref)):
        ref[...] = (summed(parts_ref, part) + received_ref[part].astype(F32)).astype(BF16)


def finish(*parts):
    vmem = pl.BlockSpec(memory_space=pltpu.VMEM)
    return pl.pallas_call(
        finish_kernel,
        out_shape=(jax.ShapeDtypeStruct((ROWS, FEATURES), BF16),) * 2,
        in_specs=[vmem] * 2,
        out_specs=(vmem, vmem),
    )(*parts)


def swapped(value, axes):
    return lax.all_to_all(value, axes, 0, 0, tiled=True)


def gathered(value, axes, count):
    return swapped(jnp.broadcast_to(value[None], (count,) + value.shape), axes)


def local(tokens, in_weight, out_weight, mr_filter, cotangent):
    half, core = lax.axis_index("h"), lax.axis_index("core")
    position = lax.axis_index(("l", "z"))
    place = jnp.stack([core, position, lax.axis_index("x"), half]).astype(jnp.int32)

    weight = swapped(packed(in_weight, out_weight), ("h", "l"))
    values = jnp.stack([tokens, cotangent], 0)
    weight, values = lax.optimization_barrier((weight, values))
    weight = lax.all_gather(weight, ("z", "core"), axis=0).reshape(8, 2, 2, 2, STREAMS, ROWS)

    band = bands(lax.dynamic_slice_in_dim(mr_filter, half * GROUPS, GROUPS, 0))
    values = gathered(values, ("h", "ylo"), 4)
    values = gathered(values, "x", 4).reshape(4, 2, 2, 2, ROWS, FEATURES)
    values, band = lax.optimization_barrier((values, band))
    cross = [(0, 1), (1, 0)]
    other = lax.ppermute(values, "core", cross)

    streams, gate, product, mixed, weight = forward(place, values, other, weight)
    ring = [(n, (n + 1) % 16) for n in range(16)]
    before = lax.ppermute(product, ("l", "z"), ring)
    after = lax.ppermute(mixed, ("l", "z"), [(b, a) for a, b in ring])

    terms = middle(place, band, streams, gate, product, mixed, before, after)
    other_terms = lax.ppermute(terms, "core", cross)

    theirs = backward(1, place, terms, other_terms, weight)
    theirs, terms = lax.optimization_barrier((theirs, terms))
    mine = backward(0, place, terms, other_terms, weight)
    theirs = swapped(theirs, ("ylo", "x"))
    theirs, mine = lax.optimization_barrier((theirs, mine))
    mine = swapped(mine, ("ylo", "x"))
    return finish(mine, lax.ppermute(combine(theirs), "h", cross))


def solution(mesh):
    fine = Mesh(mesh.devices.reshape(SIZES), AXES)
    ctx, tp = AXES[:3], AXES[3:]
    return jax.shard_map(
        local,
        mesh=fine,
        in_specs=(P(ctx, tp), P(None, ctx, tp), P(tp, ctx), P(tp, None), P(ctx, tp)),
        out_specs=(P(ctx, tp), P(ctx, tp)),
        check_vma=False,
    )
```

```python
import jax
import jax.numpy as jnp
from jax import lax
from jax.experimental import pallas as pl
from jax.experimental.pallas import tpu as pltpu
from jax.sharding import Mesh, PartitionSpec as P

AXES = ("h", "l", "z", "ylo", "x", "core")
SIZES = (2, 2, 8, 2, 4, 2)
ROWS = 128
HALF = 128
TAPS = 128
GROUP = 16
GROUPS = HALF // GROUP
FEATURES = 256
STREAMS = 4 * HALF
BACK = 3 * HALF
BF16 = jnp.bfloat16
F32 = jnp.float32
VMEM_FORWARD = 40 << 20
VMEM_SMALL = 16 << 20


def bands_kernel(base_ref, band_ref):
    for row in range(2 * GROUPS):
        spread = jnp.broadcast_to(base_ref[row : row + 1, :], (2 * ROWS, 2 * ROWS))
        rolled = pltpu.roll(spread, 0, 1, stride=1, stride_axis=0)
        band_ref[:, row * ROWS : (row + 1) * ROWS] = rolled[:, :ROWS].astype(BF16)


def bands(filters):
    zeros = jnp.zeros((GROUPS, TAPS), filters.dtype)
    causal = jnp.concatenate([zeros, filters], 1)
    anticausal = jnp.concatenate([filters[:, :1], zeros, filters[:, :0:-1]], 1)
    return pl.pallas_call(
        bands_kernel,
        out_shape=jax.ShapeDtypeStruct((2 * ROWS, 2 * GROUPS * ROWS), BF16),
        in_specs=[pl.BlockSpec(memory_space=pltpu.VMEM)],
        out_specs=pl.BlockSpec(memory_space=pltpu.VMEM),
        compiler_params=pltpu.CompilerParams(vmem_limit_bytes=VMEM_SMALL),
    )(jnp.concatenate([causal, anticausal], 0))


def forward_kernel(
    place_ref,
    own_ref,
    other_ref,
    weight_hbm,
    streams_ref,
    gate_ref,
    product_ref,
    mixed_ref,
    back_ref,
    weight_ref,
    arrived,
):
    core = place_ref[0]
    steps_to = lambda y, x: lax.rem(place_ref[4] + 4 - (2 * y + x // 2), 4)
    copies = []
    for x in range(4):
        for y in range(2):
            copies.append(
                pltpu.make_async_copy(
                    weight_hbm.at[pl.ds((x % 2) * 4, 4), core, steps_to(y, x)],
                    weight_ref.at[x, y],
                    arrived.at[2 * x + y],
                )
            )
    for x in range(4):
        for y in range(2):
            copies.append(
                pltpu.make_async_copy(
                    weight_hbm.at[pl.ds((x % 2) * 4 + 2 * core, 2), :, steps_to(y, x)],
                    back_ref.at[x % 2, y, x // 2],
                    arrived.at[8 + 2 * x + y],
                )
            )
    for copy in copies:
        copy.start()
    streams, grad_gate = 0.0, 0.0
    contract = (((1,), (1,)), ((), ()))
    for x in range(4):
        tokens, cotangent, weight = [], [], []
        copies[2 * x].wait()
        copies[2 * x + 1].wait()
        for values_ref, which in ((own_ref, core), (other_ref, 1 - core)):
            for y in range(2):
                tokens.append(values_ref[x, :, y, 0].reshape(2 * ROWS, FEATURES))
                cotangent.append(values_ref[x, :, y, 1].reshape(2 * ROWS, FEATURES))
                weight += [weight_ref[x, y, 2 * which + z] for z in range(2)]
        tokens, cotangent = jnp.concatenate(tokens, 1), jnp.concatenate(cotangent, 1)
        weight = jnp.concatenate(weight, 1)
        streams += lax.dot_general(weight[:BACK], tokens, contract, preferred_element_type=F32)
        grad_gate += lax.dot_general(weight[BACK:], cotangent, contract, preferred_element_type=F32)
    streams = streams.astype(BF16)
    streams_ref[...] = streams
    gate_ref[...] = grad_gate
    query, key, value = (streams[i * HALF : (i + 1) * HALF].astype(F32) for i in range(3))
    product_ref[...] = (key * value).astype(BF16)
    mixed_ref[...] = (grad_gate * query).astype(BF16)
    for copy in copies[8:]:
        copy.wait()


def forward(place, own, other, weight):
    vmem = pl.BlockSpec(memory_space=pltpu.VMEM)
    shape = lambda height, kind: jax.ShapeDtypeStruct((height, 2 * ROWS), kind)
    return pl.pallas_call(
        forward_kernel,
        out_shape=(
            shape(BACK, BF16),
            shape(HALF, F32),
            shape(HALF, BF16),
            shape(HALF, BF16),
            jax.ShapeDtypeStruct((2, 2, 2, 2, 2, STREAMS, ROWS), BF16),
        ),
        in_specs=[
            pl.BlockSpec(memory_space=pltpu.SMEM),
            vmem,
            vmem,
            pl.BlockSpec(memory_space=pl.ANY),
        ],
        out_specs=(vmem,) * 5,
        scratch_shapes=[pltpu.VMEM((4, 2, 4, STREAMS, ROWS), BF16), pltpu.SemaphoreType.DMA((16,))],
        compiler_params=pltpu.CompilerParams(vmem_limit_bytes=VMEM_FORWARD),
        cost_estimate=pl.CostEstimate(flops=1 << 30, bytes_accessed=9 << 20, transcendentals=0),
    )(place, own, other, weight)


def filtered(left, right, band):
    segments = [
        jnp.concatenate([left[s], right[s]], 1) for s in range(2)
    ]
    result = jnp.dot(jnp.concatenate(segments, 0), band, preferred_element_type=F32)
    return [
        jnp.concatenate(
            [
                result[s * HALF + g * GROUP : s * HALF + (g + 1) * GROUP, g * ROWS : (g + 1) * ROWS]
                for g in range(GROUPS)
            ],
            0,
        )
        for s in range(2)
    ]


def middle_kernel(
    place_ref, band_ref, streams_ref, gate_ref, product_ref, mixed_ref, before_ref, after_ref, terms_ref
):
    first = place_ref[1] == 0
    last = place_ref[1] == 15
    lanes = [slice(s * ROWS, (s + 1) * ROWS) for s in range(2)]
    product, mixed, before, after = (
        [ref[:, lanes[s]] for s in range(2)] for ref in (product_ref, mixed_ref, before_ref, after_ref)
    )
    zero = jnp.zeros_like(before[0])
    earlier = [jnp.where(first, zero, before[0]), jnp.where(first, before[0], before[1])]
    later = [jnp.where(last, after[1], after[0]), jnp.where(last, zero, after[1])]
    conv = filtered(earlier, product, band_ref[:, : GROUPS * ROWS])
    back = filtered(mixed, later, band_ref[:, GROUPS * ROWS :])
    for s in range(2):
        query, key, value = (
            streams_ref[i * HALF : (i + 1) * HALF, lanes[s]].astype(F32) for i in range(3)
        )
        terms = (gate_ref[:, lanes[s]] * conv[s], back[s] * value, back[s] * key, query * conv[s])
        for i in range(4):
            terms_ref[lanes[s], i * HALF : (i + 1) * HALF] = terms[i].T.astype(BF16)


def on_chip(kernel, out_shape, operands, flops):
    smem, vmem = pl.BlockSpec(memory_space=pltpu.SMEM), pl.BlockSpec(memory_space=pltpu.VMEM)
    return pl.pallas_call(
        kernel,
        out_shape=out_shape,
        in_specs=[smem] + [vmem] * (len(operands) - 1),
        out_specs=jax.tree.map(lambda _: vmem, out_shape),
        compiler_params=pltpu.CompilerParams(vmem_limit_bytes=VMEM_SMALL),
        cost_estimate=pl.CostEstimate(flops=flops, bytes_accessed=1 << 20, transcendentals=0),
    )(*operands)


def middle(*operands):
    return on_chip(middle_kernel, jax.ShapeDtypeStruct((2 * ROWS, STREAMS), BF16), operands, 1 << 28)


def backward_kernel(place_ref, own_ref, other_ref, weight_ref, out_ref):
    core = place_ref[0]
    for part, cols in enumerate((slice(BACK, STREAMS), slice(0, BACK))):
        terms = jnp.concatenate([own_ref[:, cols], other_ref[:, cols]], 1)
        for y in range(2):
            for x in range(4):
                weight = [
                    jnp.concatenate([weight_ref[x % 2, y, x // 2, z, which, cols] for z in range(2)], 1)
                    for which in (core, 1 - core)
                ]
                result = jnp.dot(terms, jnp.concatenate(weight, 0), preferred_element_type=F32)
                for h in range(2):
                    out_ref[4 * y + x, h, part] = result[h * ROWS : (h + 1) * ROWS].astype(BF16)


def backward(*operands):
    shape = (8, 2, 2, ROWS, FEATURES)
    return on_chip(backward_kernel, jax.ShapeDtypeStruct(shape, BF16), operands, 1 << 30)


def combine_kernel(place_ref, parts_ref, mine_ref, theirs_ref):
    half = place_ref[3]
    for part in range(2):
        mine, theirs = 0.0, 0.0
        for source in range(8):
            mine += parts_ref[source, half, part].astype(F32)
            theirs += parts_ref[source, 1 - half, part].astype(F32)
        mine_ref[part] = mine
        theirs_ref[part] = theirs.astype(BF16)


def combine(*operands):
    shape = (2, ROWS, FEATURES)
    out_shape = (jax.ShapeDtypeStruct(shape, F32), jax.ShapeDtypeStruct(shape, BF16))
    return on_chip(combine_kernel, out_shape, operands, 1 << 20)


def pack_kernel(place_ref, in_ref, out_ref, *packed_refs):
    for steps, packed_ref in enumerate(packed_refs):
        half = lax.div(lax.rem(place_ref[4] + steps, 4), 2)
        chans = pl.ds(pl.multiple_of(half * HALF, HALF), HALF)
        for stream in range(3):
            turned = in_ref[stream, :, chans].astype(F32).T.astype(BF16)
            packed_ref[stream * HALF : (stream + 1) * HALF] = turned
        packed_ref[BACK:] = out_ref[chans]


def packed(*operands):
    return on_chip(pack_kernel, (jax.ShapeDtypeStruct((STREAMS, ROWS), BF16),) * 4, operands, 1 << 20)


def finish_kernel(place_ref, mine_ref, theirs_ref, mixed_ref, grad_ref):
    for part, ref in enumerate((mixed_ref, grad_ref)):
        ref[...] = (mine_ref[part] + theirs_ref[part].astype(F32)).astype(BF16)


def finish(*operands):
    return on_chip(finish_kernel, (jax.ShapeDtypeStruct((ROWS, FEATURES), BF16),) * 2, operands, 1 << 16)


def swapped(value, axes):
    return lax.all_to_all(value, axes, 0, 0, tiled=True)


def gathered(value, axes, count):
    return swapped(jnp.broadcast_to(value[None], (count,) + value.shape), axes)


def local(tokens, in_weight, out_weight, mr_filter, cotangent):
    half, core = lax.axis_index("h"), lax.axis_index("core")
    position = lax.axis_index(("l", "z"))
    along = lax.axis_index(("h", "l"))
    place = jnp.stack([core, position, lax.axis_index("x"), half, along]).astype(jnp.int32)

    pieces = list(packed(place, in_weight, out_weight))
    for steps in (2, 1, 3):
        pieces[steps] = lax.ppermute(pieces[steps], ("h", "l"), [(n, (n + steps) % 4) for n in range(4)])
    weight = jnp.stack(pieces, 0)
    values = jnp.stack([tokens, cotangent], 0)
    weight, values = lax.optimization_barrier((weight, values))
    weight = lax.all_gather(weight, ("z", "core"), axis=0).reshape(8, 2, 4, STREAMS, ROWS)

    band = bands(lax.dynamic_slice_in_dim(mr_filter, half * GROUPS, GROUPS, 0))
    values = gathered(values, ("h", "ylo"), 4)
    values = gathered(values, "x", 4).reshape(4, 2, 2, 2, ROWS, FEATURES)
    values, band = lax.optimization_barrier((values, band))
    cross = [(0, 1), (1, 0)]
    other = lax.ppermute(values, "core", cross)

    streams, gate, product, mixed, weight = forward(place, values, other, weight)
    ring = [(n, (n + 1) % 16) for n in range(16)]
    before = lax.ppermute(product, ("l", "z"), ring)
    after = lax.ppermute(mixed, ("l", "z"), [(b, a) for a, b in ring])

    terms = middle(place, band, streams, gate, product, mixed, before, after)
    other_terms = lax.ppermute(terms, "core", cross)

    parts = swapped(backward(place, terms, other_terms, weight), ("ylo", "x"))
    mine, theirs = combine(place, parts)
    return finish(place, mine, lax.ppermute(theirs, "h", cross))


def solution(mesh):
    fine = Mesh(mesh.devices.reshape(SIZES), AXES)
    ctx, tp = AXES[:3], AXES[3:]
    return jax.shard_map(
        local,
        mesh=fine,
        in_specs=(P(ctx, tp), P(None, ctx, tp), P(tp, ctx), P(tp, None), P(ctx, tp)),
        out_specs=(P(ctx, tp), P(ctx, tp)),
        check_vma=False,
    )
```

```python
import jax
import jax.numpy as jnp
from jax import lax
from jax.experimental import pallas as pl
from jax.experimental.pallas import tpu as pltpu
from jax.sharding import Mesh, PartitionSpec as P

AXES = ("h", "l", "z", "ylo", "x", "core")
SIZES = (2, 2, 8, 2, 4, 2)
ROWS = 128
HALF = 128
TAPS = 128
GROUP = 16
GROUPS = HALF // GROUP
FEATURES = 256
STREAMS = 4 * HALF
BACK = 3 * HALF
BF16 = jnp.bfloat16
F32 = jnp.float32
VMEM_FORWARD = 40 << 20
VMEM_SMALL = 16 << 20


def bands_kernel(base_ref, band_ref):
    for row in range(2 * GROUPS):
        spread = jnp.broadcast_to(base_ref[row : row + 1, :], (2 * ROWS, 2 * ROWS))
        rolled = pltpu.roll(spread, 0, 1, stride=1, stride_axis=0)
        band_ref[:, row * ROWS : (row + 1) * ROWS] = rolled[:, :ROWS].astype(BF16)


def bands(filters):
    zeros = jnp.zeros((GROUPS, TAPS), filters.dtype)
    causal = jnp.concatenate([zeros, filters], 1)
    anticausal = jnp.concatenate([filters[:, :1], zeros, filters[:, :0:-1]], 1)
    return pl.pallas_call(
        bands_kernel,
        out_shape=jax.ShapeDtypeStruct((2 * ROWS, 2 * GROUPS * ROWS), BF16),
        in_specs=[pl.BlockSpec(memory_space=pltpu.VMEM)],
        out_specs=pl.BlockSpec(memory_space=pltpu.VMEM),
        compiler_params=pltpu.CompilerParams(vmem_limit_bytes=VMEM_SMALL),
    )(jnp.concatenate([causal, anticausal], 0))


def forward_kernel(
    place_ref,
    own_ref,
    other_hbm,
    weight_hbm,
    streams_ref,
    gate_ref,
    product_ref,
    mixed_ref,
    back_ref,
    weight_ref,
    other_ref,
    arrived,
):
    core = place_ref[0]
    copies = []
    others = [pltpu.make_async_copy(other_hbm.at[x], other_ref.at[x], arrived.at[16 + x]) for x in range(4)]
    for x in range(4):
        for y in range(2):
            copies.append(
                pltpu.make_async_copy(
                    weight_hbm.at[pl.ds((x % 2) * 4, 4), core, 2 * y + x // 2],
                    weight_ref.at[x, y],
                    arrived.at[2 * x + y],
                )
            )
    for x in range(4):
        for y in range(2):
            copies.append(
                pltpu.make_async_copy(
                    weight_hbm.at[pl.ds((x % 2) * 4 + 2 * core, 2), :, 2 * y + x // 2],
                    back_ref.at[x % 2, y, x // 2],
                    arrived.at[8 + 2 * x + y],
                )
            )
    for x in range(4):
        others[x].start()
        copies[2 * x].start()
        copies[2 * x + 1].start()
    for copy in copies[8:]:
        copy.start()
    streams, grad_gate = 0.0, 0.0
    contract = (((1,), (1,)), ((), ()))
    for x in range(4):
        tokens, cotangent, weight = [], [], []
        others[x].wait()
        copies[2 * x].wait()
        copies[2 * x + 1].wait()
        for values_ref, which in ((own_ref, core), (other_ref, 1 - core)):
            for y in range(2):
                tokens.append(values_ref[x, :, y, 0].reshape(2 * ROWS, FEATURES))
                cotangent.append(values_ref[x, :, y, 1].reshape(2 * ROWS, FEATURES))
                weight += [weight_ref[x, y, 2 * which + z] for z in range(2)]
        tokens, cotangent = jnp.concatenate(tokens, 1), jnp.concatenate(cotangent, 1)
        weight = jnp.concatenate(weight, 1)
        streams += lax.dot_general(weight[:BACK], tokens, contract, preferred_element_type=F32)
        grad_gate += lax.dot_general(weight[BACK:], cotangent, contract, preferred_element_type=F32)
    streams = streams.astype(BF16)
    streams_ref[...] = streams
    gate_ref[...] = grad_gate
    query, key, value = (streams[i * HALF : (i + 1) * HALF].astype(F32) for i in range(3))
    product_ref[...] = (key * value).astype(BF16)
    mixed_ref[...] = (grad_gate * query).astype(BF16)
    for copy in copies[8:]:
        copy.wait()


def forward(place, own, other, weight):
    vmem = pl.BlockSpec(memory_space=pltpu.VMEM)
    shape = lambda height, kind: jax.ShapeDtypeStruct((height, 2 * ROWS), kind)
    return pl.pallas_call(
        forward_kernel,
        out_shape=(
            shape(BACK, BF16),
            shape(HALF, F32),
            shape(HALF, BF16),
            shape(HALF, BF16),
            jax.ShapeDtypeStruct((2, 2, 2, 2, 2, STREAMS, ROWS), BF16),
        ),
        in_specs=[
            pl.BlockSpec(memory_space=pltpu.SMEM),
            vmem,
            pl.BlockSpec(memory_space=pl.ANY),
            pl.BlockSpec(memory_space=pl.ANY),
        ],
        out_specs=(vmem,) * 5,
        scratch_shapes=[
            pltpu.VMEM((4, 2, 4, STREAMS, ROWS), BF16),
            pltpu.VMEM((4, 2, 2, 2, ROWS, FEATURES), BF16),
            pltpu.SemaphoreType.DMA((20,)),
        ],
        compiler_params=pltpu.CompilerParams(vmem_limit_bytes=VMEM_FORWARD),
        cost_estimate=pl.CostEstimate(flops=1 << 30, bytes_accessed=9 << 20, transcendentals=0),
    )(place, own, other, weight)


def filtered(left, right, band):
    segments = [
        jnp.concatenate([left[s], right[s]], 1) for s in range(2)
    ]
    result = jnp.dot(jnp.concatenate(segments, 0), band, preferred_element_type=F32)
    return [
        jnp.concatenate(
            [
                result[s * HALF + g * GROUP : s * HALF + (g + 1) * GROUP, g * ROWS : (g + 1) * ROWS]
                for g in range(GROUPS)
            ],
            0,
        )
        for s in range(2)
    ]


def middle_kernel(
    place_ref, band_ref, streams_ref, gate_ref, product_ref, mixed_ref, before_ref, after_ref, terms_ref
):
    first = place_ref[1] == 0
    last = place_ref[1] == 15
    lanes = [slice(s * ROWS, (s + 1) * ROWS) for s in range(2)]
    product, mixed, before, after = (
        [ref[:, lanes[s]] for s in range(2)] for ref in (product_ref, mixed_ref, before_ref, after_ref)
    )
    zero = jnp.zeros_like(before[0])
    earlier = [jnp.where(first, zero, before[0]), jnp.where(first, before[0], before[1])]
    later = [jnp.where(last, after[1], after[0]), jnp.where(last, zero, after[1])]
    conv = filtered(earlier, product, band_ref[:, : GROUPS * ROWS])
    back = filtered(mixed, later, band_ref[:, GROUPS * ROWS :])
    for s in range(2):
        query, key, value = (
            streams_ref[i * HALF : (i + 1) * HALF, lanes[s]].astype(F32) for i in range(3)
        )
        terms = (gate_ref[:, lanes[s]] * conv[s], back[s] * value, back[s] * key, query * conv[s])
        for i in range(4):
            terms_ref[lanes[s], i * HALF : (i + 1) * HALF] = terms[i].T.astype(BF16)


def on_chip(kernel, out_shape, operands, flops):
    smem, vmem = pl.BlockSpec(memory_space=pltpu.SMEM), pl.BlockSpec(memory_space=pltpu.VMEM)
    return pl.pallas_call(
        kernel,
        out_shape=out_shape,
        in_specs=[smem] + [vmem] * (len(operands) - 1),
        out_specs=jax.tree.map(lambda _: vmem, out_shape),
        compiler_params=pltpu.CompilerParams(vmem_limit_bytes=VMEM_SMALL),
        cost_estimate=pl.CostEstimate(flops=flops, bytes_accessed=1 << 20, transcendentals=0),
    )(*operands)


def middle(*operands):
    return on_chip(middle_kernel, jax.ShapeDtypeStruct((2 * ROWS, STREAMS), BF16), operands, 1 << 28)


def backward_kernel(place_ref, own_ref, other_ref, weight_ref, out_ref):
    core = place_ref[0]
    for part, cols in enumerate((slice(BACK, STREAMS), slice(0, BACK))):
        terms = jnp.concatenate([own_ref[:, cols], other_ref[:, cols]], 1)
        for y in range(2):
            for x in range(4):
                weight = [
                    jnp.concatenate([weight_ref[x % 2, y, x // 2, z, which, cols] for z in range(2)], 1)
                    for which in (core, 1 - core)
                ]
                result = jnp.dot(terms, jnp.concatenate(weight, 0), preferred_element_type=F32)
                for h in range(2):
                    out_ref[4 * y + x, h, part] = result[h * ROWS : (h + 1) * ROWS].astype(BF16)


def backward(*operands):
    shape = (8, 2, 2, ROWS, FEATURES)
    return on_chip(backward_kernel, jax.ShapeDtypeStruct(shape, BF16), operands, 1 << 30)


def combine_kernel(place_ref, parts_ref, mine_ref, theirs_ref):
    half = place_ref[3]
    for part in range(2):
        mine, theirs = 0.0, 0.0
        for source in range(8):
            mine += parts_ref[source, half, part].astype(F32)
            theirs += parts_ref[source, 1 - half, part].astype(F32)
        mine_ref[part] = mine
        theirs_ref[part] = theirs.astype(BF16)


def combine(*operands):
    shape = (2, ROWS, FEATURES)
    out_shape = (jax.ShapeDtypeStruct(shape, F32), jax.ShapeDtypeStruct(shape, BF16))
    return on_chip(combine_kernel, out_shape, operands, 1 << 20)


def pack_kernel(in_ref, out_ref, packed_ref):
    for h in range(2):
        chans = slice(h * HALF, (h + 1) * HALF)
        streams = [in_ref[stream, :, chans].astype(F32).T.astype(BF16) for stream in range(3)]
        for l in range(2):
            for stream in range(3):
                packed_ref[2 * h + l, stream * HALF : (stream + 1) * HALF] = streams[stream]
            packed_ref[2 * h + l, BACK:] = out_ref[chans]


def packed(in_weight, out_weight):
    vmem = pl.BlockSpec(memory_space=pltpu.VMEM)
    return pl.pallas_call(
        pack_kernel,
        out_shape=jax.ShapeDtypeStruct((4, STREAMS, ROWS), BF16),
        in_specs=[vmem] * 2,
        out_specs=vmem,
    )(in_weight, out_weight)


def finish_kernel(place_ref, mine_ref, theirs_ref, mixed_ref, grad_ref):
    for part, ref in enumerate((mixed_ref, grad_ref)):
        ref[...] = (mine_ref[part] + theirs_ref[part].astype(F32)).astype(BF16)


def finish(*operands):
    return on_chip(finish_kernel, (jax.ShapeDtypeStruct((ROWS, FEATURES), BF16),) * 2, operands, 1 << 16)


def swapped(value, axes):
    return lax.all_to_all(value, axes, 0, 0, tiled=True)


def gathered(value, axes, count):
    return swapped(jnp.broadcast_to(value[None], (count,) + value.shape), axes)


def local(tokens, in_weight, out_weight, mr_filter, cotangent):
    half, core = lax.axis_index("h"), lax.axis_index("core")
    position = lax.axis_index(("l", "z"))
    place = jnp.stack([core, position, lax.axis_index("x"), half]).astype(jnp.int32)

    weight = swapped(packed(in_weight, out_weight), ("h", "l"))
    values = jnp.stack([tokens, cotangent], 0)
    weight, values = lax.optimization_barrier((weight, values))
    weight = lax.all_gather(weight, ("z", "core"), axis=0).reshape(8, 2, 4, STREAMS, ROWS)

    band = bands(lax.dynamic_slice_in_dim(mr_filter, half * GROUPS, GROUPS, 0))
    values = gathered(values, ("h", "ylo"), 4)
    values = gathered(values, "x", 4).reshape(4, 2, 2, 2, ROWS, FEATURES)
    values, band = lax.optimization_barrier((values, band))
    cross = [(0, 1), (1, 0)]
    other = lax.ppermute(values, "core", cross)

    streams, gate, product, mixed, weight = forward(place, values, other, weight)
    ring = [(n, (n + 1) % 16) for n in range(16)]
    before = lax.ppermute(product, ("l", "z"), ring)
    after = lax.ppermute(mixed, ("l", "z"), [(b, a) for a, b in ring])

    terms = middle(place, band, streams, gate, product, mixed, before, after)
    other_terms = lax.ppermute(terms, "core", cross)

    parts = swapped(backward(place, terms, other_terms, weight), ("ylo", "x"))
    mine, theirs = combine(place, parts)
    return finish(place, mine, lax.ppermute(theirs, "h", cross))


def solution(mesh):
    fine = Mesh(mesh.devices.reshape(SIZES), AXES)
    ctx, tp = AXES[:3], AXES[3:]
    return jax.shard_map(
        local,
        mesh=fine,
        in_specs=(P(ctx, tp), P(None, ctx, tp), P(tp, ctx), P(tp, None), P(ctx, tp)),
        out_specs=(P(ctx, tp), P(ctx, tp)),
        check_vma=False,
    )
```

```python
import jax
import jax.numpy as jnp
from jax import lax
from jax.experimental import pallas as pl
from jax.experimental.pallas import tpu as pltpu
from jax.sharding import Mesh, PartitionSpec as P

AXES = ("l", "h", "z", "ylo", "x", "core")
SIZES = (2, 2, 8, 2, 4, 2)
ROWS = 128
HALF = 128
TAPS = 128
GROUP = 16
GROUPS = HALF // GROUP
FEATURES = 256
STREAMS = 4 * HALF
BACK = 3 * HALF
BF16 = jnp.bfloat16
F32 = jnp.float32
VMEM_FORWARD = 40 << 20
VMEM_SMALL = 16 << 20


def bands_kernel(base_ref, band_ref):
    for row in range(2 * GROUPS):
        spread = jnp.broadcast_to(base_ref[row : row + 1, :], (2 * ROWS, 2 * ROWS))
        rolled = pltpu.roll(spread, 0, 1, stride=1, stride_axis=0)
        band_ref[:, row * ROWS : (row + 1) * ROWS] = rolled[:, :ROWS].astype(BF16)


def bands(filters):
    zeros = jnp.zeros((GROUPS, TAPS), filters.dtype)
    causal = jnp.concatenate([zeros, filters], 1)
    anticausal = jnp.concatenate([filters[:, :1], zeros, filters[:, :0:-1]], 1)
    return pl.pallas_call(
        bands_kernel,
        out_shape=jax.ShapeDtypeStruct((2 * ROWS, 2 * GROUPS * ROWS), BF16),
        in_specs=[pl.BlockSpec(memory_space=pltpu.VMEM)],
        out_specs=pl.BlockSpec(memory_space=pltpu.VMEM),
        compiler_params=pltpu.CompilerParams(vmem_limit_bytes=VMEM_SMALL),
    )(jnp.concatenate([causal, anticausal], 0))


def forward_kernel(
    place_ref,
    own_ref,
    other_hbm,
    weight_hbm,
    streams_ref,
    gate_ref,
    product_ref,
    mixed_ref,
    edge_ref,
    back_ref,
    weight_ref,
    other_ref,
    arrived,
):
    core = place_ref[0]
    copies = []
    others = [pltpu.make_async_copy(other_hbm.at[x], other_ref.at[x], arrived.at[16 + x]) for x in range(4)]
    for x in range(4):
        for y in range(2):
            copies.append(
                pltpu.make_async_copy(
                    weight_hbm.at[pl.ds((x % 2) * 4, 4), core, 2 * y + x // 2],
                    weight_ref.at[x, y],
                    arrived.at[2 * x + y],
                )
            )
    for x in range(4):
        for y in range(2):
            copies.append(
                pltpu.make_async_copy(
                    weight_hbm.at[pl.ds((x % 2) * 4 + 2 * core, 2), :, 2 * y + x // 2],
                    back_ref.at[x % 2, y, x // 2],
                    arrived.at[8 + 2 * x + y],
                )
            )
    for x in range(4):
        others[x].start()
        copies[2 * x].start()
        copies[2 * x + 1].start()
    for copy in copies[8:]:
        copy.start()
    streams, grad_gate = 0.0, 0.0
    contract = (((1,), (1,)), ((), ()))
    for x in range(4):
        tokens, cotangent, weight = [], [], []
        others[x].wait()
        copies[2 * x].wait()
        copies[2 * x + 1].wait()
        for values_ref, which in ((own_ref, core), (other_ref, 1 - core)):
            for y in range(2):
                tokens.append(values_ref[x, :, y, 0].reshape(2 * ROWS, FEATURES))
                cotangent.append(values_ref[x, :, y, 1].reshape(2 * ROWS, FEATURES))
                weight += [weight_ref[x, y, 2 * which + z] for z in range(2)]
        tokens, cotangent = jnp.concatenate(tokens, 1), jnp.concatenate(cotangent, 1)
        weight = jnp.concatenate(weight, 1)
        streams += lax.dot_general(weight[:BACK], tokens, contract, preferred_element_type=F32)
        grad_gate += lax.dot_general(weight[BACK:], cotangent, contract, preferred_element_type=F32)
    streams = streams.astype(BF16)
    streams_ref[...] = streams
    gate_ref[...] = grad_gate
    query, key, value = (streams[i * HALF : (i + 1) * HALF].astype(F32) for i in range(3))
    product = (key * value).astype(BF16)
    mixed = (grad_gate * query).astype(BF16)
    product_ref[...] = product
    mixed_ref[...] = mixed
    edge_ref[...] = jnp.where(place_ref[1] == 7, product[:, ROWS:], mixed[:, :ROWS])
    for copy in copies[8:]:
        copy.wait()


def forward(place, own, other, weight):
    vmem = pl.BlockSpec(memory_space=pltpu.VMEM)
    shape = lambda height, kind: jax.ShapeDtypeStruct((height, 2 * ROWS), kind)
    return pl.pallas_call(
        forward_kernel,
        out_shape=(
            shape(BACK, BF16),
            shape(HALF, F32),
            shape(HALF, BF16),
            shape(HALF, BF16),
            jax.ShapeDtypeStruct((HALF, ROWS), BF16),
            jax.ShapeDtypeStruct((2, 2, 2, 2, 2, STREAMS, ROWS), BF16),
        ),
        in_specs=[
            pl.BlockSpec(memory_space=pltpu.SMEM),
            vmem,
            pl.BlockSpec(memory_space=pl.ANY),
            pl.BlockSpec(memory_space=pl.ANY),
        ],
        out_specs=(vmem,) * 6,
        scratch_shapes=[
            pltpu.VMEM((4, 2, 4, STREAMS, ROWS), BF16),
            pltpu.VMEM((4, 2, 2, 2, ROWS, FEATURES), BF16),
            pltpu.SemaphoreType.DMA((20,)),
        ],
        compiler_params=pltpu.CompilerParams(vmem_limit_bytes=VMEM_FORWARD),
        cost_estimate=pl.CostEstimate(flops=1 << 30, bytes_accessed=9 << 20, transcendentals=0),
    )(place, own, other, weight)


def filtered(left, right, band):
    segments = [
        jnp.concatenate([left[s], right[s]], 1) for s in range(2)
    ]
    result = jnp.dot(jnp.concatenate(segments, 0), band, preferred_element_type=F32)
    return [
        jnp.concatenate(
            [
                result[s * HALF + g * GROUP : s * HALF + (g + 1) * GROUP, g * ROWS : (g + 1) * ROWS]
                for g in range(GROUPS)
            ],
            0,
        )
        for s in range(2)
    ]


def middle_kernel(
    place_ref, band_ref, streams_ref, gate_ref, product_ref, mixed_ref, before_ref, after_ref, edge_ref, terms_ref
):
    first = place_ref[1] == 0
    last = place_ref[1] == 7
    lanes = [slice(s * ROWS, (s + 1) * ROWS) for s in range(2)]
    product, mixed, before, after = (
        [ref[:, lanes[s]] for s in range(2)] for ref in (product_ref, mixed_ref, before_ref, after_ref)
    )
    edge = edge_ref[...]
    earlier = [jnp.where(first, edge, before[0]), jnp.where(first, before[0], before[1])]
    later = [jnp.where(last, after[1], after[0]), jnp.where(last, edge, after[1])]
    conv = filtered(earlier, product, band_ref[:, : GROUPS * ROWS])
    back = filtered(mixed, later, band_ref[:, GROUPS * ROWS :])
    for s in range(2):
        query, key, value = (
            streams_ref[i * HALF : (i + 1) * HALF, lanes[s]].astype(F32) for i in range(3)
        )
        terms = (gate_ref[:, lanes[s]] * conv[s], back[s] * value, back[s] * key, query * conv[s])
        for i in range(4):
            terms_ref[lanes[s], i * HALF : (i + 1) * HALF] = terms[i].T.astype(BF16)


def on_chip(kernel, out_shape, operands, flops):
    smem, vmem = pl.BlockSpec(memory_space=pltpu.SMEM), pl.BlockSpec(memory_space=pltpu.VMEM)
    return pl.pallas_call(
        kernel,
        out_shape=out_shape,
        in_specs=[smem] + [vmem] * (len(operands) - 1),
        out_specs=jax.tree.map(lambda _: vmem, out_shape),
        compiler_params=pltpu.CompilerParams(vmem_limit_bytes=VMEM_SMALL),
        cost_estimate=pl.CostEstimate(flops=flops, bytes_accessed=1 << 20, transcendentals=0),
    )(*operands)


def middle(*operands):
    return on_chip(middle_kernel, jax.ShapeDtypeStruct((2 * ROWS, STREAMS), BF16), operands, 1 << 28)


def backward_kernel(place_ref, own_ref, other_ref, weight_ref, out_ref):
    core = place_ref[0]
    for part, cols in enumerate((slice(BACK, STREAMS), slice(0, BACK))):
        terms = jnp.concatenate([own_ref[:, cols], other_ref[:, cols]], 1)
        for y in range(2):
            for x in range(4):
                weight = [
                    jnp.concatenate([weight_ref[x % 2, y, x // 2, z, which, cols] for z in range(2)], 1)
                    for which in (core, 1 - core)
                ]
                result = jnp.dot(terms, jnp.concatenate(weight, 0), preferred_element_type=F32)
                for h in range(2):
                    out_ref[4 * y + x, h, part] = result[h * ROWS : (h + 1) * ROWS].astype(BF16)


def backward(*operands):
    shape = (8, 2, 2, ROWS, FEATURES)
    return on_chip(backward_kernel, jax.ShapeDtypeStruct(shape, BF16), operands, 1 << 30)


def combine_kernel(place_ref, parts_ref, mine_ref, theirs_ref):
    half = place_ref[3]
    for part in range(2):
        mine, theirs = 0.0, 0.0
        for source in range(8):
            mine += parts_ref[source, half, part].astype(F32)
            theirs += parts_ref[source, 1 - half, part].astype(F32)
        mine_ref[part] = mine
        theirs_ref[part] = theirs.astype(BF16)


def combine(*operands):
    shape = (2, ROWS, FEATURES)
    out_shape = (jax.ShapeDtypeStruct(shape, F32), jax.ShapeDtypeStruct(shape, BF16))
    return on_chip(combine_kernel, out_shape, operands, 1 << 20)


def pack_kernel(in_ref, out_ref, packed_ref):
    for h in range(2):
        chans = slice(h * HALF, (h + 1) * HALF)
        streams = [in_ref[stream, :, chans].astype(F32).T.astype(BF16) for stream in range(3)]
        for l in range(2):
            for stream in range(3):
                packed_ref[2 * l + h, stream * HALF : (stream + 1) * HALF] = streams[stream]
            packed_ref[2 * l + h, BACK:] = out_ref[chans]


def packed(in_weight, out_weight):
    vmem = pl.BlockSpec(memory_space=pltpu.VMEM)
    return pl.pallas_call(
        pack_kernel,
        out_shape=jax.ShapeDtypeStruct((4, STREAMS, ROWS), BF16),
        in_specs=[vmem] * 2,
        out_specs=vmem,
    )(in_weight, out_weight)


def finish_kernel(place_ref, mine_ref, theirs_ref, mixed_ref, grad_ref):
    for part, ref in enumerate((mixed_ref, grad_ref)):
        ref[...] = (mine_ref[part] + theirs_ref[part].astype(F32)).astype(BF16)


def finish(*operands):
    return on_chip(finish_kernel, (jax.ShapeDtypeStruct((ROWS, FEATURES), BF16),) * 2, operands, 1 << 16)


def swapped(value, axes):
    return lax.all_to_all(value, axes, 0, 0, tiled=True)


def gathered(value, axes, count):
    return swapped(jnp.broadcast_to(value[None], (count,) + value.shape), axes)


def local(tokens, in_weight, out_weight, mr_filter, cotangent):
    half, core = lax.axis_index("h"), lax.axis_index("core")
    place = jnp.stack([core, lax.axis_index("z"), lax.axis_index("x"), half]).astype(jnp.int32)

    weight = swapped(packed(in_weight, out_weight), ("l", "h"))
    values = jnp.stack([tokens, cotangent], 0)
    weight, values = lax.optimization_barrier((weight, values))
    weight = lax.all_gather(weight, ("z", "core"), axis=0).reshape(8, 2, 4, STREAMS, ROWS)

    band = bands(lax.dynamic_slice_in_dim(mr_filter, half * GROUPS, GROUPS, 0))
    values = gathered(values, ("h", "ylo"), 4)
    values = gathered(values, "x", 4).reshape(4, 2, 2, 2, ROWS, FEATURES)
    values, band = lax.optimization_barrier((values, band))
    cross = [(0, 1), (1, 0)]
    other = lax.ppermute(values, "core", cross)

    streams, gate, product, mixed, edge, weight = forward(place, values, other, weight)
    ring = [(n, (n + 1) % 8) for n in range(8)]
    before = lax.ppermute(product, "z", ring)
    after = lax.ppermute(mixed, "z", [(b, a) for a, b in ring])
    edge = lax.ppermute(edge, ("l", "z"), [(7, 8), (8, 7)])

    terms = middle(place, band, streams, gate, product, mixed, before, after, edge)
    other_terms = lax.ppermute(terms, "core", cross)

    parts = swapped(backward(place, terms, other_terms, weight), ("ylo", "x"))
    mine, theirs = combine(place, parts)
    return finish(place, mine, lax.ppermute(theirs, "h", cross))


def solution(mesh):
    fine = Mesh(mesh.devices.reshape(SIZES), AXES)
    ctx, tp = AXES[:3], AXES[3:]
    return jax.shard_map(
        local,
        mesh=fine,
        in_specs=(P(ctx, tp), P(None, ctx, tp), P(tp, ctx), P(tp, None), P(ctx, tp)),
        out_specs=(P(ctx, tp), P(ctx, tp)),
        check_vma=False,
    )
```

```python
import jax
import jax.numpy as jnp
from jax import lax
from jax.experimental import pallas as pl
from jax.experimental.pallas import tpu as pltpu
from jax.sharding import Mesh, PartitionSpec as P

AXES = ("l", "h", "z", "ylo", "x", "core")
SIZES = (2, 2, 8, 2, 4, 2)
ROWS = 128
HALF = 128
TAPS = 128
GROUP = 16
GROUPS = HALF // GROUP
FEATURES = 256
STREAMS = 4 * HALF
BACK = 3 * HALF
BF16 = jnp.bfloat16
F32 = jnp.float32
VMEM_FORWARD = 40 << 20
VMEM_SMALL = 16 << 20


def bands_kernel(base_ref, band_ref):
    for row in range(2 * GROUPS):
        spread = jnp.broadcast_to(base_ref[row : row + 1, :], (2 * ROWS, 2 * ROWS))
        rolled = pltpu.roll(spread, 0, 1, stride=1, stride_axis=0)
        band_ref[:, row * ROWS : (row + 1) * ROWS] = rolled[:, :ROWS].astype(BF16)


def bands(filters):
    zeros = jnp.zeros((GROUPS, TAPS), filters.dtype)
    causal = jnp.concatenate([zeros, filters], 1)
    anticausal = jnp.concatenate([filters[:, :1], zeros, filters[:, :0:-1]], 1)
    return pl.pallas_call(
        bands_kernel,
        out_shape=jax.ShapeDtypeStruct((2 * ROWS, 2 * GROUPS * ROWS), BF16),
        in_specs=[pl.BlockSpec(memory_space=pltpu.VMEM)],
        out_specs=pl.BlockSpec(memory_space=pltpu.VMEM),
        compiler_params=pltpu.CompilerParams(vmem_limit_bytes=VMEM_SMALL),
    )(jnp.concatenate([causal, anticausal], 0))


def forward_kernel(
    place_ref,
    own_ref,
    other_hbm,
    weight_hbm,
    streams_ref,
    gate_ref,
    product_ref,
    mixed_ref,
    edge_ref,
    back_ref,
    weight_ref,
    other_ref,
    arrived,
):
    core = place_ref[0]
    copies = []
    others = [pltpu.make_async_copy(other_hbm.at[x], other_ref.at[x], arrived.at[16 + x]) for x in range(4)]
    for x in range(4):
        for y in range(2):
            copies.append(
                pltpu.make_async_copy(
                    weight_hbm.at[pl.ds((x % 2) * 4, 4), core, 2 * y + x // 2],
                    weight_ref.at[x, y],
                    arrived.at[2 * x + y],
                )
            )
    for x in range(4):
        for y in range(2):
            copies.append(
                pltpu.make_async_copy(
                    weight_hbm.at[pl.ds((x % 2) * 4 + 2 * core, 2), :, 2 * y + x // 2],
                    back_ref.at[x % 2, y, x // 2],
                    arrived.at[8 + 2 * x + y],
                )
            )
    for x in range(4):
        others[x].start()
        copies[2 * x].start()
        copies[2 * x + 1].start()
    for copy in copies[8:]:
        copy.start()
    streams, grad_gate = 0.0, 0.0
    contract = (((1,), (1,)), ((), ()))
    for x in range(4):
        tokens, cotangent, weight = [], [], []
        others[x].wait()
        copies[2 * x].wait()
        copies[2 * x + 1].wait()
        for values_ref, which in ((own_ref, core), (other_ref, 1 - core)):
            for y in range(2):
                tokens.append(values_ref[x, :, y, 0].reshape(2 * ROWS, FEATURES))
                cotangent.append(values_ref[x, :, y, 1].reshape(2 * ROWS, FEATURES))
                weight += [weight_ref[x, y, 2 * which + z] for z in range(2)]
        tokens, cotangent = jnp.concatenate(tokens, 1), jnp.concatenate(cotangent, 1)
        weight = jnp.concatenate(weight, 1)
        streams += lax.dot_general(weight[:BACK], tokens, contract, preferred_element_type=F32)
        grad_gate += lax.dot_general(weight[BACK:], cotangent, contract, preferred_element_type=F32)
    streams = streams.astype(BF16)
    streams_ref[...] = streams
    gate_ref[...] = grad_gate
    query, key, value = (streams[i * HALF : (i + 1) * HALF].astype(F32) for i in range(3))
    product = (key * value).astype(BF16)
    mixed = (grad_gate * query).astype(BF16)
    product_ref[...] = product
    mixed_ref[...] = mixed
    edge_ref[...] = jnp.where(place_ref[1] == 7, product, mixed)
    for copy in copies[8:]:
        copy.wait()


def forward(place, own, other, weight):
    vmem = pl.BlockSpec(memory_space=pltpu.VMEM)
    shape = lambda height, kind: jax.ShapeDtypeStruct((height, 2 * ROWS), kind)
    return pl.pallas_call(
        forward_kernel,
        out_shape=(
            shape(BACK, BF16),
            shape(HALF, F32),
            shape(HALF, BF16),
            shape(HALF, BF16),
            shape(HALF, BF16),
            jax.ShapeDtypeStruct((2, 2, 2, 2, 2, STREAMS, ROWS), BF16),
        ),
        in_specs=[
            pl.BlockSpec(memory_space=pltpu.SMEM),
            vmem,
            pl.BlockSpec(memory_space=pl.ANY),
            pl.BlockSpec(memory_space=pl.ANY),
        ],
        out_specs=(vmem,) * 6,
        scratch_shapes=[
            pltpu.VMEM((4, 2, 4, STREAMS, ROWS), BF16),
            pltpu.VMEM((4, 2, 2, 2, ROWS, FEATURES), BF16),
            pltpu.SemaphoreType.DMA((20,)),
        ],
        compiler_params=pltpu.CompilerParams(vmem_limit_bytes=VMEM_FORWARD),
        cost_estimate=pl.CostEstimate(flops=1 << 30, bytes_accessed=9 << 20, transcendentals=0),
    )(place, own, other, weight)


def filtered(left, right, band):
    segments = [
        jnp.concatenate([left[s], right[s]], 1) for s in range(2)
    ]
    result = jnp.dot(jnp.concatenate(segments, 0), band, preferred_element_type=F32)
    return [
        jnp.concatenate(
            [
                result[s * HALF + g * GROUP : s * HALF + (g + 1) * GROUP, g * ROWS : (g + 1) * ROWS]
                for g in range(GROUPS)
            ],
            0,
        )
        for s in range(2)
    ]


def middle_kernel(
    place_ref, band_ref, streams_ref, gate_ref, product_ref, mixed_ref, before_ref, after_ref, edge_ref, terms_ref
):
    first = place_ref[1] == 0
    last = place_ref[1] == 7
    lanes = [slice(s * ROWS, (s + 1) * ROWS) for s in range(2)]
    product, mixed, before, after = (
        [ref[:, lanes[s]] for s in range(2)] for ref in (product_ref, mixed_ref, before_ref, after_ref)
    )
    edge = [edge_ref[:, lanes[s]] for s in range(2)]
    earlier = [jnp.where(first, edge[1], before[0]), jnp.where(first, before[0], before[1])]
    later = [jnp.where(last, after[1], after[0]), jnp.where(last, edge[0], after[1])]
    conv = filtered(earlier, product, band_ref[:, : GROUPS * ROWS])
    back = filtered(mixed, later, band_ref[:, GROUPS * ROWS :])
    for s in range(2):
        query, key, value = (
            streams_ref[i * HALF : (i + 1) * HALF, lanes[s]].astype(F32) for i in range(3)
        )
        terms = (gate_ref[:, lanes[s]] * conv[s], back[s] * value, back[s] * key, query * conv[s])
        for i in range(4):
            terms_ref[lanes[s], i * HALF : (i + 1) * HALF] = terms[i].T.astype(BF16)


def on_chip(kernel, out_shape, operands, flops):
    smem, vmem = pl.BlockSpec(memory_space=pltpu.SMEM), pl.BlockSpec(memory_space=pltpu.VMEM)
    return pl.pallas_call(
        kernel,
        out_shape=out_shape,
        in_specs=[smem] + [vmem] * (len(operands) - 1),
        out_specs=jax.tree.map(lambda _: vmem, out_shape),
        compiler_params=pltpu.CompilerParams(vmem_limit_bytes=VMEM_SMALL),
        cost_estimate=pl.CostEstimate(flops=flops, bytes_accessed=1 << 20, transcendentals=0),
    )(*operands)


def middle(*operands):
    return on_chip(middle_kernel, jax.ShapeDtypeStruct((2 * ROWS, STREAMS), BF16), operands, 1 << 28)


def backward_kernel(place_ref, own_ref, other_ref, weight_ref, out_ref):
    core = place_ref[0]
    for part, cols in enumerate((slice(BACK, STREAMS), slice(0, BACK))):
        terms = jnp.concatenate([own_ref[:, cols], other_ref[:, cols]], 1)
        for y in range(2):
            for x in range(4):
                weight = [
                    jnp.concatenate([weight_ref[x % 2, y, x // 2, z, which, cols] for z in range(2)], 1)
                    for which in (core, 1 - core)
                ]
                result = jnp.dot(terms, jnp.concatenate(weight, 0), preferred_element_type=F32)
                for h in range(2):
                    out_ref[4 * y + x, h, part] = result[h * ROWS : (h + 1) * ROWS].astype(BF16)


def backward(*operands):
    shape = (8, 2, 2, ROWS, FEATURES)
    return on_chip(backward_kernel, jax.ShapeDtypeStruct(shape, BF16), operands, 1 << 30)


def combine_kernel(place_ref, parts_ref, mine_ref, theirs_ref):
    half = place_ref[3]
    for part in range(2):
        mine, theirs = 0.0, 0.0
        for source in range(8):
            mine += parts_ref[source, half, part].astype(F32)
            theirs += parts_ref[source, 1 - half, part].astype(F32)
        mine_ref[part] = mine
        theirs_ref[part] = theirs.astype(BF16)


def combine(*operands):
    shape = (2, ROWS, FEATURES)
    out_shape = (jax.ShapeDtypeStruct(shape, F32), jax.ShapeDtypeStruct(shape, BF16))
    return on_chip(combine_kernel, out_shape, operands, 1 << 20)


def pack_kernel(in_ref, out_ref, packed_ref):
    for h in range(2):
        chans = slice(h * HALF, (h + 1) * HALF)
        streams = [in_ref[stream, :, chans].astype(F32).T.astype(BF16) for stream in range(3)]
        for l in range(2):
            for stream in range(3):
                packed_ref[2 * l + h, stream * HALF : (stream + 1) * HALF] = streams[stream]
            packed_ref[2 * l + h, BACK:] = out_ref[chans]


def packed(in_weight, out_weight):
    vmem = pl.BlockSpec(memory_space=pltpu.VMEM)
    return pl.pallas_call(
        pack_kernel,
        out_shape=jax.ShapeDtypeStruct((4, STREAMS, ROWS), BF16),
        in_specs=[vmem] * 2,
        out_specs=vmem,
    )(in_weight, out_weight)


def finish_kernel(place_ref, mine_ref, theirs_ref, mixed_ref, grad_ref):
    for part, ref in enumerate((mixed_ref, grad_ref)):
        ref[...] = (mine_ref[part] + theirs_ref[part].astype(F32)).astype(BF16)


def finish(*operands):
    return on_chip(finish_kernel, (jax.ShapeDtypeStruct((ROWS, FEATURES), BF16),) * 2, operands, 1 << 16)


def swapped(value, axes):
    return lax.all_to_all(value, axes, 0, 0, tiled=True)


def gathered(value, axes, count):
    return swapped(jnp.broadcast_to(value[None], (count,) + value.shape), axes)


def local(tokens, in_weight, out_weight, mr_filter, cotangent):
    half, core = lax.axis_index("h"), lax.axis_index("core")
    place = jnp.stack([core, lax.axis_index("z"), lax.axis_index("x"), half]).astype(jnp.int32)

    weight = swapped(packed(in_weight, out_weight), ("l", "h"))
    values = jnp.stack([tokens, cotangent], 0)
    weight, values = lax.optimization_barrier((weight, values))
    weight = lax.all_gather(weight, ("z", "core"), axis=0).reshape(8, 2, 4, STREAMS, ROWS)

    band = bands(lax.dynamic_slice_in_dim(mr_filter, half * GROUPS, GROUPS, 0))
    values = gathered(values, ("h", "ylo"), 4)
    values = gathered(values, "x", 4).reshape(4, 2, 2, 2, ROWS, FEATURES)
    values, band = lax.optimization_barrier((values, band))
    cross = [(0, 1), (1, 0)]
    other = lax.ppermute(values, "core", cross)

    streams, gate, product, mixed, edge, weight = forward(place, values, other, weight)
    ring = [(n, (n + 1) % 8) for n in range(8)]
    edge = lax.ppermute(edge, ("l", "z"), [(7, 8), (8, 7)])
    before = lax.ppermute(product, "z", ring)
    after = lax.ppermute(mixed, "z", [(b, a) for a, b in ring])

    terms = middle(place, band, streams, gate, product, mixed, before, after, edge)
    other_terms = lax.ppermute(terms, "core", cross)

    parts = swapped(backward(place, terms, other_terms, weight), ("ylo", "x"))
    mine, theirs = combine(place, parts)
    return finish(place, mine, lax.ppermute(theirs, "h", cross))


def solution(mesh):
    fine = Mesh(mesh.devices.reshape(SIZES), AXES)
    ctx, tp = AXES[:3], AXES[3:]
    return jax.shard_map(
        local,
        mesh=fine,
        in_specs=(P(ctx, tp), P(None, ctx, tp), P(tp, ctx), P(tp, None), P(ctx, tp)),
        out_specs=(P(ctx, tp), P(ctx, tp)),
        check_vma=False,
    )
```

```python
import jax
import jax.numpy as jnp
from jax import lax
from jax.experimental import pallas as pl
from jax.experimental.pallas import tpu as pltpu
from jax.sharding import Mesh, PartitionSpec as P

AXES = ("h", "l", "z", "ylo", "x", "core")
SIZES = (2, 2, 8, 2, 4, 2)
ROWS = 128
HALF = 128
TAPS = 128
GROUP = 16
GROUPS = HALF // GROUP
FEATURES = 256
STREAMS = 4 * HALF
BACK = 3 * HALF
BF16 = jnp.bfloat16
F32 = jnp.float32
VMEM_FORWARD = 40 << 20
VMEM_SMALL = 16 << 20


def bands_kernel(base_ref, band_ref):
    for row in range(2 * GROUPS):
        spread = jnp.broadcast_to(base_ref[row : row + 1, :], (2 * ROWS, 2 * ROWS))
        rolled = pltpu.roll(spread, 0, 1, stride=1, stride_axis=0)
        band_ref[:, row * ROWS : (row + 1) * ROWS] = rolled[:, :ROWS].astype(BF16)


def bands(filters):
    zeros = jnp.zeros((GROUPS, TAPS), filters.dtype)
    causal = jnp.concatenate([zeros, filters], 1)
    anticausal = jnp.concatenate([filters[:, :1], zeros, filters[:, :0:-1]], 1)
    return pl.pallas_call(
        bands_kernel,
        out_shape=jax.ShapeDtypeStruct((2 * ROWS, 2 * GROUPS * ROWS), BF16),
        in_specs=[pl.BlockSpec(memory_space=pltpu.VMEM)],
        out_specs=pl.BlockSpec(memory_space=pltpu.VMEM),
        compiler_params=pltpu.CompilerParams(vmem_limit_bytes=VMEM_SMALL),
    )(jnp.concatenate([causal, anticausal], 0))


def forward_kernel(
    place_ref,
    own_ref,
    other_hbm,
    weight_hbm,
    streams_ref,
    gate_ref,
    product_ref,
    mixed_ref,
    edge_ref,
    back_ref,
    weight_ref,
    other_ref,
    arrived,
):
    core = place_ref[0]
    copies = []
    others = [pltpu.make_async_copy(other_hbm.at[x], other_ref.at[x], arrived.at[16 + x]) for x in range(4)]
    for x in range(4):
        for y in range(2):
            copies.append(
                pltpu.make_async_copy(
                    weight_hbm.at[pl.ds((x % 2) * 4, 4), core, 2 * y + x // 2],
                    weight_ref.at[x, y],
                    arrived.at[2 * x + y],
                )
            )
    for x in range(4):
        for y in range(2):
            copies.append(
                pltpu.make_async_copy(
                    weight_hbm.at[pl.ds((x % 2) * 4 + 2 * core, 2), :, 2 * y + x // 2],
                    back_ref.at[x % 2, y, x // 2],
                    arrived.at[8 + 2 * x + y],
                )
            )
    for x in range(4):
        others[x].start()
        copies[2 * x].start()
        copies[2 * x + 1].start()
    for copy in copies[8:]:
        copy.start()
    streams, grad_gate = 0.0, 0.0
    contract = (((1,), (1,)), ((), ()))
    for x in range(4):
        tokens, cotangent, weight = [], [], []
        others[x].wait()
        copies[2 * x].wait()
        copies[2 * x + 1].wait()
        for values_ref, which in ((own_ref, core), (other_ref, 1 - core)):
            for y in range(2):
                tokens.append(values_ref[x, :, y, 0].reshape(2 * ROWS, FEATURES))
                cotangent.append(values_ref[x, :, y, 1].reshape(2 * ROWS, FEATURES))
                weight += [weight_ref[x, y, 2 * which + z] for z in range(2)]
        tokens, cotangent = jnp.concatenate(tokens, 1), jnp.concatenate(cotangent, 1)
        weight = jnp.concatenate(weight, 1)
        streams += lax.dot_general(weight[:BACK], tokens, contract, preferred_element_type=F32)
        grad_gate += lax.dot_general(weight[BACK:], cotangent, contract, preferred_element_type=F32)
    streams = streams.astype(BF16)
    streams_ref[...] = streams
    gate_ref[...] = grad_gate
    query, key, value = (streams[i * HALF : (i + 1) * HALF].astype(F32) for i in range(3))
    product = (key * value).astype(BF16)
    mixed = (grad_gate * query).astype(BF16)
    product_ref[...] = product
    mixed_ref[...] = mixed
    edge_ref[...] = jnp.where(lax.rem(place_ref[1], 8) == 7, product, mixed)
    for copy in copies[8:]:
        copy.wait()


def forward(place, own, other, weight):
    vmem = pl.BlockSpec(memory_space=pltpu.VMEM)
    shape = lambda height, kind: jax.ShapeDtypeStruct((height, 2 * ROWS), kind)
    return pl.pallas_call(
        forward_kernel,
        out_shape=(
            shape(BACK, BF16),
            shape(HALF, F32),
            shape(HALF, BF16),
            shape(HALF, BF16),
            shape(HALF, BF16),
            jax.ShapeDtypeStruct((2, 2, 2, 2, 2, STREAMS, ROWS), BF16),
        ),
        in_specs=[
            pl.BlockSpec(memory_space=pltpu.SMEM),
            vmem,
            pl.BlockSpec(memory_space=pl.ANY),
            pl.BlockSpec(memory_space=pl.ANY),
        ],
        out_specs=(vmem,) * 6,
        scratch_shapes=[
            pltpu.VMEM((4, 2, 4, STREAMS, ROWS), BF16),
            pltpu.VMEM((4, 2, 2, 2, ROWS, FEATURES), BF16),
            pltpu.SemaphoreType.DMA((20,)),
        ],
        compiler_params=pltpu.CompilerParams(vmem_limit_bytes=VMEM_FORWARD),
        cost_estimate=pl.CostEstimate(flops=1 << 30, bytes_accessed=9 << 20, transcendentals=0),
    )(place, own, other, weight)


def filtered(left, right, band):
    segments = [
        jnp.concatenate([left[s], right[s]], 1) for s in range(2)
    ]
    result = jnp.dot(jnp.concatenate(segments, 0), band, preferred_element_type=F32)
    return [
        jnp.concatenate(
            [
                result[s * HALF + g * GROUP : s * HALF + (g + 1) * GROUP, g * ROWS : (g + 1) * ROWS]
                for g in range(GROUPS)
            ],
            0,
        )
        for s in range(2)
    ]


def middle_kernel(
    place_ref, band_ref, streams_ref, gate_ref, product_ref, mixed_ref, before_ref, after_ref, edge_ref, terms_ref
):
    first = place_ref[1] == 0
    last = place_ref[1] == 15
    lanes = [slice(s * ROWS, (s + 1) * ROWS) for s in range(2)]
    product, mixed, before, after, edge = (
        [ref[:, lanes[s]] for s in range(2)]
        for ref in (product_ref, mixed_ref, before_ref, after_ref, edge_ref)
    )
    z = lax.rem(place_ref[1], 8)
    before = [jnp.where(z == 0, edge[s], before[s]) for s in range(2)]
    after = [jnp.where(z == 7, edge[s], after[s]) for s in range(2)]
    zero = jnp.zeros_like(before[0])
    earlier = [jnp.where(first, zero, before[0]), jnp.where(first, before[0], before[1])]
    later = [jnp.where(last, after[1], after[0]), jnp.where(last, zero, after[1])]
    conv = filtered(earlier, product, band_ref[:, : GROUPS * ROWS])
    back = filtered(mixed, later, band_ref[:, GROUPS * ROWS :])
    for s in range(2):
        query, key, value = (
            streams_ref[i * HALF : (i + 1) * HALF, lanes[s]].astype(F32) for i in range(3)
        )
        terms = (gate_ref[:, lanes[s]] * conv[s], back[s] * value, back[s] * key, query * conv[s])
        for i in range(4):
            terms_ref[lanes[s], i * HALF : (i + 1) * HALF] = terms[i].T.astype(BF16)


def on_chip(kernel, out_shape, operands, flops):
    smem, vmem = pl.BlockSpec(memory_space=pltpu.SMEM), pl.BlockSpec(memory_space=pltpu.VMEM)
    return pl.pallas_call(
        kernel,
        out_shape=out_shape,
        in_specs=[smem] + [vmem] * (len(operands) - 1),
        out_specs=jax.tree.map(lambda _: vmem, out_shape),
        compiler_params=pltpu.CompilerParams(vmem_limit_bytes=VMEM_SMALL),
        cost_estimate=pl.CostEstimate(flops=flops, bytes_accessed=1 << 20, transcendentals=0),
    )(*operands)


def middle(*operands):
    return on_chip(middle_kernel, jax.ShapeDtypeStruct((2 * ROWS, STREAMS), BF16), operands, 1 << 28)


def backward_kernel(place_ref, own_ref, other_ref, weight_ref, out_ref):
    core = place_ref[0]
    for part, cols in enumerate((slice(BACK, STREAMS), slice(0, BACK))):
        terms = jnp.concatenate([own_ref[:, cols], other_ref[:, cols]], 1)
        for y in range(2):
            for x in range(4):
                weight = [
                    jnp.concatenate([weight_ref[x % 2, y, x // 2, z, which, cols] for z in range(2)], 1)
                    for which in (core, 1 - core)
                ]
                result = jnp.dot(terms, jnp.concatenate(weight, 0), preferred_element_type=F32)
                for h in range(2):
                    out_ref[4 * y + x, h, part] = result[h * ROWS : (h + 1) * ROWS].astype(BF16)


def backward(*operands):
    shape = (8, 2, 2, ROWS, FEATURES)
    return on_chip(backward_kernel, jax.ShapeDtypeStruct(shape, BF16), operands, 1 << 30)


def combine_kernel(place_ref, parts_ref, mine_ref, theirs_ref):
    half = place_ref[3]
    for part in range(2):
        mine, theirs = 0.0, 0.0
        for source in range(8):
            mine += parts_ref[source, half, part].astype(F32)
            theirs += parts_ref[source, 1 - half, part].astype(F32)
        mine_ref[part] = mine
        theirs_ref[part] = theirs.astype(BF16)


def combine(*operands):
    shape = (2, ROWS, FEATURES)
    out_shape = (jax.ShapeDtypeStruct(shape, F32), jax.ShapeDtypeStruct(shape, BF16))
    return on_chip(combine_kernel, out_shape, operands, 1 << 20)


def pack_kernel(in_ref, out_ref, packed_ref):
    for h in range(2):
        chans = slice(h * HALF, (h + 1) * HALF)
        streams = [in_ref[stream, :, chans].astype(F32).T.astype(BF16) for stream in range(3)]
        for l in range(2):
            for stream in range(3):
                packed_ref[2 * h + l, stream * HALF : (stream + 1) * HALF] = streams[stream]
            packed_ref[2 * h + l, BACK:] = out_ref[chans]


def packed(in_weight, out_weight):
    vmem = pl.BlockSpec(memory_space=pltpu.VMEM)
    return pl.pallas_call(
        pack_kernel,
        out_shape=jax.ShapeDtypeStruct((4, STREAMS, ROWS), BF16),
        in_specs=[vmem] * 2,
        out_specs=vmem,
    )(in_weight, out_weight)


def finish_kernel(place_ref, mine_ref, theirs_ref, mixed_ref, grad_ref):
    for part, ref in enumerate((mixed_ref, grad_ref)):
        ref[...] = (mine_ref[part] + theirs_ref[part].astype(F32)).astype(BF16)


def finish(*operands):
    return on_chip(finish_kernel, (jax.ShapeDtypeStruct((ROWS, FEATURES), BF16),) * 2, operands, 1 << 16)


def swapped(value, axes):
    return lax.all_to_all(value, axes, 0, 0, tiled=True)


def gathered(value, axes, count):
    return swapped(jnp.broadcast_to(value[None], (count,) + value.shape), axes)


def local(tokens, in_weight, out_weight, mr_filter, cotangent):
    half, core = lax.axis_index("h"), lax.axis_index("core")
    position = lax.axis_index(("l", "z"))
    place = jnp.stack([core, position, lax.axis_index("x"), half]).astype(jnp.int32)

    weight = swapped(packed(in_weight, out_weight), ("h", "l"))
    values = jnp.stack([tokens, cotangent], 0)
    weight, values = lax.optimization_barrier((weight, values))
    weight = lax.all_gather(weight, ("z", "core"), axis=0).reshape(8, 2, 4, STREAMS, ROWS)

    band = bands(lax.dynamic_slice_in_dim(mr_filter, half * GROUPS, GROUPS, 0))
    values = gathered(values, ("h", "ylo"), 4)
    values = gathered(values, "x", 4).reshape(4, 2, 2, 2, ROWS, FEATURES)
    values, band = lax.optimization_barrier((values, band))
    cross = [(0, 1), (1, 0)]
    other = lax.ppermute(values, "core", cross)

    streams, gate, product, mixed, edge, weight = forward(place, values, other, weight)
    edge = lax.ppermute(edge, ("l", "z"), [(7, 8), (8, 7), (15, 0), (0, 15)])
    before = lax.ppermute(product, "z", [(n, n + 1) for n in range(7)])
    after = lax.ppermute(mixed, "z", [(n + 1, n) for n in range(7)])

    terms = middle(place, band, streams, gate, product, mixed, before, after, edge)
    other_terms = lax.ppermute(terms, "core", cross)

    parts = swapped(backward(place, terms, other_terms, weight), ("ylo", "x"))
    mine, theirs = combine(place, parts)
    return finish(place, mine, lax.ppermute(theirs, "h", cross))


def solution(mesh):
    fine = Mesh(mesh.devices.reshape(SIZES), AXES)
    ctx, tp = AXES[:3], AXES[3:]
    return jax.shard_map(
        local,
        mesh=fine,
        in_specs=(P(ctx, tp), P(None, ctx, tp), P(tp, ctx), P(tp, None), P(ctx, tp)),
        out_specs=(P(ctx, tp), P(ctx, tp)),
        check_vma=False,
    )
```

```python
import jax
import jax.numpy as jnp
from jax import lax
from jax.experimental import pallas as pl
from jax.experimental.pallas import tpu as pltpu
from jax.sharding import Mesh, PartitionSpec as P

AXES = ("h", "l", "z", "ylo", "x", "core")
SIZES = (2, 2, 8, 2, 4, 2)
ROWS = 128
HALF = 128
TAPS = 128
GROUP = 16
GROUPS = HALF // GROUP
FEATURES = 256
STREAMS = 4 * HALF
BACK = 3 * HALF
BF16 = jnp.bfloat16
F32 = jnp.float32
VMEM_FORWARD = 40 << 20
VMEM_SMALL = 16 << 20


def bands_kernel(base_ref, band_ref):
    for row in range(2 * GROUPS):
        spread = jnp.broadcast_to(base_ref[row : row + 1, :], (2 * ROWS, 2 * ROWS))
        rolled = pltpu.roll(spread, 0, 1, stride=1, stride_axis=0)
        band_ref[:, row * ROWS : (row + 1) * ROWS] = rolled[:, :ROWS].astype(BF16)


def bands(filters):
    zeros = jnp.zeros((GROUPS, TAPS), filters.dtype)
    causal = jnp.concatenate([zeros, filters], 1)
    anticausal = jnp.concatenate([filters[:, :1], zeros, filters[:, :0:-1]], 1)
    return pl.pallas_call(
        bands_kernel,
        out_shape=jax.ShapeDtypeStruct((2 * ROWS, 2 * GROUPS * ROWS), BF16),
        in_specs=[pl.BlockSpec(memory_space=pltpu.VMEM)],
        out_specs=pl.BlockSpec(memory_space=pltpu.VMEM),
        compiler_params=pltpu.CompilerParams(vmem_limit_bytes=VMEM_SMALL),
    )(jnp.concatenate([causal, anticausal], 0))


def forward_kernel(
    place_ref,
    own_ref,
    other_hbm,
    weight_hbm,
    streams_ref,
    gate_ref,
    product_ref,
    mixed_ref,
    back_ref,
    weight_ref,
    other_ref,
    arrived,
):
    core = place_ref[0]
    copies = []
    others = [pltpu.make_async_copy(other_hbm.at[x], other_ref.at[x], arrived.at[16 + x]) for x in range(4)]
    for x in range(4):
        for y in range(2):
            copies.append(
                pltpu.make_async_copy(
                    weight_hbm.at[pl.ds((x % 2) * 4, 4), core, 2 * y + x // 2],
                    weight_ref.at[x, y],
                    arrived.at[2 * x + y],
                )
            )
    for x in range(4):
        for y in range(2):
            copies.append(
                pltpu.make_async_copy(
                    weight_hbm.at[pl.ds((x % 2) * 4 + 2 * core, 2), :, 2 * y + x // 2],
                    back_ref.at[x % 2, y, x // 2],
                    arrived.at[8 + 2 * x + y],
                )
            )
    for x in range(4):
        others[x].start()
        copies[2 * x].start()
        copies[2 * x + 1].start()
    for copy in copies[8:]:
        copy.start()
    streams, grad_gate = 0.0, 0.0
    contract = (((1,), (1,)), ((), ()))
    for x in range(4):
        tokens, cotangent, weight = [], [], []
        others[x].wait()
        copies[2 * x].wait()
        copies[2 * x + 1].wait()
        for values_ref, which in ((own_ref, core), (other_ref, 1 - core)):
            for y in range(2):
                tokens.append(values_ref[x, :, y, 0].reshape(2 * ROWS, FEATURES))
                cotangent.append(values_ref[x, :, y, 1].reshape(2 * ROWS, FEATURES))
                weight += [weight_ref[x, y, 2 * which + z] for z in range(2)]
        tokens, cotangent = jnp.concatenate(tokens, 1), jnp.concatenate(cotangent, 1)
        weight = jnp.concatenate(weight, 1)
        streams += lax.dot_general(weight[:BACK], tokens, contract, preferred_element_type=F32)
        grad_gate += lax.dot_general(weight[BACK:], cotangent, contract, preferred_element_type=F32)
    streams = streams.astype(BF16)
    streams_ref[...] = streams
    gate_ref[...] = grad_gate
    query, key, value = (streams[i * HALF : (i + 1) * HALF].astype(F32) for i in range(3))
    product_ref[...] = (key * value).astype(BF16)
    mixed_ref[...] = (grad_gate * query).astype(BF16)
    for copy in copies[8:]:
        copy.wait()


def forward(place, own, other, weight):
    vmem = pl.BlockSpec(memory_space=pltpu.VMEM)
    shape = lambda height, kind: jax.ShapeDtypeStruct((height, 2 * ROWS), kind)
    return pl.pallas_call(
        forward_kernel,
        out_shape=(
            shape(BACK, BF16),
            shape(HALF, F32),
            shape(HALF, BF16),
            shape(HALF, BF16),
            jax.ShapeDtypeStruct((2, 2, 2, 2, 2, STREAMS, ROWS), BF16),
        ),
        in_specs=[
            pl.BlockSpec(memory_space=pltpu.SMEM),
            vmem,
            pl.BlockSpec(memory_space=pl.ANY),
            pl.BlockSpec(memory_space=pl.ANY),
        ],
        out_specs=(vmem,) * 5,
        scratch_shapes=[
            pltpu.VMEM((4, 2, 4, STREAMS, ROWS), BF16),
            pltpu.VMEM((4, 2, 2, 2, ROWS, FEATURES), BF16),
            pltpu.SemaphoreType.DMA((20,)),
        ],
        compiler_params=pltpu.CompilerParams(vmem_limit_bytes=VMEM_FORWARD),
        cost_estimate=pl.CostEstimate(flops=1 << 30, bytes_accessed=9 << 20, transcendentals=0),
    )(place, own, other, weight)


def filtered(left, right, band):
    segments = [
        jnp.concatenate([left[s], right[s]], 1) for s in range(2)
    ]
    result = jnp.dot(jnp.concatenate(segments, 0), band, preferred_element_type=F32)
    return [
        jnp.concatenate(
            [
                result[s * HALF + g * GROUP : s * HALF + (g + 1) * GROUP, g * ROWS : (g + 1) * ROWS]
                for g in range(GROUPS)
            ],
            0,
        )
        for s in range(2)
    ]


def middle_kernel(
    place_ref, band_ref, streams_ref, gate_ref, product_ref, mixed_ref, before_ref, after_ref, terms_ref
):
    first = place_ref[1] == 0
    last = place_ref[1] == 15
    lanes = [slice(s * ROWS, (s + 1) * ROWS) for s in range(2)]
    product, mixed, before, after = (
        [ref[:, lanes[s]] for s in range(2)] for ref in (product_ref, mixed_ref, before_ref, after_ref)
    )
    zero = jnp.zeros_like(before[0])
    earlier = [jnp.where(first, zero, before[0]), jnp.where(first, before[0], before[1])]
    later = [jnp.where(last, after[1], after[0]), jnp.where(last, zero, after[1])]
    conv = filtered(earlier, product, band_ref[:, : GROUPS * ROWS])
    back = filtered(mixed, later, band_ref[:, GROUPS * ROWS :])
    for s in range(2):
        query, key, value = (
            streams_ref[i * HALF : (i + 1) * HALF, lanes[s]].astype(F32) for i in range(3)
        )
        terms = (gate_ref[:, lanes[s]] * conv[s], back[s] * value, back[s] * key, query * conv[s])
        for i in range(4):
            terms_ref[lanes[s], i * HALF : (i + 1) * HALF] = terms[i].T.astype(BF16)


def on_chip(kernel, out_shape, operands, flops):
    smem, vmem = pl.BlockSpec(memory_space=pltpu.SMEM), pl.BlockSpec(memory_space=pltpu.VMEM)
    return pl.pallas_call(
        kernel,
        out_shape=out_shape,
        in_specs=[smem] + [vmem] * (len(operands) - 1),
        out_specs=jax.tree.map(lambda _: vmem, out_shape),
        compiler_params=pltpu.CompilerParams(vmem_limit_bytes=VMEM_SMALL),
        cost_estimate=pl.CostEstimate(flops=flops, bytes_accessed=1 << 20, transcendentals=0),
    )(*operands)


def middle(*operands):
    return on_chip(middle_kernel, jax.ShapeDtypeStruct((2 * ROWS, STREAMS), BF16), operands, 1 << 28)


def backward_kernel(place_ref, own_ref, other_ref, weight_ref, out_ref):
    core = place_ref[0]
    for part, cols in enumerate((slice(BACK, STREAMS), slice(0, BACK))):
        terms = jnp.concatenate([own_ref[:, cols], other_ref[:, cols]], 1)
        for y in range(2):
            for x in range(4):
                weight = [
                    jnp.concatenate([weight_ref[x % 2, y, x // 2, z, which, cols] for z in range(2)], 1)
                    for which in (core, 1 - core)
                ]
                result = jnp.dot(terms, jnp.concatenate(weight, 0), preferred_element_type=F32)
                for h in range(2):
                    out_ref[2 * x + y, h, part] = result[h * ROWS : (h + 1) * ROWS].astype(BF16)


def backward(*operands):
    shape = (8, 2, 2, ROWS, FEATURES)
    return on_chip(backward_kernel, jax.ShapeDtypeStruct(shape, BF16), operands, 1 << 30)


def combine(place, parts, turn):
    def kernel(place_ref, parts_ref, total_ref):
        block = place_ref[3] if turn == 0 else 1 - place_ref[3]
        for part in range(2):
            total = 0.0
            for source in range(8):
                total += parts_ref[source, block, part].astype(F32)
            total_ref[part] = total.astype(total_ref.dtype)

    out_shape = jax.ShapeDtypeStruct((2, ROWS, FEATURES), BF16 if turn else F32)
    return on_chip(kernel, out_shape, (place, parts), 1 << 20)


def pack_kernel(in_ref, out_ref, packed_ref):
    for h in range(2):
        chans = slice(h * HALF, (h + 1) * HALF)
        streams = [in_ref[stream, :, chans].astype(F32).T.astype(BF16) for stream in range(3)]
        for l in range(2):
            for stream in range(3):
                packed_ref[2 * h + l, stream * HALF : (stream + 1) * HALF] = streams[stream]
            packed_ref[2 * h + l, BACK:] = out_ref[chans]


def packed(in_weight, out_weight):
    vmem = pl.BlockSpec(memory_space=pltpu.VMEM)
    return pl.pallas_call(
        pack_kernel,
        out_shape=jax.ShapeDtypeStruct((4, STREAMS, ROWS), BF16),
        in_specs=[vmem] * 2,
        out_specs=vmem,
    )(in_weight, out_weight)


def finish_kernel(place_ref, mine_ref, theirs_ref, mixed_ref, grad_ref):
    for part, ref in enumerate((mixed_ref, grad_ref)):
        ref[...] = (mine_ref[part] + theirs_ref[part].astype(F32)).astype(BF16)


def finish(*operands):
    return on_chip(finish_kernel, (jax.ShapeDtypeStruct((ROWS, FEATURES), BF16),) * 2, operands, 1 << 16)


def swapped(value, axes):
    return lax.all_to_all(value, axes, 0, 0, tiled=True)


def gathered(value, axes, count):
    return swapped(jnp.broadcast_to(value[None], (count,) + value.shape), axes)


def local(tokens, in_weight, out_weight, mr_filter, cotangent):
    half, core = lax.axis_index("h"), lax.axis_index("core")
    position = lax.axis_index(("l", "z"))
    place = jnp.stack([core, position, lax.axis_index("x"), half]).astype(jnp.int32)

    weight = swapped(packed(in_weight, out_weight), ("h", "l"))
    values = jnp.stack([tokens, cotangent], 0)
    weight, values = lax.optimization_barrier((weight, values))
    weight = lax.all_gather(weight, ("z", "core"), axis=0).reshape(8, 2, 4, STREAMS, ROWS)

    band = bands(lax.dynamic_slice_in_dim(mr_filter, half * GROUPS, GROUPS, 0))
    values = gathered(values, ("h", "ylo"), 4)
    values = gathered(values, "x", 4).reshape(4, 2, 2, 2, ROWS, FEATURES)
    values, band = lax.optimization_barrier((values, band))
    cross = [(0, 1), (1, 0)]
    other = lax.ppermute(values, "core", cross)

    streams, gate, product, mixed, weight = forward(place, values, other, weight)
    ring = [(n, (n + 1) % 16) for n in range(16)]
    before = lax.ppermute(product, ("l", "z"), ring)
    after = lax.ppermute(mixed, ("l", "z"), [(b, a) for a, b in ring])

    terms = middle(place, band, streams, gate, product, mixed, before, after)
    other_terms = lax.ppermute(terms, "core", cross)

    parts = swapped(backward(place, terms, other_terms, weight), ("x", "ylo"))
    theirs = combine(place, parts, 1)
    theirs, parts = lax.optimization_barrier((theirs, parts))
    theirs = lax.ppermute(theirs, "h", cross)
    return finish(place, combine(place, parts, 0), theirs)


def solution(mesh):
    fine = Mesh(mesh.devices.reshape(SIZES), AXES)
    ctx, tp = AXES[:3], AXES[3:]
    return jax.shard_map(
        local,
        mesh=fine,
        in_specs=(P(ctx, tp), P(None, ctx, tp), P(tp, ctx), P(tp, None), P(ctx, tp)),
        out_specs=(P(ctx, tp), P(ctx, tp)),
        check_vma=False,
    )
```

```python
import jax
import jax.numpy as jnp
from jax import lax
from jax.experimental import pallas as pl
from jax.experimental.pallas import tpu as pltpu
from jax.sharding import Mesh, PartitionSpec as P

AXES = ("h", "l", "z", "ylo", "x", "core")
SIZES = (2, 2, 8, 2, 4, 2)
ROWS = 128
HALF = 128
TAPS = 128
GROUP = 16
GROUPS = HALF // GROUP
FEATURES = 256
STREAMS = 4 * HALF
BACK = 3 * HALF
BF16 = jnp.bfloat16
F32 = jnp.float32
VMEM_FORWARD = 40 << 20
VMEM_SMALL = 16 << 20
VMEM_BANDS = 62 << 20


def bands_kernel(base_ref, band_ref):
    for row in range(2 * GROUPS):
        spread = jnp.broadcast_to(base_ref[row : row + 1, :], (2 * ROWS, 2 * ROWS))
        rolled = pltpu.roll(spread, 0, 1, stride=1, stride_axis=0)
        band_ref[:, row * ROWS : (row + 1) * ROWS] = rolled[:, :ROWS].astype(BF16)


def bands(filters):
    zeros = jnp.zeros((GROUPS, TAPS), filters.dtype)
    causal = jnp.concatenate([zeros, filters], 1)
    anticausal = jnp.concatenate([filters[:, :1], zeros, filters[:, :0:-1]], 1)
    return pl.pallas_call(
        bands_kernel,
        out_shape=jax.ShapeDtypeStruct((2 * ROWS, 2 * GROUPS * ROWS), BF16),
        in_specs=[pl.BlockSpec(memory_space=pltpu.VMEM)],
        out_specs=pl.BlockSpec(memory_space=pltpu.VMEM),
        compiler_params=pltpu.CompilerParams(vmem_limit_bytes=VMEM_BANDS),
    )(jnp.concatenate([causal, anticausal], 0))


def forward_kernel(
    place_ref,
    own_ref,
    other_hbm,
    weight_hbm,
    streams_ref,
    gate_ref,
    product_ref,
    mixed_ref,
    back_ref,
    weight_ref,
    other_ref,
    arrived,
):
    core = place_ref[0]
    copies = []
    others = [pltpu.make_async_copy(other_hbm.at[x], other_ref.at[x], arrived.at[16 + x]) for x in range(4)]
    for x in range(4):
        for y in range(2):
            copies.append(
                pltpu.make_async_copy(
                    weight_hbm.at[pl.ds((x % 2) * 4, 4), core, 2 * y + x // 2],
                    weight_ref.at[x, y],
                    arrived.at[2 * x + y],
                )
            )
    for x in range(4):
        for y in range(2):
            copies.append(
                pltpu.make_async_copy(
                    weight_hbm.at[pl.ds((x % 2) * 4 + 2 * core, 2), :, 2 * y + x // 2],
                    back_ref.at[x % 2, y, x // 2],
                    arrived.at[8 + 2 * x + y],
                )
            )
    for x in range(4):
        others[x].start()
        copies[2 * x].start()
        copies[2 * x + 1].start()
    for copy in copies[8:]:
        copy.start()
    streams, grad_gate = 0.0, 0.0
    contract = (((1,), (1,)), ((), ()))
    for x in range(4):
        tokens, cotangent, weight = [], [], []
        others[x].wait()
        copies[2 * x].wait()
        copies[2 * x + 1].wait()
        for values_ref, which in ((own_ref, core), (other_ref, 1 - core)):
            for y in range(2):
                tokens.append(values_ref[x, :, y, 0].reshape(2 * ROWS, FEATURES))
                cotangent.append(values_ref[x, :, y, 1].reshape(2 * ROWS, FEATURES))
                weight += [weight_ref[x, y, 2 * which + z] for z in range(2)]
        tokens, cotangent = jnp.concatenate(tokens, 1), jnp.concatenate(cotangent, 1)
        weight = jnp.concatenate(weight, 1)
        streams += lax.dot_general(weight[:BACK], tokens, contract, preferred_element_type=F32)
        grad_gate += lax.dot_general(weight[BACK:], cotangent, contract, preferred_element_type=F32)
    streams = streams.astype(BF16)
    streams_ref[...] = streams
    gate_ref[...] = grad_gate
    query, key, value = (streams[i * HALF : (i + 1) * HALF].astype(F32) for i in range(3))
    product_ref[...] = (key * value).astype(BF16)
    mixed_ref[...] = (grad_gate * query).astype(BF16)
    for copy in copies[8:]:
        copy.wait()


def forward(place, own, other, weight):
    vmem = pl.BlockSpec(memory_space=pltpu.VMEM)
    shape = lambda height, kind: jax.ShapeDtypeStruct((height, 2 * ROWS), kind)
    return pl.pallas_call(
        forward_kernel,
        out_shape=(
            shape(BACK, BF16),
            shape(HALF, F32),
            shape(HALF, BF16),
            shape(HALF, BF16),
            jax.ShapeDtypeStruct((2, 2, 2, 2, 2, STREAMS, ROWS), BF16),
        ),
        in_specs=[
            pl.BlockSpec(memory_space=pltpu.SMEM),
            vmem,
            pl.BlockSpec(memory_space=pl.ANY),
            pl.BlockSpec(memory_space=pl.ANY),
        ],
        out_specs=(vmem,) * 5,
        scratch_shapes=[
            pltpu.VMEM((4, 2, 4, STREAMS, ROWS), BF16),
            pltpu.VMEM((4, 2, 2, 2, ROWS, FEATURES), BF16),
            pltpu.SemaphoreType.DMA((20,)),
        ],
        compiler_params=pltpu.CompilerParams(vmem_limit_bytes=VMEM_FORWARD),
        cost_estimate=pl.CostEstimate(flops=1 << 30, bytes_accessed=9 << 20, transcendentals=0),
    )(place, own, other, weight)


def filtered(left, right, band):
    segments = [
        jnp.concatenate([left[s], right[s]], 1) for s in range(2)
    ]
    result = jnp.dot(jnp.concatenate(segments, 0), band, preferred_element_type=F32)
    return [
        jnp.concatenate(
            [
                result[s * HALF + g * GROUP : s * HALF + (g + 1) * GROUP, g * ROWS : (g + 1) * ROWS]
                for g in range(GROUPS)
            ],
            0,
        )
        for s in range(2)
    ]


def middle_kernel(
    place_ref, band_ref, streams_ref, gate_ref, product_ref, mixed_ref, before_ref, after_ref, terms_ref
):
    first = place_ref[1] == 0
    last = place_ref[1] == 15
    lanes = [slice(s * ROWS, (s + 1) * ROWS) for s in range(2)]
    product, mixed, before, after = (
        [ref[:, lanes[s]] for s in range(2)] for ref in (product_ref, mixed_ref, before_ref, after_ref)
    )
    zero = jnp.zeros_like(before[0])
    earlier = [jnp.where(first, zero, before[0]), jnp.where(first, before[0], before[1])]
    later = [jnp.where(last, after[1], after[0]), jnp.where(last, zero, after[1])]
    conv = filtered(earlier, product, band_ref[:, : GROUPS * ROWS])
    back = filtered(mixed, later, band_ref[:, GROUPS * ROWS :])
    for s in range(2):
        query, key, value = (
            streams_ref[i * HALF : (i + 1) * HALF, lanes[s]].astype(F32) for i in range(3)
        )
        terms = (gate_ref[:, lanes[s]] * conv[s], back[s] * value, back[s] * key, query * conv[s])
        for i in range(4):
            terms_ref[lanes[s], i * HALF : (i + 1) * HALF] = terms[i].T.astype(BF16)


def on_chip(kernel, out_shape, operands, flops):
    smem, vmem = pl.BlockSpec(memory_space=pltpu.SMEM), pl.BlockSpec(memory_space=pltpu.VMEM)
    return pl.pallas_call(
        kernel,
        out_shape=out_shape,
        in_specs=[smem] + [vmem] * (len(operands) - 1),
        out_specs=jax.tree.map(lambda _: vmem, out_shape),
        compiler_params=pltpu.CompilerParams(vmem_limit_bytes=VMEM_SMALL),
        cost_estimate=pl.CostEstimate(flops=flops, bytes_accessed=1 << 20, transcendentals=0),
    )(*operands)


def middle(*operands):
    return on_chip(middle_kernel, jax.ShapeDtypeStruct((2 * ROWS, STREAMS), BF16), operands, 1 << 28)


def backward_kernel(place_ref, own_ref, other_ref, weight_ref, out_ref):
    core = place_ref[0]
    for part, cols in enumerate((slice(BACK, STREAMS), slice(0, BACK))):
        terms = jnp.concatenate([own_ref[:, cols], other_ref[:, cols]], 1)
        for y in range(2):
            for x in range(4):
                weight = [
                    jnp.concatenate([weight_ref[x % 2, y, x // 2, z, which, cols] for z in range(2)], 1)
                    for which in (core, 1 - core)
                ]
                result = jnp.dot(terms, jnp.concatenate(weight, 0), preferred_element_type=F32)
                for h in range(2):
                    out_ref[2 * x + y, h, part] = result[h * ROWS : (h + 1) * ROWS].astype(BF16)


def backward(*operands):
    shape = (8, 2, 2, ROWS, FEATURES)
    return on_chip(backward_kernel, jax.ShapeDtypeStruct(shape, BF16), operands, 1 << 30)


def combine_kernel(place_ref, parts_ref, mine_ref, theirs_ref):
    half = place_ref[3]
    for part in range(2):
        mine, theirs = 0.0, 0.0
        for source in range(8):
            mine += parts_ref[source, half, part].astype(F32)
            theirs += parts_ref[source, 1 - half, part].astype(F32)
        mine_ref[part] = mine
        theirs_ref[part] = theirs.astype(BF16)


def combine(*operands):
    shape = (2, ROWS, FEATURES)
    out_shape = (jax.ShapeDtypeStruct(shape, F32), jax.ShapeDtypeStruct(shape, BF16))
    return on_chip(combine_kernel, out_shape, operands, 1 << 20)


def pack_kernel(in_ref, out_ref, packed_ref):
    for h in range(2):
        chans = slice(h * HALF, (h + 1) * HALF)
        streams = [in_ref[stream, :, chans].astype(F32).T.astype(BF16) for stream in range(3)]
        for l in range(2):
            for stream in range(3):
                packed_ref[2 * h + l, stream * HALF : (stream + 1) * HALF] = streams[stream]
            packed_ref[2 * h + l, BACK:] = out_ref[chans]


def packed(in_weight, out_weight):
    vmem = pl.BlockSpec(memory_space=pltpu.VMEM)
    return pl.pallas_call(
        pack_kernel,
        out_shape=jax.ShapeDtypeStruct((4, STREAMS, ROWS), BF16),
        in_specs=[vmem] * 2,
        out_specs=vmem,
    )(in_weight, out_weight)


def finish_kernel(place_ref, mine_ref, theirs_ref, mixed_ref, grad_ref):
    for part, ref in enumerate((mixed_ref, grad_ref)):
        ref[...] = (mine_ref[part] + theirs_ref[part].astype(F32)).astype(BF16)


def finish(*operands):
    return on_chip(finish_kernel, (jax.ShapeDtypeStruct((ROWS, FEATURES), BF16),) * 2, operands, 1 << 16)


def swapped(value, axes):
    return lax.all_to_all(value, axes, 0, 0, tiled=True)


def gathered(value, axes, count):
    return swapped(jnp.broadcast_to(value[None], (count,) + value.shape), axes)


def local(tokens, in_weight, out_weight, mr_filter, cotangent):
    half, core = lax.axis_index("h"), lax.axis_index("core")
    position = lax.axis_index(("l", "z"))
    place = jnp.stack([core, position, lax.axis_index("x"), half]).astype(jnp.int32)

    weight = swapped(packed(in_weight, out_weight), ("h", "l"))
    values = jnp.stack([tokens, cotangent], 0)
    band = bands(lax.dynamic_slice_in_dim(mr_filter, half * GROUPS, GROUPS, 0))
    weight, values, band = lax.optimization_barrier((weight, values, band))
    weight = lax.all_gather(weight, ("z", "core"), axis=0).reshape(8, 2, 4, STREAMS, ROWS)

    values = gathered(values, ("h", "ylo"), 4)
    values = gathered(values, "x", 4).reshape(4, 2, 2, 2, ROWS, FEATURES)
    cross = [(0, 1), (1, 0)]
    other = lax.ppermute(values, "core", cross)

    streams, gate, product, mixed, weight = forward(place, values, other, weight)
    ring = [(n, (n + 1) % 16) for n in range(16)]
    before = lax.ppermute(product, ("l", "z"), ring)
    after = lax.ppermute(mixed, ("l", "z"), [(b, a) for a, b in ring])

    terms = middle(place, band, streams, gate, product, mixed, before, after)
    other_terms = lax.ppermute(terms, "core", cross)

    parts = swapped(backward(place, terms, other_terms, weight), ("x", "ylo"))
    mine, theirs = combine(place, parts)
    return finish(place, mine, lax.ppermute(theirs, "h", cross))


def solution(mesh):
    fine = Mesh(mesh.devices.reshape(SIZES), AXES)
    ctx, tp = AXES[:3], AXES[3:]
    return jax.shard_map(
        local,
        mesh=fine,
        in_specs=(P(ctx, tp), P(None, ctx, tp), P(tp, ctx), P(tp, None), P(ctx, tp)),
        out_specs=(P(ctx, tp), P(ctx, tp)),
        check_vma=False,
    )
```

```python
import jax
import jax.numpy as jnp
from jax import lax
from jax.experimental import pallas as pl
from jax.experimental.pallas import tpu as pltpu
from jax.sharding import Mesh, PartitionSpec as P

AXES = ("h", "l", "z", "ylo", "x", "core")
SIZES = (2, 2, 8, 2, 4, 2)
ROWS = 128
HALF = 128
TAPS = 128
GROUP = 16
GROUPS = HALF // GROUP
FEATURES = 256
STREAMS = 4 * HALF
BACK = 3 * HALF
BF16 = jnp.bfloat16
F32 = jnp.float32
VMEM_FORWARD = 40 << 20
VMEM_SMALL = 16 << 20


def bands_kernel(base_ref, band_ref):
    for row in range(2 * GROUPS):
        spread = jnp.broadcast_to(base_ref[row : row + 1, :], (2 * ROWS, 2 * ROWS))
        rolled = pltpu.roll(spread, 0, 1, stride=1, stride_axis=0)
        band_ref[:, row * ROWS : (row + 1) * ROWS] = rolled[:, :ROWS].astype(BF16)


def bands(filters):
    zeros = jnp.zeros((GROUPS, TAPS), filters.dtype)
    causal = jnp.concatenate([zeros, filters], 1)
    anticausal = jnp.concatenate([filters[:, :1], zeros, filters[:, :0:-1]], 1)
    return pl.pallas_call(
        bands_kernel,
        out_shape=jax.ShapeDtypeStruct((2 * ROWS, 2 * GROUPS * ROWS), BF16),
        in_specs=[pl.BlockSpec(memory_space=pltpu.VMEM)],
        out_specs=pl.BlockSpec(memory_space=pltpu.VMEM),
        compiler_params=pltpu.CompilerParams(vmem_limit_bytes=VMEM_SMALL),
    )(jnp.concatenate([causal, anticausal], 0))


def forward_kernel(
    place_ref,
    own_ref,
    other_hbm,
    weight_hbm,
    streams_ref,
    gate_ref,
    product_ref,
    mixed_ref,
    back_ref,
    weight_ref,
    other_ref,
    arrived,
):
    core = place_ref[0]
    copies = []
    others = [pltpu.make_async_copy(other_hbm.at[x], other_ref.at[x], arrived.at[16 + x]) for x in range(4)]
    for x in range(4):
        for y in range(2):
            copies.append(
                pltpu.make_async_copy(
                    weight_hbm.at[pl.ds((x % 2) * 4, 4), core, 2 * y + x // 2],
                    weight_ref.at[x, y],
                    arrived.at[2 * x + y],
                )
            )
    for x in range(4):
        for y in range(2):
            copies.append(
                pltpu.make_async_copy(
                    weight_hbm.at[pl.ds((x % 2) * 4 + 2 * core, 2), :, 2 * y + x // 2],
                    back_ref.at[x % 2, y, x // 2],
                    arrived.at[8 + 2 * x + y],
                )
            )
    for x in range(4):
        others[x].start()
        copies[2 * x].start()
        copies[2 * x + 1].start()
    for copy in copies[8:]:
        copy.start()
    streams, grad_gate = 0.0, 0.0
    contract = (((1,), (1,)), ((), ()))
    for x in range(4):
        tokens, cotangent, weight = [], [], []
        others[x].wait()
        copies[2 * x].wait()
        copies[2 * x + 1].wait()
        for values_ref, which in ((own_ref, core), (other_ref, 1 - core)):
            for y in range(2):
                tokens.append(values_ref[x, :, y, 0].reshape(2 * ROWS, FEATURES))
                cotangent.append(values_ref[x, :, y, 1].reshape(2 * ROWS, FEATURES))
                weight += [weight_ref[x, y, 2 * which + z] for z in range(2)]
        tokens, cotangent = jnp.concatenate(tokens, 1), jnp.concatenate(cotangent, 1)
        weight = jnp.concatenate(weight, 1)
        streams += lax.dot_general(weight[:BACK], tokens, contract, preferred_element_type=F32)
        grad_gate += lax.dot_general(weight[BACK:], cotangent, contract, preferred_element_type=F32)
    streams = streams.astype(BF16)
    streams_ref[...] = streams
    gate_ref[...] = grad_gate
    query, key, value = (streams[i * HALF : (i + 1) * HALF].astype(F32) for i in range(3))
    product_ref[...] = (key * value).astype(BF16)
    mixed_ref[...] = (grad_gate * query).astype(BF16)
    for copy in copies[8:]:
        copy.wait()


def forward(place, own, other, weight):
    vmem = pl.BlockSpec(memory_space=pltpu.VMEM)
    shape = lambda height, kind: jax.ShapeDtypeStruct((height, 2 * ROWS), kind)
    return pl.pallas_call(
        forward_kernel,
        out_shape=(
            shape(BACK, BF16),
            shape(HALF, F32),
            shape(HALF, BF16),
            shape(HALF, BF16),
            jax.ShapeDtypeStruct((2, 2, 2, 2, 2, STREAMS, ROWS), BF16),
        ),
        in_specs=[
            pl.BlockSpec(memory_space=pltpu.SMEM),
            vmem,
            pl.BlockSpec(memory_space=pl.ANY),
            pl.BlockSpec(memory_space=pl.ANY),
        ],
        out_specs=(vmem,) * 5,
        scratch_shapes=[
            pltpu.VMEM((4, 2, 4, STREAMS, ROWS), BF16),
            pltpu.VMEM((4, 2, 2, 2, ROWS, FEATURES), BF16),
            pltpu.SemaphoreType.DMA((20,)),
        ],
        compiler_params=pltpu.CompilerParams(vmem_limit_bytes=VMEM_FORWARD),
        cost_estimate=pl.CostEstimate(flops=1 << 30, bytes_accessed=9 << 20, transcendentals=0),
    )(place, own, other, weight)


def filtered(left, right, band):
    segments = [
        jnp.concatenate([left[s], right[s]], 1) for s in range(2)
    ]
    result = jnp.dot(jnp.concatenate(segments, 0), band, preferred_element_type=F32)
    return [
        jnp.concatenate(
            [
                result[s * HALF + g * GROUP : s * HALF + (g + 1) * GROUP, g * ROWS : (g + 1) * ROWS]
                for g in range(GROUPS)
            ],
            0,
        )
        for s in range(2)
    ]


def middle_kernel(
    place_ref, band_ref, streams_ref, gate_ref, product_ref, mixed_ref, before_ref, after_ref, terms_ref
):
    first = place_ref[1] == 0
    last = place_ref[1] == 15
    lanes = [slice(s * ROWS, (s + 1) * ROWS) for s in range(2)]
    product, mixed, before, after = (
        [ref[:, lanes[s]] for s in range(2)] for ref in (product_ref, mixed_ref, before_ref, after_ref)
    )
    zero = jnp.zeros_like(before[0])
    earlier = [jnp.where(first, zero, before[0]), jnp.where(first, before[0], before[1])]
    later = [jnp.where(last, after[1], after[0]), jnp.where(last, zero, after[1])]
    conv = filtered(earlier, product, band_ref[:, : GROUPS * ROWS])
    back = filtered(mixed, later, band_ref[:, GROUPS * ROWS :])
    for s in range(2):
        query, key, value = (
            streams_ref[i * HALF : (i + 1) * HALF, lanes[s]].astype(F32) for i in range(3)
        )
        terms = (gate_ref[:, lanes[s]] * conv[s], back[s] * value, back[s] * key, query * conv[s])
        for i in range(4):
            terms_ref[lanes[s], i * HALF : (i + 1) * HALF] = terms[i].T.astype(BF16)


def on_chip(kernel, out_shape, operands, flops):
    smem, vmem = pl.BlockSpec(memory_space=pltpu.SMEM), pl.BlockSpec(memory_space=pltpu.VMEM)
    return pl.pallas_call(
        kernel,
        out_shape=out_shape,
        in_specs=[smem] + [vmem] * (len(operands) - 1),
        out_specs=jax.tree.map(lambda _: vmem, out_shape),
        compiler_params=pltpu.CompilerParams(vmem_limit_bytes=VMEM_SMALL),
        cost_estimate=pl.CostEstimate(flops=flops, bytes_accessed=1 << 20, transcendentals=0),
    )(*operands)


def middle(*operands):
    return on_chip(middle_kernel, jax.ShapeDtypeStruct((2 * ROWS, STREAMS), BF16), operands, 1 << 28)


def backward_kernel(place_ref, terms_ref, weight_ref, out_ref):
    for part, cols in enumerate((slice(BACK, STREAMS), slice(0, BACK))):
        terms = jnp.concatenate([terms_ref[core, :, cols] for core in range(2)], 1)
        for y in range(2):
            for x in range(4):
                weight = [
                    jnp.concatenate([weight_ref[x % 2, y, x // 2, z, core, cols] for z in range(2)], 1)
                    for core in range(2)
                ]
                result = jnp.dot(terms, jnp.concatenate(weight, 0), preferred_element_type=F32)
                for h in range(2):
                    out_ref[4 * y + x, h, part] = result[h * ROWS : (h + 1) * ROWS].astype(BF16)


def backward(*operands):
    shape = (8, 2, 2, ROWS, FEATURES)
    return on_chip(backward_kernel, jax.ShapeDtypeStruct(shape, BF16), operands, 1 << 30)


def combine_kernel(place_ref, parts_ref, mine_ref, theirs_ref):
    half = place_ref[3]
    for part in range(2):
        mine, theirs = 0.0, 0.0
        for source in range(8):
            mine += parts_ref[source, half, part].astype(F32)
            theirs += parts_ref[source, 1 - half, part].astype(F32)
        mine_ref[part] = mine
        theirs_ref[part] = theirs.astype(BF16)


def combine(*operands):
    shape = (2, ROWS, FEATURES)
    out_shape = (jax.ShapeDtypeStruct(shape, F32), jax.ShapeDtypeStruct(shape, BF16))
    return on_chip(combine_kernel, out_shape, operands, 1 << 20)


def pack_kernel(in_ref, out_ref, packed_ref):
    for h in range(2):
        chans = slice(h * HALF, (h + 1) * HALF)
        streams = [in_ref[stream, :, chans].astype(F32).T.astype(BF16) for stream in range(3)]
        for l in range(2):
            for stream in range(3):
                packed_ref[2 * h + l, stream * HALF : (stream + 1) * HALF] = streams[stream]
            packed_ref[2 * h + l, BACK:] = out_ref[chans]


def packed(in_weight, out_weight):
    vmem = pl.BlockSpec(memory_space=pltpu.VMEM)
    return pl.pallas_call(
        pack_kernel,
        out_shape=jax.ShapeDtypeStruct((4, STREAMS, ROWS), BF16),
        in_specs=[vmem] * 2,
        out_specs=vmem,
    )(in_weight, out_weight)


def finish_kernel(place_ref, mine_ref, theirs_ref, mixed_ref, grad_ref):
    for part, ref in enumerate((mixed_ref, grad_ref)):
        ref[...] = (mine_ref[part] + theirs_ref[part].astype(F32)).astype(BF16)


def finish(*operands):
    return on_chip(finish_kernel, (jax.ShapeDtypeStruct((ROWS, FEATURES), BF16),) * 2, operands, 1 << 16)


def swapped(value, axes):
    return lax.all_to_all(value, axes, 0, 0, tiled=True)


def gathered(value, axes, count):
    return swapped(jnp.broadcast_to(value[None], (count,) + value.shape), axes)


def local(tokens, in_weight, out_weight, mr_filter, cotangent):
    half, core = lax.axis_index("h"), lax.axis_index("core")
    position = lax.axis_index(("l", "z"))
    place = jnp.stack([core, position, lax.axis_index("x"), half]).astype(jnp.int32)

    weight = swapped(packed(in_weight, out_weight), ("h", "l"))
    values = jnp.stack([tokens, cotangent], 0)
    weight, values = lax.optimization_barrier((weight, values))
    weight = lax.all_gather(weight, ("z", "core"), axis=0).reshape(8, 2, 4, STREAMS, ROWS)

    band = bands(lax.dynamic_slice_in_dim(mr_filter, half * GROUPS, GROUPS, 0))
    values = gathered(values, ("h", "ylo"), 4)
    values = gathered(values, "x", 4).reshape(4, 2, 2, 2, ROWS, FEATURES)
    values, band = lax.optimization_barrier((values, band))
    cross = [(0, 1), (1, 0)]
    other = lax.ppermute(values, "core", cross)

    streams, gate, product, mixed, weight = forward(place, values, other, weight)
    ring = [(n, (n + 1) % 16) for n in range(16)]
    before = lax.ppermute(product, ("l", "z"), ring)
    after = lax.ppermute(mixed, ("l", "z"), [(b, a) for a, b in ring])

    terms = middle(place, band, streams, gate, product, mixed, before, after)
    terms = lax.all_gather(terms, "core", axis=0)

    parts = swapped(backward(place, terms, weight), ("ylo", "x"))
    mine, theirs = combine(place, parts)
    return finish(place, mine, lax.ppermute(theirs, "h", cross))


def solution(mesh):
    fine = Mesh(mesh.devices.reshape(SIZES), AXES)
    ctx, tp = AXES[:3], AXES[3:]
    return jax.shard_map(
        local,
        mesh=fine,
        in_specs=(P(ctx, tp), P(None, ctx, tp), P(tp, ctx), P(tp, None), P(ctx, tp)),
        out_specs=(P(ctx, tp), P(ctx, tp)),
        check_vma=False,
    )
```

```python
import jax
import jax.numpy as jnp
from jax import lax
from jax.experimental import pallas as pl
from jax.experimental.pallas import tpu as pltpu
from jax.sharding import Mesh, PartitionSpec as P

AXES = ("h", "l", "z", "ylo", "x", "core")
SIZES = (2, 2, 8, 2, 4, 2)
ROWS = 128
HALF = 128
TAPS = 128
GROUP = 16
GROUPS = HALF // GROUP
FEATURES = 256
STREAMS = 4 * HALF
BACK = 3 * HALF
BF16 = jnp.bfloat16
F32 = jnp.float32
VMEM_FORWARD = 40 << 20
VMEM_SMALL = 16 << 20


def bands_kernel(base_ref, band_ref):
    for row in range(2 * GROUPS):
        spread = jnp.broadcast_to(base_ref[row : row + 1, :], (2 * ROWS, 2 * ROWS))
        rolled = pltpu.roll(spread, 0, 1, stride=1, stride_axis=0)
        band_ref[:, row * ROWS : (row + 1) * ROWS] = rolled[:, :ROWS].astype(BF16)


def bands(filters):
    zeros = jnp.zeros((GROUPS, TAPS), filters.dtype)
    causal = jnp.concatenate([zeros, filters], 1)
    anticausal = jnp.concatenate([filters[:, :1], zeros, filters[:, :0:-1]], 1)
    return pl.pallas_call(
        bands_kernel,
        out_shape=jax.ShapeDtypeStruct((2 * ROWS, 2 * GROUPS * ROWS), BF16),
        in_specs=[pl.BlockSpec(memory_space=pltpu.VMEM)],
        out_specs=pl.BlockSpec(memory_space=pltpu.VMEM),
        compiler_params=pltpu.CompilerParams(vmem_limit_bytes=VMEM_SMALL),
    )(jnp.concatenate([causal, anticausal], 0))


def forward_kernel(
    place_ref,
    own_ref,
    other_hbm,
    weight_hbm,
    streams_ref,
    gate_ref,
    product_ref,
    mixed_ref,
    first_ref,
    second_ref,
    back_ref,
    weight_ref,
    other_ref,
    arrived,
):
    core = place_ref[0]
    copies = []
    others = [pltpu.make_async_copy(other_hbm.at[x], other_ref.at[x], arrived.at[16 + x]) for x in range(4)]
    for x in range(4):
        for y in range(2):
            copies.append(
                pltpu.make_async_copy(
                    weight_hbm.at[pl.ds((x % 2) * 4, 4), core, 2 * y + x // 2],
                    weight_ref.at[x, y],
                    arrived.at[2 * x + y],
                )
            )
    for x in range(4):
        for y in range(2):
            copies.append(
                pltpu.make_async_copy(
                    weight_hbm.at[pl.ds((x % 2) * 4 + 2 * core, 2), :, 2 * y + x // 2],
                    back_ref.at[x % 2, y, x // 2],
                    arrived.at[8 + 2 * x + y],
                )
            )
    for x in range(4):
        others[x].start()
        copies[2 * x].start()
        copies[2 * x + 1].start()
    for copy in copies[8:]:
        copy.start()
    streams, grad_gate = 0.0, 0.0
    contract = (((1,), (1,)), ((), ()))
    for x in range(4):
        tokens, cotangent, weight = [], [], []
        others[x].wait()
        copies[2 * x].wait()
        copies[2 * x + 1].wait()
        for values_ref, which in ((own_ref, core), (other_ref, 1 - core)):
            for y in range(2):
                tokens.append(values_ref[x, :, y, 0].reshape(2 * ROWS, FEATURES))
                cotangent.append(values_ref[x, :, y, 1].reshape(2 * ROWS, FEATURES))
                weight += [weight_ref[x, y, 2 * which + z] for z in range(2)]
        tokens, cotangent = jnp.concatenate(tokens, 1), jnp.concatenate(cotangent, 1)
        weight = jnp.concatenate(weight, 1)
        streams += lax.dot_general(weight[:BACK], tokens, contract, preferred_element_type=F32)
        grad_gate += lax.dot_general(weight[BACK:], cotangent, contract, preferred_element_type=F32)
    streams = streams.astype(BF16)
    streams_ref[...] = streams
    gate_ref[...] = grad_gate
    query, key, value = (streams[i * HALF : (i + 1) * HALF].astype(F32) for i in range(3))
    product = (key * value).astype(BF16)
    mixed = (grad_gate * query).astype(BF16)
    product_ref[...] = product
    mixed_ref[...] = mixed
    even = lax.rem(place_ref[1], 2) == 0
    first_ref[...] = jnp.where(even, product, mixed)
    second_ref[...] = jnp.where(even, mixed, product)
    for copy in copies[8:]:
        copy.wait()


def forward(place, own, other, weight):
    vmem = pl.BlockSpec(memory_space=pltpu.VMEM)
    shape = lambda height, kind: jax.ShapeDtypeStruct((height, 2 * ROWS), kind)
    return pl.pallas_call(
        forward_kernel,
        out_shape=(
            shape(BACK, BF16),
            shape(HALF, F32),
            shape(HALF, BF16),
            shape(HALF, BF16),
            shape(HALF, BF16),
            shape(HALF, BF16),
            jax.ShapeDtypeStruct((2, 2, 2, 2, 2, STREAMS, ROWS), BF16),
        ),
        in_specs=[
            pl.BlockSpec(memory_space=pltpu.SMEM),
            vmem,
            pl.BlockSpec(memory_space=pl.ANY),
            pl.BlockSpec(memory_space=pl.ANY),
        ],
        out_specs=(vmem,) * 7,
        scratch_shapes=[
            pltpu.VMEM((4, 2, 4, STREAMS, ROWS), BF16),
            pltpu.VMEM((4, 2, 2, 2, ROWS, FEATURES), BF16),
            pltpu.SemaphoreType.DMA((20,)),
        ],
        compiler_params=pltpu.CompilerParams(vmem_limit_bytes=VMEM_FORWARD),
        cost_estimate=pl.CostEstimate(flops=1 << 30, bytes_accessed=9 << 20, transcendentals=0),
    )(place, own, other, weight)


def filtered(left, right, band):
    segments = [
        jnp.concatenate([left[s], right[s]], 1) for s in range(2)
    ]
    result = jnp.dot(jnp.concatenate(segments, 0), band, preferred_element_type=F32)
    return [
        jnp.concatenate(
            [
                result[s * HALF + g * GROUP : s * HALF + (g + 1) * GROUP, g * ROWS : (g + 1) * ROWS]
                for g in range(GROUPS)
            ],
            0,
        )
        for s in range(2)
    ]


def middle_kernel(
    place_ref, band_ref, streams_ref, gate_ref, product_ref, mixed_ref, first_ref, second_ref, terms_ref
):
    first = place_ref[1] == 0
    last = place_ref[1] == 15
    lanes = [slice(s * ROWS, (s + 1) * ROWS) for s in range(2)]
    even = lax.rem(place_ref[1], 2) == 0
    product, mixed, one, two = (
        [ref[:, lanes[s]] for s in range(2)] for ref in (product_ref, mixed_ref, first_ref, second_ref)
    )
    before = [jnp.where(even, two[s], one[s]) for s in range(2)]
    after = [jnp.where(even, one[s], two[s]) for s in range(2)]
    zero = jnp.zeros_like(before[0])
    earlier = [jnp.where(first, zero, before[0]), jnp.where(first, before[0], before[1])]
    later = [jnp.where(last, after[1], after[0]), jnp.where(last, zero, after[1])]
    conv = filtered(earlier, product, band_ref[:, : GROUPS * ROWS])
    back = filtered(mixed, later, band_ref[:, GROUPS * ROWS :])
    for s in range(2):
        query, key, value = (
            streams_ref[i * HALF : (i + 1) * HALF, lanes[s]].astype(F32) for i in range(3)
        )
        terms = (gate_ref[:, lanes[s]] * conv[s], back[s] * value, back[s] * key, query * conv[s])
        for i in range(4):
            terms_ref[lanes[s], i * HALF : (i + 1) * HALF] = terms[i].T.astype(BF16)


def on_chip(kernel, out_shape, operands, flops):
    smem, vmem = pl.BlockSpec(memory_space=pltpu.SMEM), pl.BlockSpec(memory_space=pltpu.VMEM)
    return pl.pallas_call(
        kernel,
        out_shape=out_shape,
        in_specs=[smem] + [vmem] * (len(operands) - 1),
        out_specs=jax.tree.map(lambda _: vmem, out_shape),
        compiler_params=pltpu.CompilerParams(vmem_limit_bytes=VMEM_SMALL),
        cost_estimate=pl.CostEstimate(flops=flops, bytes_accessed=1 << 20, transcendentals=0),
    )(*operands)


def middle(*operands):
    return on_chip(middle_kernel, jax.ShapeDtypeStruct((2 * ROWS, STREAMS), BF16), operands, 1 << 28)


def backward_kernel(place_ref, terms_ref, weight_ref, out_ref):
    for part, cols in enumerate((slice(BACK, STREAMS), slice(0, BACK))):
        terms = jnp.concatenate([terms_ref[core, :, cols] for core in range(2)], 1)
        for y in range(2):
            for x in range(4):
                weight = [
                    jnp.concatenate([weight_ref[x % 2, y, x // 2, z, core, cols] for z in range(2)], 1)
                    for core in range(2)
                ]
                result = jnp.dot(terms, jnp.concatenate(weight, 0), preferred_element_type=F32)
                for h in range(2):
                    out_ref[4 * y + x, h, part] = result[h * ROWS : (h + 1) * ROWS].astype(BF16)


def backward(*operands):
    shape = (8, 2, 2, ROWS, FEATURES)
    return on_chip(backward_kernel, jax.ShapeDtypeStruct(shape, BF16), operands, 1 << 30)


def combine_kernel(place_ref, parts_ref, mine_ref, theirs_ref):
    half = place_ref[3]
    for part in range(2):
        mine, theirs = 0.0, 0.0
        for source in range(8):
            mine += parts_ref[source, half, part].astype(F32)
            theirs += parts_ref[source, 1 - half, part].astype(F32)
        mine_ref[part] = mine
        theirs_ref[part] = theirs.astype(BF16)


def combine(*operands):
    shape = (2, ROWS, FEATURES)
    out_shape = (jax.ShapeDtypeStruct(shape, F32), jax.ShapeDtypeStruct(shape, BF16))
    return on_chip(combine_kernel, out_shape, operands, 1 << 20)


def pack_kernel(in_ref, out_ref, packed_ref):
    for h in range(2):
        chans = slice(h * HALF, (h + 1) * HALF)
        streams = [in_ref[stream, :, chans].astype(F32).T.astype(BF16) for stream in range(3)]
        for l in range(2):
            for stream in range(3):
                packed_ref[2 * h + l, stream * HALF : (stream + 1) * HALF] = streams[stream]
            packed_ref[2 * h + l, BACK:] = out_ref[chans]


def packed(in_weight, out_weight):
    vmem = pl.BlockSpec(memory_space=pltpu.VMEM)
    return pl.pallas_call(
        pack_kernel,
        out_shape=jax.ShapeDtypeStruct((4, STREAMS, ROWS), BF16),
        in_specs=[vmem] * 2,
        out_specs=vmem,
    )(in_weight, out_weight)


def finish_kernel(place_ref, mine_ref, theirs_ref, mixed_ref, grad_ref):
    for part, ref in enumerate((mixed_ref, grad_ref)):
        ref[...] = (mine_ref[part] + theirs_ref[part].astype(F32)).astype(BF16)


def finish(*operands):
    return on_chip(finish_kernel, (jax.ShapeDtypeStruct((ROWS, FEATURES), BF16),) * 2, operands, 1 << 16)


def swapped(value, axes):
    return lax.all_to_all(value, axes, 0, 0, tiled=True)


def gathered(value, axes, count):
    return swapped(jnp.broadcast_to(value[None], (count,) + value.shape), axes)


def local(tokens, in_weight, out_weight, mr_filter, cotangent):
    half, core = lax.axis_index("h"), lax.axis_index("core")
    position = lax.axis_index(("l", "z"))
    place = jnp.stack([core, position, lax.axis_index("x"), half]).astype(jnp.int32)

    weight = swapped(packed(in_weight, out_weight), ("h", "l"))
    values = jnp.stack([tokens, cotangent], 0)
    weight, values = lax.optimization_barrier((weight, values))
    weight = lax.all_gather(weight, ("z", "core"), axis=0).reshape(8, 2, 4, STREAMS, ROWS)

    band = bands(lax.dynamic_slice_in_dim(mr_filter, half * GROUPS, GROUPS, 0))
    values = gathered(values, ("h", "ylo"), 4)
    values = gathered(values, "x", 4).reshape(4, 2, 2, 2, ROWS, FEATURES)
    values, band = lax.optimization_barrier((values, band))
    cross = [(0, 1), (1, 0)]
    other = lax.ppermute(values, "core", cross)

    streams, gate, product, mixed, first, second, weight = forward(place, values, other, weight)
    first = lax.ppermute(first, ("l", "z"), [(n, n ^ 1) for n in range(16)])
    second = lax.ppermute(second, ("l", "z"), [(n, ((n + 1) ^ 1) - 1 & 15) for n in range(16)])

    terms = middle(place, band, streams, gate, product, mixed, first, second)
    terms = lax.all_gather(terms, "core", axis=0)

    parts = swapped(backward(place, terms, weight), ("ylo", "x"))
    mine, theirs = combine(place, parts)
    return finish(place, mine, lax.ppermute(theirs, "h", cross))


def solution(mesh):
    fine = Mesh(mesh.devices.reshape(SIZES), AXES)
    ctx, tp = AXES[:3], AXES[3:]
    return jax.shard_map(
        local,
        mesh=fine,
        in_specs=(P(ctx, tp), P(None, ctx, tp), P(tp, ctx), P(tp, None), P(ctx, tp)),
        out_specs=(P(ctx, tp), P(ctx, tp)),
        check_vma=False,
    )
```

```python
import jax
import jax.numpy as jnp
from jax import lax
from jax.experimental import pallas as pl
from jax.experimental.pallas import tpu as pltpu
from jax.sharding import Mesh, PartitionSpec as P

AXES = ("h", "l", "z", "ylo", "x", "core")
SIZES = (2, 2, 8, 2, 4, 2)
ROWS = 128
HALF = 128
TAPS = 128
GROUP = 16
GROUPS = HALF // GROUP
FEATURES = 256
STREAMS = 4 * HALF
BACK = 3 * HALF
BF16 = jnp.bfloat16
F32 = jnp.float32
VMEM_FORWARD = 40 << 20
VMEM_SMALL = 16 << 20


def bands_kernel(base_ref, band_ref):
    for row in range(2 * GROUPS):
        spread = jnp.broadcast_to(base_ref[row : row + 1, :], (2 * ROWS, 2 * ROWS))
        rolled = pltpu.roll(spread, 0, 1, stride=1, stride_axis=0)
        band_ref[:, row * ROWS : (row + 1) * ROWS] = rolled[:, :ROWS].astype(BF16)


def bands(filters):
    zeros = jnp.zeros((GROUPS, TAPS), filters.dtype)
    causal = jnp.concatenate([zeros, filters], 1)
    anticausal = jnp.concatenate([filters[:, :1], zeros, filters[:, :0:-1]], 1)
    return pl.pallas_call(
        bands_kernel,
        out_shape=jax.ShapeDtypeStruct((2 * ROWS, 2 * GROUPS * ROWS), BF16),
        in_specs=[pl.BlockSpec(memory_space=pltpu.VMEM)],
        out_specs=pl.BlockSpec(memory_space=pltpu.VMEM),
        compiler_params=pltpu.CompilerParams(vmem_limit_bytes=VMEM_SMALL),
    )(jnp.concatenate([causal, anticausal], 0))


def forward_kernel(
    place_ref,
    own_ref,
    other_hbm,
    weight_hbm,
    streams_ref,
    gate_ref,
    product_ref,
    mixed_ref,
    back_ref,
    weight_ref,
    other_ref,
    arrived,
):
    core = place_ref[0]
    copies = []
    others = [pltpu.make_async_copy(other_hbm.at[x], other_ref.at[x], arrived.at[16 + x]) for x in range(4)]
    for x in range(4):
        for y in range(2):
            copies.append(
                pltpu.make_async_copy(
                    weight_hbm.at[pl.ds((x % 2) * 4, 4), core, 2 * y + x // 2],
                    weight_ref.at[x, y],
                    arrived.at[2 * x + y],
                )
            )
    for x in range(4):
        for y in range(2):
            copies.append(
                pltpu.make_async_copy(
                    weight_hbm.at[pl.ds((x % 2) * 4 + 2 * core, 2), :, 2 * y + x // 2],
                    back_ref.at[x % 2, y, x // 2],
                    arrived.at[8 + 2 * x + y],
                )
            )
    for x in range(4):
        others[x].start()
        copies[2 * x].start()
        copies[2 * x + 1].start()
    for copy in copies[8:]:
        copy.start()
    streams, grad_gate = 0.0, 0.0
    contract = (((1,), (1,)), ((), ()))
    for x in range(4):
        tokens, cotangent, weight = [], [], []
        others[x].wait()
        copies[2 * x].wait()
        copies[2 * x + 1].wait()
        for values_ref, which in ((own_ref, core), (other_ref, 1 - core)):
            for y in range(2):
                tokens.append(values_ref[x, :, y, 0].reshape(2 * ROWS, FEATURES))
                cotangent.append(values_ref[x, :, y, 1].reshape(2 * ROWS, FEATURES))
                weight += [weight_ref[x, y, 2 * which + z] for z in range(2)]
        tokens, cotangent = jnp.concatenate(tokens, 1), jnp.concatenate(cotangent, 1)
        weight = jnp.concatenate(weight, 1)
        streams += lax.dot_general(weight[:BACK], tokens, contract, preferred_element_type=F32)
        grad_gate += lax.dot_general(weight[BACK:], cotangent, contract, preferred_element_type=F32)
    streams = streams.astype(BF16)
    streams_ref[...] = streams
    gate_ref[...] = grad_gate
    query, key, value = (streams[i * HALF : (i + 1) * HALF].astype(F32) for i in range(3))
    product_ref[...] = (key * value).astype(BF16)
    mixed_ref[...] = (grad_gate * query).astype(BF16)
    for copy in copies[8:]:
        copy.wait()


def forward(place, own, other, weight):
    vmem = pl.BlockSpec(memory_space=pltpu.VMEM)
    shape = lambda height, kind: jax.ShapeDtypeStruct((height, 2 * ROWS), kind)
    return pl.pallas_call(
        forward_kernel,
        out_shape=(
            shape(BACK, BF16),
            shape(HALF, F32),
            shape(HALF, BF16),
            shape(HALF, BF16),
            jax.ShapeDtypeStruct((2, 2, 2, 2, 2, STREAMS, ROWS), BF16),
        ),
        in_specs=[
            pl.BlockSpec(memory_space=pltpu.SMEM),
            vmem,
            pl.BlockSpec(memory_space=pl.ANY),
            pl.BlockSpec(memory_space=pl.ANY),
        ],
        out_specs=(vmem,) * 5,
        scratch_shapes=[
            pltpu.VMEM((4, 2, 4, STREAMS, ROWS), BF16),
            pltpu.VMEM((4, 2, 2, 2, ROWS, FEATURES), BF16),
            pltpu.SemaphoreType.DMA((20,)),
        ],
        compiler_params=pltpu.CompilerParams(vmem_limit_bytes=VMEM_FORWARD),
        cost_estimate=pl.CostEstimate(flops=1 << 30, bytes_accessed=9 << 20, transcendentals=0),
    )(place, own, other, weight)


def filtered(left, right, band):
    segments = [
        jnp.concatenate([left[s], right[s]], 1) for s in range(2)
    ]
    result = jnp.dot(jnp.concatenate(segments, 0), band, preferred_element_type=F32)
    return [
        jnp.concatenate(
            [
                result[s * HALF + g * GROUP : s * HALF + (g + 1) * GROUP, g * ROWS : (g + 1) * ROWS]
                for g in range(GROUPS)
            ],
            0,
        )
        for s in range(2)
    ]


def middle_kernel(
    place_ref, band_ref, streams_ref, gate_ref, product_ref, mixed_ref, before_ref, after_ref, terms_ref
):
    first = place_ref[1] == 0
    last = place_ref[1] == 15
    lanes = [slice(s * ROWS, (s + 1) * ROWS) for s in range(2)]
    product, mixed, before, after = (
        [ref[:, lanes[s]] for s in range(2)] for ref in (product_ref, mixed_ref, before_ref, after_ref)
    )
    zero = jnp.zeros_like(before[0])
    earlier = [jnp.where(first, zero, before[0]), jnp.where(first, before[0], before[1])]
    later = [jnp.where(last, after[1], after[0]), jnp.where(last, zero, after[1])]
    conv = filtered(earlier, product, band_ref[:, : GROUPS * ROWS])
    back = filtered(mixed, later, band_ref[:, GROUPS * ROWS :])
    for s in range(2):
        query, key, value = (
            streams_ref[i * HALF : (i + 1) * HALF, lanes[s]].astype(F32) for i in range(3)
        )
        terms = (gate_ref[:, lanes[s]] * conv[s], back[s] * value, back[s] * key, query * conv[s])
        for i in range(4):
            terms_ref[lanes[s], i * HALF : (i + 1) * HALF] = terms[i].T.astype(BF16)


def on_chip(kernel, out_shape, operands, flops):
    smem, vmem = pl.BlockSpec(memory_space=pltpu.SMEM), pl.BlockSpec(memory_space=pltpu.VMEM)
    return pl.pallas_call(
        kernel,
        out_shape=out_shape,
        in_specs=[smem] + [vmem] * (len(operands) - 1),
        out_specs=jax.tree.map(lambda _: vmem, out_shape),
        compiler_params=pltpu.CompilerParams(vmem_limit_bytes=VMEM_SMALL),
        cost_estimate=pl.CostEstimate(flops=flops, bytes_accessed=1 << 20, transcendentals=0),
    )(*operands)


def middle(*operands):
    return on_chip(middle_kernel, jax.ShapeDtypeStruct((2 * ROWS, STREAMS), BF16), operands, 1 << 28)


def backward_kernel(place_ref, terms_ref, weight_ref, out_ref):
    for part, cols in enumerate((slice(BACK, STREAMS), slice(0, BACK))):
        terms = jnp.concatenate([terms_ref[core, :, cols] for core in range(2)], 1)
        for y in range(2):
            for x in range(4):
                weight = [
                    jnp.concatenate([weight_ref[x % 2, y, x // 2, z, core, cols] for z in range(2)], 1)
                    for core in range(2)
                ]
                result = jnp.dot(terms, jnp.concatenate(weight, 0), preferred_element_type=F32)
                for h in range(2):
                    out_ref[4 * y + x, h, part] = result[h * ROWS : (h + 1) * ROWS].astype(BF16)


def backward(*operands):
    shape = (8, 2, 2, ROWS, FEATURES)
    return on_chip(backward_kernel, jax.ShapeDtypeStruct(shape, BF16), operands, 1 << 30)


def combine_kernel(place_ref, parts_ref, mine_ref, theirs_ref):
    half = place_ref[3]
    for part in range(2):
        mine, theirs = 0.0, 0.0
        for source in range(8):
            mine += parts_ref[source, half, part].astype(F32)
            theirs += parts_ref[source, 1 - half, part].astype(F32)
        mine_ref[part] = mine
        theirs_ref[part] = theirs.astype(BF16)


def combine(*operands):
    shape = (2, ROWS, FEATURES)
    out_shape = (jax.ShapeDtypeStruct(shape, F32), jax.ShapeDtypeStruct(shape, BF16))
    return on_chip(combine_kernel, out_shape, operands, 1 << 20)


def pack_kernel(in_ref, out_ref, packed_ref):
    for h in range(2):
        chans = slice(h * HALF, (h + 1) * HALF)
        streams = [in_ref[stream, :, chans].astype(F32).T.astype(BF16) for stream in range(3)]
        for l in range(2):
            for stream in range(3):
                packed_ref[2 * h + l, stream * HALF : (stream + 1) * HALF] = streams[stream]
            packed_ref[2 * h + l, BACK:] = out_ref[chans]


def packed(in_weight, out_weight):
    vmem = pl.BlockSpec(memory_space=pltpu.VMEM)
    return pl.pallas_call(
        pack_kernel,
        out_shape=jax.ShapeDtypeStruct((4, STREAMS, ROWS), BF16),
        in_specs=[vmem] * 2,
        out_specs=vmem,
    )(in_weight, out_weight)


def finish_kernel(place_ref, mine_ref, theirs_ref, mixed_ref, grad_ref):
    for part, ref in enumerate((mixed_ref, grad_ref)):
        ref[...] = (mine_ref[part] + theirs_ref[part].astype(F32)).astype(BF16)


def finish(*operands):
    return on_chip(finish_kernel, (jax.ShapeDtypeStruct((ROWS, FEATURES), BF16),) * 2, operands, 1 << 16)


def swapped(value, axes):
    return lax.all_to_all(value, axes, 0, 0, tiled=True)


def gathered(value, axes, count):
    return swapped(jnp.broadcast_to(value[None], (count,) + value.shape), axes)


def local(tokens, in_weight, out_weight, mr_filter, cotangent):
    half, core = lax.axis_index("h"), lax.axis_index("core")
    position = lax.axis_index(("l", "z"))
    place = jnp.stack([core, position, lax.axis_index("x"), half]).astype(jnp.int32)

    weight = swapped(packed(in_weight, out_weight), ("h", "l"))
    weight, tokens, cotangent = lax.optimization_barrier((weight, tokens, cotangent))
    values = jnp.stack([tokens, cotangent], 0)
    weight = lax.all_gather(weight, ("z", "core"), axis=0).reshape(8, 2, 4, STREAMS, ROWS)

    band = bands(lax.dynamic_slice_in_dim(mr_filter, half * GROUPS, GROUPS, 0))
    values = gathered(values, ("h", "ylo"), 4)
    values = gathered(values, "x", 4).reshape(4, 2, 2, 2, ROWS, FEATURES)
    values, band = lax.optimization_barrier((values, band))
    cross = [(0, 1), (1, 0)]
    other = lax.ppermute(values, "core", cross)

    streams, gate, product, mixed, weight = forward(place, values, other, weight)
    ring = [(n, (n + 1) % 16) for n in range(16)]
    before = lax.ppermute(product, ("l", "z"), ring)
    after = lax.ppermute(mixed, ("l", "z"), [(b, a) for a, b in ring])

    terms = middle(place, band, streams, gate, product, mixed, before, after)
    terms = lax.all_gather(terms, "core", axis=0)

    parts = swapped(backward(place, terms, weight), ("ylo", "x"))
    mine, theirs = combine(place, parts)
    return finish(place, mine, lax.ppermute(theirs, "h", cross))


def solution(mesh):
    fine = Mesh(mesh.devices.reshape(SIZES), AXES)
    ctx, tp = AXES[:3], AXES[3:]
    return jax.shard_map(
        local,
        mesh=fine,
        in_specs=(P(ctx, tp), P(None, ctx, tp), P(tp, ctx), P(tp, None), P(ctx, tp)),
        out_specs=(P(ctx, tp), P(ctx, tp)),
        check_vma=False,
    )
```

```python
import jax
import jax.numpy as jnp
from jax import lax
from jax.experimental import pallas as pl
from jax.experimental.pallas import tpu as pltpu
from jax.sharding import Mesh, PartitionSpec as P

AXES = ("h", "l", "z", "ylo", "x", "core")
SIZES = (2, 2, 8, 2, 4, 2)
ROWS = 128
HALF = 128
TAPS = 128
GROUP = 16
GROUPS = HALF // GROUP
FEATURES = 256
STREAMS = 4 * HALF
BACK = 3 * HALF
BF16 = jnp.bfloat16
F32 = jnp.float32
VMEM_FORWARD = 40 << 20
VMEM_SMALL = 16 << 20


def bands_kernel(base_ref, band_ref):
    for row in range(2 * GROUPS):
        spread = jnp.broadcast_to(base_ref[row : row + 1, :], (2 * ROWS, 2 * ROWS))
        rolled = pltpu.roll(spread, 0, 1, stride=1, stride_axis=0)
        band_ref[:, row * ROWS : (row + 1) * ROWS] = rolled[:, :ROWS].astype(BF16)


def bands(filters):
    zeros = jnp.zeros((GROUPS, TAPS), filters.dtype)
    causal = jnp.concatenate([zeros, filters], 1)
    anticausal = jnp.concatenate([filters[:, :1], zeros, filters[:, :0:-1]], 1)
    return pl.pallas_call(
        bands_kernel,
        out_shape=jax.ShapeDtypeStruct((2 * ROWS, 2 * GROUPS * ROWS), BF16),
        in_specs=[pl.BlockSpec(memory_space=pltpu.VMEM)],
        out_specs=pl.BlockSpec(memory_space=pltpu.VMEM),
        compiler_params=pltpu.CompilerParams(vmem_limit_bytes=VMEM_SMALL),
    )(jnp.concatenate([causal, anticausal], 0))


def forward_kernel(
    place_ref,
    own_ref,
    other_hbm,
    weight_hbm,
    streams_ref,
    gate_ref,
    product_ref,
    mixed_ref,
    back_ref,
    weight_ref,
    other_ref,
    arrived,
):
    core = place_ref[0]
    copies = []
    others = [pltpu.make_async_copy(other_hbm.at[x], other_ref.at[x], arrived.at[16 + x]) for x in range(4)]
    for x in range(4):
        for y in range(2):
            copies.append(
                pltpu.make_async_copy(
                    weight_hbm.at[pl.ds((x % 2) * 4 + 2 * (1 - core), 2), core, 2 * y + x // 2],
                    weight_ref.at[x, y],
                    arrived.at[2 * x + y],
                )
            )
    for x in range(4):
        for y in range(2):
            copies.append(
                pltpu.make_async_copy(
                    weight_hbm.at[pl.ds((x % 2) * 4 + 2 * core, 2), :, 2 * y + x // 2],
                    back_ref.at[x % 2, y, x // 2],
                    arrived.at[8 + 2 * x + y],
                )
            )
    for copy in copies[8:]:
        copy.start()
    for x in range(4):
        others[x].start()
        copies[2 * x].start()
        copies[2 * x + 1].start()
    streams, grad_gate = 0.0, 0.0
    contract = (((1,), (1,)), ((), ()))
    for values_ref in (own_ref, other_ref):
        for x in range(4):
            tokens, cotangent, weight = [], [], []
            if values_ref is other_ref:
                others[x].wait()
            for y in range(2):
                if values_ref is own_ref:
                    copies[8 + 2 * x + y].wait()
                    weight += [back_ref[x % 2, y, x // 2, z, core] for z in range(2)]
                else:
                    copies[2 * x + y].wait()
                    weight += [weight_ref[x, y, z] for z in range(2)]
                tokens.append(values_ref[x, :, y, 0].reshape(2 * ROWS, FEATURES))
                cotangent.append(values_ref[x, :, y, 1].reshape(2 * ROWS, FEATURES))
            tokens, cotangent = jnp.concatenate(tokens, 1), jnp.concatenate(cotangent, 1)
            weight = jnp.concatenate(weight, 1)
            streams += lax.dot_general(weight[:BACK], tokens, contract, preferred_element_type=F32)
            grad_gate += lax.dot_general(weight[BACK:], cotangent, contract, preferred_element_type=F32)
    streams = streams.astype(BF16)
    streams_ref[...] = streams
    gate_ref[...] = grad_gate
    query, key, value = (streams[i * HALF : (i + 1) * HALF].astype(F32) for i in range(3))
    product_ref[...] = (key * value).astype(BF16)
    mixed_ref[...] = (grad_gate * query).astype(BF16)


def forward(place, own, other, weight):
    vmem = pl.BlockSpec(memory_space=pltpu.VMEM)
    shape = lambda height, kind: jax.ShapeDtypeStruct((height, 2 * ROWS), kind)
    return pl.pallas_call(
        forward_kernel,
        out_shape=(
            shape(BACK, BF16),
            shape(HALF, F32),
            shape(HALF, BF16),
            shape(HALF, BF16),
            jax.ShapeDtypeStruct((2, 2, 2, 2, 2, STREAMS, ROWS), BF16),
        ),
        in_specs=[
            pl.BlockSpec(memory_space=pltpu.SMEM),
            vmem,
            pl.BlockSpec(memory_space=pl.ANY),
            pl.BlockSpec(memory_space=pl.ANY),
        ],
        out_specs=(vmem,) * 5,
        scratch_shapes=[
            pltpu.VMEM((4, 2, 2, STREAMS, ROWS), BF16),
            pltpu.VMEM((4, 2, 2, 2, ROWS, FEATURES), BF16),
            pltpu.SemaphoreType.DMA((20,)),
        ],
        compiler_params=pltpu.CompilerParams(vmem_limit_bytes=VMEM_FORWARD),
        cost_estimate=pl.CostEstimate(flops=1 << 30, bytes_accessed=9 << 20, transcendentals=0),
    )(place, own, other, weight)


def filtered(left, right, band):
    segments = [
        jnp.concatenate([left[s], right[s]], 1) for s in range(2)
    ]
    result = jnp.dot(jnp.concatenate(segments, 0), band, preferred_element_type=F32)
    return [
        jnp.concatenate(
            [
                result[s * HALF + g * GROUP : s * HALF + (g + 1) * GROUP, g * ROWS : (g + 1) * ROWS]
                for g in range(GROUPS)
            ],
            0,
        )
        for s in range(2)
    ]


def middle_kernel(
    place_ref, band_ref, streams_ref, gate_ref, product_ref, mixed_ref, before_ref, after_ref, terms_ref
):
    first = place_ref[1] == 0
    last = place_ref[1] == 15
    lanes = [slice(s * ROWS, (s + 1) * ROWS) for s in range(2)]
    product, mixed, before, after = (
        [ref[:, lanes[s]] for s in range(2)] for ref in (product_ref, mixed_ref, before_ref, after_ref)
    )
    zero = jnp.zeros_like(before[0])
    earlier = [jnp.where(first, zero, before[0]), jnp.where(first, before[0], before[1])]
    later = [jnp.where(last, after[1], after[0]), jnp.where(last, zero, after[1])]
    conv = filtered(earlier, product, band_ref[:, : GROUPS * ROWS])
    back = filtered(mixed, later, band_ref[:, GROUPS * ROWS :])
    for s in range(2):
        query, key, value = (
            streams_ref[i * HALF : (i + 1) * HALF, lanes[s]].astype(F32) for i in range(3)
        )
        terms = (gate_ref[:, lanes[s]] * conv[s], back[s] * value, back[s] * key, query * conv[s])
        for i in range(4):
            terms_ref[lanes[s], i * HALF : (i + 1) * HALF] = terms[i].T.astype(BF16)


def on_chip(kernel, out_shape, operands, flops):
    smem, vmem = pl.BlockSpec(memory_space=pltpu.SMEM), pl.BlockSpec(memory_space=pltpu.VMEM)
    return pl.pallas_call(
        kernel,
        out_shape=out_shape,
        in_specs=[smem] + [vmem] * (len(operands) - 1),
        out_specs=jax.tree.map(lambda _: vmem, out_shape),
        compiler_params=pltpu.CompilerParams(vmem_limit_bytes=VMEM_SMALL),
        cost_estimate=pl.CostEstimate(flops=flops, bytes_accessed=1 << 20, transcendentals=0),
    )(*operands)


def middle(*operands):
    return on_chip(middle_kernel, jax.ShapeDtypeStruct((2 * ROWS, STREAMS), BF16), operands, 1 << 28)


def backward_kernel(place_ref, terms_ref, weight_ref, out_ref):
    for part, cols in enumerate((slice(BACK, STREAMS), slice(0, BACK))):
        terms = jnp.concatenate([terms_ref[core, :, cols] for core in range(2)], 1)
        for y in range(2):
            for x in range(4):
                weight = [
                    jnp.concatenate([weight_ref[x % 2, y, x // 2, z, core, cols] for z in range(2)], 1)
                    for core in range(2)
                ]
                result = jnp.dot(terms, jnp.concatenate(weight, 0), preferred_element_type=F32)
                for h in range(2):
                    out_ref[4 * y + x, h, part] = result[h * ROWS : (h + 1) * ROWS].astype(BF16)


def backward(*operands):
    shape = (8, 2, 2, ROWS, FEATURES)
    return on_chip(backward_kernel, jax.ShapeDtypeStruct(shape, BF16), operands, 1 << 30)


def combine_kernel(place_ref, parts_ref, mine_ref, theirs_ref):
    half = place_ref[3]
    for part in range(2):
        mine, theirs = 0.0, 0.0
        for source in range(8):
            mine += parts_ref[source, half, part].astype(F32)
            theirs += parts_ref[source, 1 - half, part].astype(F32)
        mine_ref[part] = mine
        theirs_ref[part] = theirs.astype(BF16)


def combine(*operands):
    shape = (2, ROWS, FEATURES)
    out_shape = (jax.ShapeDtypeStruct(shape, F32), jax.ShapeDtypeStruct(shape, BF16))
    return on_chip(combine_kernel, out_shape, operands, 1 << 20)


def pack_kernel(in_ref, out_ref, packed_ref):
    for h in range(2):
        chans = slice(h * HALF, (h + 1) * HALF)
        streams = [in_ref[stream, :, chans].astype(F32).T.astype(BF16) for stream in range(3)]
        for l in range(2):
            for stream in range(3):
                packed_ref[2 * h + l, stream * HALF : (stream + 1) * HALF] = streams[stream]
            packed_ref[2 * h + l, BACK:] = out_ref[chans]


def packed(in_weight, out_weight):
    vmem = pl.BlockSpec(memory_space=pltpu.VMEM)
    return pl.pallas_call(
        pack_kernel,
        out_shape=jax.ShapeDtypeStruct((4, STREAMS, ROWS), BF16),
        in_specs=[vmem] * 2,
        out_specs=vmem,
    )(in_weight, out_weight)


def finish_kernel(place_ref, mine_ref, theirs_ref, mixed_ref, grad_ref):
    for part, ref in enumerate((mixed_ref, grad_ref)):
        ref[...] = (mine_ref[part] + theirs_ref[part].astype(F32)).astype(BF16)


def finish(*operands):
    return on_chip(finish_kernel, (jax.ShapeDtypeStruct((ROWS, FEATURES), BF16),) * 2, operands, 1 << 16)


def swapped(value, axes):
    return lax.all_to_all(value, axes, 0, 0, tiled=True)


def gathered(value, axes, count):
    return swapped(jnp.broadcast_to(value[None], (count,) + value.shape), axes)


def local(tokens, in_weight, out_weight, mr_filter, cotangent):
    half, core = lax.axis_index("h"), lax.axis_index("core")
    position = lax.axis_index(("l", "z"))
    place = jnp.stack([core, position, lax.axis_index("x"), half]).astype(jnp.int32)

    weight = swapped(packed(in_weight, out_weight), ("h", "l"))
    weight, tokens, cotangent = lax.optimization_barrier((weight, tokens, cotangent))
    values = jnp.stack([tokens, cotangent], 0)
    weight = lax.all_gather(weight, ("z", "core"), axis=0).reshape(8, 2, 4, STREAMS, ROWS)

    band = bands(lax.dynamic_slice_in_dim(mr_filter, half * GROUPS, GROUPS, 0))
    values = gathered(values, ("h", "ylo"), 4)
    values = gathered(values, "x", 4).reshape(4, 2, 2, 2, ROWS, FEATURES)
    values, band = lax.optimization_barrier((values, band))
    cross = [(0, 1), (1, 0)]
    other = lax.ppermute(values, "core", cross)

    streams, gate, product, mixed, weight = forward(place, values, other, weight)
    ring = [(n, (n + 1) % 16) for n in range(16)]
    before = lax.ppermute(product, ("l", "z"), ring)
    after = lax.ppermute(mixed, ("l", "z"), [(b, a) for a, b in ring])

    terms = middle(place, band, streams, gate, product, mixed, before, after)
    terms = lax.all_gather(terms, "core", axis=0)

    parts = swapped(backward(place, terms, weight), ("ylo", "x"))
    mine, theirs = combine(place, parts)
    return finish(place, mine, lax.ppermute(theirs, "h", cross))


def solution(mesh):
    fine = Mesh(mesh.devices.reshape(SIZES), AXES)
    ctx, tp = AXES[:3], AXES[3:]
    return jax.shard_map(
        local,
        mesh=fine,
        in_specs=(P(ctx, tp), P(None, ctx, tp), P(tp, ctx), P(tp, None), P(ctx, tp)),
        out_specs=(P(ctx, tp), P(ctx, tp)),
        check_vma=False,
    )
```

```python
import jax
import jax.numpy as jnp
from jax import lax
from jax.experimental import pallas as pl
from jax.experimental.pallas import tpu as pltpu
from jax.sharding import Mesh, PartitionSpec as P

AXES = ("h", "l", "z", "ylo", "x", "core")
SIZES = (2, 2, 8, 2, 4, 2)
ROWS = 128
HALF = 128
TAPS = 128
GROUP = 16
GROUPS = HALF // GROUP
FEATURES = 256
STREAMS = 4 * HALF
BACK = 3 * HALF
BF16 = jnp.bfloat16
F32 = jnp.float32
VMEM_FORWARD = 40 << 20
VMEM_SMALL = 16 << 20


def bands_kernel(base_ref, band_ref):
    for row in range(2 * GROUPS):
        spread = jnp.broadcast_to(base_ref[row : row + 1, :], (2 * ROWS, 2 * ROWS))
        rolled = pltpu.roll(spread, 0, 1, stride=1, stride_axis=0)
        band_ref[:, row * ROWS : (row + 1) * ROWS] = rolled[:, :ROWS].astype(BF16)


def bands(filters):
    zeros = jnp.zeros((GROUPS, TAPS), filters.dtype)
    causal = jnp.concatenate([zeros, filters], 1)
    anticausal = jnp.concatenate([filters[:, :1], zeros, filters[:, :0:-1]], 1)
    return pl.pallas_call(
        bands_kernel,
        out_shape=jax.ShapeDtypeStruct((2 * ROWS, 2 * GROUPS * ROWS), BF16),
        in_specs=[pl.BlockSpec(memory_space=pltpu.VMEM)],
        out_specs=pl.BlockSpec(memory_space=pltpu.VMEM),
        compiler_params=pltpu.CompilerParams(vmem_limit_bytes=VMEM_SMALL),
    )(jnp.concatenate([causal, anticausal], 0))


def forward_kernel(
    place_ref,
    own_ref,
    other_hbm,
    weight_hbm,
    streams_ref,
    gate_ref,
    product_ref,
    mixed_ref,
    back_ref,
    weight_ref,
    other_ref,
    arrived,
):
    core = place_ref[0]
    copies = []
    others = [pltpu.make_async_copy(other_hbm.at[x], other_ref.at[x], arrived.at[16 + x]) for x in range(4)]
    for x in range(4):
        for y in range(2):
            copies.append(
                pltpu.make_async_copy(
                    weight_hbm.at[pl.ds((x % 2) * 4 + 2 * (1 - core), 2), core, 2 * y + x // 2],
                    weight_ref.at[x, y],
                    arrived.at[2 * x + y],
                )
            )
    for x in range(4):
        for y in range(2):
            copies.append(
                pltpu.make_async_copy(
                    weight_hbm.at[pl.ds((x % 2) * 4 + 2 * core, 2), :, 2 * y + x // 2],
                    back_ref.at[x % 2, y, x // 2],
                    arrived.at[8 + 2 * x + y],
                )
            )
    for copy in copies[8:]:
        copy.start()
    for x in range(4):
        others[x].start()
        copies[2 * x].start()
        copies[2 * x + 1].start()
    streams, grad_gate = 0.0, 0.0
    contract = (((1,), (1,)), ((), ()))
    for values_ref in (own_ref, other_ref):
        for x in range(4):
            tokens, cotangent, weight = [], [], []
            if values_ref is other_ref:
                others[x].wait()
            for y in range(2):
                if values_ref is own_ref:
                    copies[8 + 2 * x + y].wait()
                    weight += [back_ref[x % 2, y, x // 2, z, core] for z in range(2)]
                else:
                    copies[2 * x + y].wait()
                    weight += [weight_ref[x, y, z] for z in range(2)]
                tokens.append(values_ref[x, :, y, 0].reshape(2 * ROWS, FEATURES))
                cotangent.append(values_ref[x, :, y, 1].reshape(2 * ROWS, FEATURES))
            tokens, cotangent = jnp.concatenate(tokens, 1), jnp.concatenate(cotangent, 1)
            weight = jnp.concatenate(weight, 1)
            streams += lax.dot_general(weight[:BACK], tokens, contract, preferred_element_type=F32)
            grad_gate += lax.dot_general(weight[BACK:], cotangent, contract, preferred_element_type=F32)
    streams = streams.astype(BF16)
    streams_ref[...] = streams
    gate_ref[...] = grad_gate
    query, key, value = (streams[i * HALF : (i + 1) * HALF].astype(F32) for i in range(3))
    product_ref[...] = (key * value).astype(BF16)
    mixed_ref[...] = (grad_gate * query).astype(BF16)


def forward(place, own, other, weight):
    vmem = pl.BlockSpec(memory_space=pltpu.VMEM)
    shape = lambda height, kind: jax.ShapeDtypeStruct((height, 2 * ROWS), kind)
    return pl.pallas_call(
        forward_kernel,
        out_shape=(
            shape(BACK, BF16),
            shape(HALF, F32),
            shape(HALF, BF16),
            shape(HALF, BF16),
            jax.ShapeDtypeStruct((2, 2, 2, 2, 2, STREAMS, ROWS), BF16),
        ),
        in_specs=[
            pl.BlockSpec(memory_space=pltpu.SMEM),
            vmem,
            pl.BlockSpec(memory_space=pl.ANY),
            pl.BlockSpec(memory_space=pl.ANY),
        ],
        out_specs=(vmem,) * 5,
        scratch_shapes=[
            pltpu.VMEM((4, 2, 2, STREAMS, ROWS), BF16),
            pltpu.VMEM((4, 2, 2, 2, ROWS, FEATURES), BF16),
            pltpu.SemaphoreType.DMA((20,)),
        ],
        compiler_params=pltpu.CompilerParams(vmem_limit_bytes=VMEM_FORWARD),
        cost_estimate=pl.CostEstimate(flops=1 << 30, bytes_accessed=9 << 20, transcendentals=0),
    )(place, own, other, weight)


def filtered(left, right, band):
    segments = [
        jnp.concatenate([left[s], right[s]], 1) for s in range(2)
    ]
    result = jnp.dot(jnp.concatenate(segments, 0), band, preferred_element_type=F32)
    return [
        jnp.concatenate(
            [
                result[s * HALF + g * GROUP : s * HALF + (g + 1) * GROUP, g * ROWS : (g + 1) * ROWS]
                for g in range(GROUPS)
            ],
            0,
        )
        for s in range(2)
    ]


def middle_kernel(
    place_ref, band_ref, streams_ref, gate_ref, product_ref, mixed_ref, before_ref, after_ref, terms_ref
):
    first = place_ref[1] == 0
    last = place_ref[1] == 15
    lanes = [slice(s * ROWS, (s + 1) * ROWS) for s in range(2)]
    product, mixed, before, after = (
        [ref[:, lanes[s]] for s in range(2)] for ref in (product_ref, mixed_ref, before_ref, after_ref)
    )
    zero = jnp.zeros_like(before[0])
    earlier = [jnp.where(first, zero, before[0]), jnp.where(first, before[0], before[1])]
    later = [jnp.where(last, after[1], after[0]), jnp.where(last, zero, after[1])]
    conv = filtered(earlier, product, band_ref[:, : GROUPS * ROWS])
    back = filtered(mixed, later, band_ref[:, GROUPS * ROWS :])
    for s in range(2):
        query, key, value = (
            streams_ref[i * HALF : (i + 1) * HALF, lanes[s]].astype(F32) for i in range(3)
        )
        terms = (gate_ref[:, lanes[s]] * conv[s], back[s] * value, back[s] * key, query * conv[s])
        for i in range(4):
            terms_ref[lanes[s], i * HALF : (i + 1) * HALF] = terms[i].T.astype(BF16)


def on_chip(kernel, out_shape, operands, flops):
    smem, vmem = pl.BlockSpec(memory_space=pltpu.SMEM), pl.BlockSpec(memory_space=pltpu.VMEM)
    return pl.pallas_call(
        kernel,
        out_shape=out_shape,
        in_specs=[smem] + [vmem] * (len(operands) - 1),
        out_specs=jax.tree.map(lambda _: vmem, out_shape),
        compiler_params=pltpu.CompilerParams(vmem_limit_bytes=VMEM_SMALL),
        cost_estimate=pl.CostEstimate(flops=flops, bytes_accessed=1 << 20, transcendentals=0),
    )(*operands)


def middle(*operands):
    return on_chip(middle_kernel, jax.ShapeDtypeStruct((2 * ROWS, STREAMS), BF16), operands, 1 << 28)


def backward_kernel(place_ref, terms_ref, weight_ref, out_ref):
    for part, cols in enumerate((slice(BACK, STREAMS), slice(0, BACK))):
        terms = jnp.concatenate([terms_ref[core, :, cols] for core in range(2)], 1)
        for y in range(2):
            for x in range(4):
                weight = [
                    jnp.concatenate([weight_ref[x % 2, y, x // 2, z, core, cols] for z in range(2)], 1)
                    for core in range(2)
                ]
                result = jnp.dot(terms, jnp.concatenate(weight, 0), preferred_element_type=F32)
                for h in range(2):
                    out_ref[4 * y + x, h, part] = result[h * ROWS : (h + 1) * ROWS].astype(BF16)


def backward(*operands):
    shape = (8, 2, 2, ROWS, FEATURES)
    return on_chip(backward_kernel, jax.ShapeDtypeStruct(shape, BF16), operands, 1 << 30)


def combine_kernel(place_ref, parts_ref, mine_ref, theirs_ref):
    half = place_ref[3]
    for part in range(2):
        mine, theirs = 0.0, 0.0
        for source in range(8):
            mine += parts_ref[source, half, part].astype(F32)
            theirs += parts_ref[source, 1 - half, part].astype(F32)
        mine_ref[part] = mine
        theirs_ref[part] = theirs.astype(BF16)


def combine(*operands):
    shape = (2, ROWS, FEATURES)
    out_shape = (jax.ShapeDtypeStruct(shape, F32), jax.ShapeDtypeStruct(shape, BF16))
    return on_chip(combine_kernel, out_shape, operands, 1 << 20)


def pack_kernel(in_hbm, out_hbm, packed_ref, in_ref, out_ref, arrived):
    copies = [pltpu.make_async_copy(in_hbm.at[i], in_ref.at[i], arrived.at[i]) for i in range(3)]
    copies.append(pltpu.make_async_copy(out_hbm, out_ref, arrived.at[3]))
    for copy in copies:
        copy.start()
    for stream in range(4):
        copies[stream].wait()
        rows = slice(stream * HALF, (stream + 1) * HALF)
        for h in range(2):
            chans = slice(h * HALF, (h + 1) * HALF)
            piece = out_ref[chans] if stream == 3 else in_ref[stream, :, chans].astype(F32).T.astype(BF16)
            for l in range(2):
                packed_ref[2 * h + l, rows] = piece


def packed(in_weight, out_weight):
    return pl.pallas_call(
        pack_kernel,
        out_shape=jax.ShapeDtypeStruct((4, STREAMS, ROWS), BF16),
        in_specs=[pl.BlockSpec(memory_space=pl.ANY)] * 2,
        out_specs=pl.BlockSpec(memory_space=pltpu.VMEM),
        scratch_shapes=[
            pltpu.VMEM((3, ROWS, FEATURES), BF16),
            pltpu.VMEM((FEATURES, ROWS), BF16),
            pltpu.SemaphoreType.DMA((4,)),
        ],
        compiler_params=pltpu.CompilerParams(vmem_limit_bytes=VMEM_SMALL),
    )(in_weight, out_weight)


def finish_kernel(place_ref, mine_ref, theirs_ref, mixed_ref, grad_ref):
    for part, ref in enumerate((mixed_ref, grad_ref)):
        ref[...] = (mine_ref[part] + theirs_ref[part].astype(F32)).astype(BF16)


def finish(*operands):
    return on_chip(finish_kernel, (jax.ShapeDtypeStruct((ROWS, FEATURES), BF16),) * 2, operands, 1 << 16)


def swapped(value, axes):
    return lax.all_to_all(value, axes, 0, 0, tiled=True)


def gathered(value, axes, count):
    return swapped(jnp.broadcast_to(value[None], (count,) + value.shape), axes)


def local(tokens, in_weight, out_weight, mr_filter, cotangent):
    half, core = lax.axis_index("h"), lax.axis_index("core")
    position = lax.axis_index(("l", "z"))
    place = jnp.stack([core, position, lax.axis_index("x"), half]).astype(jnp.int32)

    weight = swapped(packed(in_weight, out_weight), ("h", "l"))
    weight, tokens, cotangent = lax.optimization_barrier((weight, tokens, cotangent))
    values = jnp.stack([tokens, cotangent], 0)
    weight = lax.all_gather(weight, ("z", "core"), axis=0).reshape(8, 2, 4, STREAMS, ROWS)

    band = bands(lax.dynamic_slice_in_dim(mr_filter, half * GROUPS, GROUPS, 0))
    values = gathered(values, ("h", "ylo"), 4)
    values = gathered(values, "x", 4).reshape(4, 2, 2, 2, ROWS, FEATURES)
    values, band = lax.optimization_barrier((values, band))
    cross = [(0, 1), (1, 0)]
    other = lax.ppermute(values, "core", cross)

    streams, gate, product, mixed, weight = forward(place, values, other, weight)
    ring = [(n, (n + 1) % 16) for n in range(16)]
    before = lax.ppermute(product, ("l", "z"), ring)
    after = lax.ppermute(mixed, ("l", "z"), [(b, a) for a, b in ring])

    terms = middle(place, band, streams, gate, product, mixed, before, after)
    terms = lax.all_gather(terms, "core", axis=0)

    parts = swapped(backward(place, terms, weight), ("ylo", "x"))
    mine, theirs = combine(place, parts)
    return finish(place, mine, lax.ppermute(theirs, "h", cross))


def solution(mesh):
    fine = Mesh(mesh.devices.reshape(SIZES), AXES)
    ctx, tp = AXES[:3], AXES[3:]
    return jax.shard_map(
        local,
        mesh=fine,
        in_specs=(P(ctx, tp), P(None, ctx, tp), P(tp, ctx), P(tp, None), P(ctx, tp)),
        out_specs=(P(ctx, tp), P(ctx, tp)),
        check_vma=False,
    )
```

```python
import jax
import jax.numpy as jnp
from jax import lax
from jax.experimental import pallas as pl
from jax.experimental.pallas import tpu as pltpu
from jax.sharding import Mesh, PartitionSpec as P

AXES = ("h", "l", "z", "ylo", "x", "core")
SIZES = (2, 2, 8, 2, 4, 2)
ROWS = 128
HALF = 128
TAPS = 128
GROUP = 16
GROUPS = HALF // GROUP
FEATURES = 256
STREAMS = 4 * HALF
BACK = 3 * HALF
BF16 = jnp.bfloat16
F32 = jnp.float32
VMEM_FORWARD = 40 << 20
VMEM_SMALL = 16 << 20


def bands_kernel(base_ref, band_ref):
    for row in range(2 * GROUPS):
        spread = jnp.broadcast_to(base_ref[row : row + 1, :], (2 * ROWS, 2 * ROWS))
        rolled = pltpu.roll(spread, 0, 1, stride=1, stride_axis=0)
        band_ref[:, row * ROWS : (row + 1) * ROWS] = rolled[:, :ROWS].astype(BF16)


def bands(filters):
    zeros = jnp.zeros((GROUPS, TAPS), filters.dtype)
    causal = jnp.concatenate([zeros, filters], 1)
    anticausal = jnp.concatenate([filters[:, :1], zeros, filters[:, :0:-1]], 1)
    return pl.pallas_call(
        bands_kernel,
        out_shape=jax.ShapeDtypeStruct((2 * ROWS, 2 * GROUPS * ROWS), BF16),
        in_specs=[pl.BlockSpec(memory_space=pltpu.VMEM)],
        out_specs=pl.BlockSpec(memory_space=pltpu.VMEM),
        compiler_params=pltpu.CompilerParams(vmem_limit_bytes=VMEM_SMALL),
    )(jnp.concatenate([causal, anticausal], 0))


def forward_kernel(
    place_ref,
    own_ref,
    other_hbm,
    weight_hbm,
    streams_ref,
    gate_ref,
    product_ref,
    mixed_ref,
    back_ref,
    weight_ref,
    other_ref,
    arrived,
):
    core = place_ref[0]
    copies = []
    others = [pltpu.make_async_copy(other_hbm.at[x], other_ref.at[x], arrived.at[16 + x]) for x in range(4)]
    for x in range(4):
        for y in range(2):
            copies.append(
                pltpu.make_async_copy(
                    weight_hbm.at[pl.ds((x % 2) * 4 + 2 * (1 - core), 2), core, 2 * y + x // 2],
                    weight_ref.at[x, y],
                    arrived.at[2 * x + y],
                )
            )
    for x in range(4):
        for y in range(2):
            copies.append(
                pltpu.make_async_copy(
                    weight_hbm.at[pl.ds((x % 2) * 4 + 2 * core, 2), :, 2 * y + x // 2],
                    back_ref.at[x % 2, y, x // 2],
                    arrived.at[8 + 2 * x + y],
                )
            )
    for copy in copies[8:]:
        copy.start()
    for x in range(4):
        others[x].start()
        copies[2 * x].start()
        copies[2 * x + 1].start()
    streams, grad_gate = 0.0, 0.0
    contract = (((1,), (1,)), ((), ()))
    for values_ref in (own_ref, other_ref):
        for x in range(4):
            tokens, cotangent, weight = [], [], []
            if values_ref is other_ref:
                others[x].wait()
            for y in range(2):
                if values_ref is own_ref:
                    copies[8 + 2 * x + y].wait()
                    weight += [back_ref[x % 2, y, x // 2, z, core] for z in range(2)]
                else:
                    copies[2 * x + y].wait()
                    weight += [weight_ref[x, y, z] for z in range(2)]
                tokens.append(values_ref[x, :, y, 0].reshape(2 * ROWS, FEATURES))
                cotangent.append(values_ref[x, :, y, 1].reshape(2 * ROWS, FEATURES))
            tokens, cotangent = jnp.concatenate(tokens, 1), jnp.concatenate(cotangent, 1)
            weight = jnp.concatenate(weight, 1)
            streams += lax.dot_general(weight[:BACK], tokens, contract, preferred_element_type=F32)
            grad_gate += lax.dot_general(weight[BACK:], cotangent, contract, preferred_element_type=F32)
    streams = streams.astype(BF16)
    streams_ref[...] = streams
    gate_ref[...] = grad_gate
    query, key, value = (streams[i * HALF : (i + 1) * HALF].astype(F32) for i in range(3))
    product_ref[...] = (key * value).astype(BF16)
    mixed_ref[...] = (grad_gate * query).astype(BF16)


def forward(place, own, other, weight):
    vmem = pl.BlockSpec(memory_space=pltpu.VMEM)
    shape = lambda height, kind: jax.ShapeDtypeStruct((height, 2 * ROWS), kind)
    return pl.pallas_call(
        forward_kernel,
        out_shape=(
            shape(BACK, BF16),
            shape(HALF, F32),
            shape(HALF, BF16),
            shape(HALF, BF16),
            jax.ShapeDtypeStruct((2, 2, 2, 2, 2, STREAMS, ROWS), BF16),
        ),
        in_specs=[
            pl.BlockSpec(memory_space=pltpu.SMEM),
            vmem,
            pl.BlockSpec(memory_space=pl.ANY),
            pl.BlockSpec(memory_space=pl.ANY),
        ],
        out_specs=(vmem,) * 5,
        scratch_shapes=[
            pltpu.VMEM((4, 2, 2, STREAMS, ROWS), BF16),
            pltpu.VMEM((4, 2, 2, 2, ROWS, FEATURES), BF16),
            pltpu.SemaphoreType.DMA((20,)),
        ],
        compiler_params=pltpu.CompilerParams(vmem_limit_bytes=VMEM_FORWARD),
        cost_estimate=pl.CostEstimate(flops=1 << 30, bytes_accessed=9 << 20, transcendentals=0),
    )(place, own, other, weight)


def filtered(left, right, band):
    segments = [
        jnp.concatenate([left[s], right[s]], 1) for s in range(2)
    ]
    result = jnp.dot(jnp.concatenate(segments, 0), band, preferred_element_type=F32)
    return [
        jnp.concatenate(
            [
                result[s * HALF + g * GROUP : s * HALF + (g + 1) * GROUP, g * ROWS : (g + 1) * ROWS]
                for g in range(GROUPS)
            ],
            0,
        )
        for s in range(2)
    ]


def middle_kernel(
    place_ref, band_ref, streams_ref, gate_ref, product_ref, mixed_ref, before_ref, after_ref, terms_ref
):
    first = place_ref[1] == 0
    last = place_ref[1] == 15
    lanes = [slice(s * ROWS, (s + 1) * ROWS) for s in range(2)]
    product, mixed, before, after = (
        [ref[:, lanes[s]] for s in range(2)] for ref in (product_ref, mixed_ref, before_ref, after_ref)
    )
    zero = jnp.zeros_like(before[0])
    earlier = [jnp.where(first, zero, before[0]), jnp.where(first, before[0], before[1])]
    later = [jnp.where(last, after[1], after[0]), jnp.where(last, zero, after[1])]
    conv = filtered(earlier, product, band_ref[:, : GROUPS * ROWS])
    back = filtered(mixed, later, band_ref[:, GROUPS * ROWS :])
    for s in range(2):
        query, key, value = (
            streams_ref[i * HALF : (i + 1) * HALF, lanes[s]].astype(F32) for i in range(3)
        )
        terms = (gate_ref[:, lanes[s]] * conv[s], back[s] * value, back[s] * key, query * conv[s])
        for i in range(4):
            terms_ref[lanes[s], i * HALF : (i + 1) * HALF] = terms[i].T.astype(BF16)


def on_chip(kernel, out_shape, operands, flops):
    smem, vmem = pl.BlockSpec(memory_space=pltpu.SMEM), pl.BlockSpec(memory_space=pltpu.VMEM)
    return pl.pallas_call(
        kernel,
        out_shape=out_shape,
        in_specs=[smem] + [vmem] * (len(operands) - 1),
        out_specs=jax.tree.map(lambda _: vmem, out_shape),
        compiler_params=pltpu.CompilerParams(vmem_limit_bytes=VMEM_SMALL),
        cost_estimate=pl.CostEstimate(flops=flops, bytes_accessed=1 << 20, transcendentals=0),
    )(*operands)


def middle(*operands):
    return on_chip(middle_kernel, jax.ShapeDtypeStruct((2 * ROWS, STREAMS), BF16), operands, 1 << 28)


def backward_kernel(place_ref, terms_ref, weight_ref, out_ref):
    for part, cols in enumerate((slice(BACK, STREAMS), slice(0, BACK))):
        terms = jnp.concatenate([terms_ref[core, :, cols] for core in range(2)], 1)
        for y in range(2):
            for x in range(4):
                weight = [
                    jnp.concatenate([weight_ref[x % 2, y, x // 2, z, core, cols] for z in range(2)], 1)
                    for core in range(2)
                ]
                result = jnp.dot(terms, jnp.concatenate(weight, 0), preferred_element_type=F32)
                for h in range(2):
                    out_ref[2 * x + y, h, part] = result[h * ROWS : (h + 1) * ROWS].astype(BF16)


def backward(*operands):
    shape = (8, 2, 2, ROWS, FEATURES)
    return on_chip(backward_kernel, jax.ShapeDtypeStruct(shape, BF16), operands, 1 << 30)


def combine_kernel(place_ref, parts_ref, mine_ref, theirs_ref):
    half = place_ref[3]
    for part in range(2):
        mine, theirs = 0.0, 0.0
        for source in range(8):
            mine += parts_ref[source, half, part].astype(F32)
            theirs += parts_ref[source, 1 - half, part].astype(F32)
        mine_ref[part] = mine
        theirs_ref[part] = theirs.astype(BF16)


def combine(*operands):
    shape = (2, ROWS, FEATURES)
    out_shape = (jax.ShapeDtypeStruct(shape, F32), jax.ShapeDtypeStruct(shape, BF16))
    return on_chip(combine_kernel, out_shape, operands, 1 << 20)


def pack_kernel(in_ref, out_ref, packed_ref):
    for h in range(2):
        chans = slice(h * HALF, (h + 1) * HALF)
        streams = [in_ref[stream, :, chans].astype(F32).T.astype(BF16) for stream in range(3)]
        for l in range(2):
            for stream in range(3):
                packed_ref[2 * h + l, stream * HALF : (stream + 1) * HALF] = streams[stream]
            packed_ref[2 * h + l, BACK:] = out_ref[chans]


def packed(in_weight, out_weight):
    vmem = pl.BlockSpec(memory_space=pltpu.VMEM)
    return pl.pallas_call(
        pack_kernel,
        out_shape=jax.ShapeDtypeStruct((4, STREAMS, ROWS), BF16),
        in_specs=[vmem] * 2,
        out_specs=vmem,
    )(in_weight, out_weight)


def finish_kernel(place_ref, mine_ref, theirs_ref, mixed_ref, grad_ref):
    for part, ref in enumerate((mixed_ref, grad_ref)):
        ref[...] = (mine_ref[part] + theirs_ref[part].astype(F32)).astype(BF16)


def finish(*operands):
    return on_chip(finish_kernel, (jax.ShapeDtypeStruct((ROWS, FEATURES), BF16),) * 2, operands, 1 << 16)


def swapped(value, axes):
    return lax.all_to_all(value, axes, 0, 0, tiled=True)


def gathered(value, axes, count):
    return swapped(jnp.broadcast_to(value[None], (count,) + value.shape), axes)


def local(tokens, in_weight, out_weight, mr_filter, cotangent):
    half, core = lax.axis_index("h"), lax.axis_index("core")
    position = lax.axis_index(("l", "z"))
    place = jnp.stack([core, position, lax.axis_index("x"), half]).astype(jnp.int32)

    weight = swapped(packed(in_weight, out_weight), ("h", "l"))
    weight, tokens, cotangent = lax.optimization_barrier((weight, tokens, cotangent))
    values = jnp.stack([tokens, cotangent], 0)
    weight = lax.all_gather(weight, ("z", "core"), axis=0).reshape(8, 2, 4, STREAMS, ROWS)

    band = bands(lax.dynamic_slice_in_dim(mr_filter, half * GROUPS, GROUPS, 0))
    values = gathered(values, ("h", "ylo"), 4)
    values = gathered(values, "x", 4).reshape(4, 2, 2, 2, ROWS, FEATURES)
    values, band = lax.optimization_barrier((values, band))
    cross = [(0, 1), (1, 0)]
    other = lax.ppermute(values, "core", cross)

    streams, gate, product, mixed, weight = forward(place, values, other, weight)
    ring = [(n, (n + 1) % 16) for n in range(16)]
    before = lax.ppermute(product, ("l", "z"), ring)
    after = lax.ppermute(mixed, ("l", "z"), [(b, a) for a, b in ring])

    terms = middle(place, band, streams, gate, product, mixed, before, after)
    terms = lax.all_gather(terms, "core", axis=0)

    parts = swapped(backward(place, terms, weight), ("x", "ylo"))
    mine, theirs = combine(place, parts)
    return finish(place, mine, lax.ppermute(theirs, "h", cross))


def solution(mesh):
    fine = Mesh(mesh.devices.reshape(SIZES), AXES)
    ctx, tp = AXES[:3], AXES[3:]
    return jax.shard_map(
        local,
        mesh=fine,
        in_specs=(P(ctx, tp), P(None, ctx, tp), P(tp, ctx), P(tp, None), P(ctx, tp)),
        out_specs=(P(ctx, tp), P(ctx, tp)),
        check_vma=False,
    )
```
